32 devices in a mesh: expert: 8 (over z, x), shard: 4 (over y, core).
Axes of the slice: x: 2, y: 2, z: 4, core: 2. Of those that a mesh axis runs over, the one named last changes fastest.
Arguments:
- tokens: bfloat16 [8192, 1536], P(('expert', 'shard')), may hold values from -6 to 6
- lengths: int32 [8, 4], P('expert'), may hold values from 1 to 770, 1024 in all within a row
- routes: int32 [8192, 4], P(('expert', 'shard')), may hold values from 0 to 7, all different within a row
- slot_order: int32 [32, 1024], P(('expert', 'shard')), may hold values from 0 to 1023, each once within a row
- cotangent: bfloat16 [8192, 1536], P(('expert', 'shard')), may hold values from -6 to 6
- q_weight: bfloat16 [2, 1536, 1536], P(None, 'shard'), may hold values from -0.15625 to 0.15625
- key_matrix: bfloat16 [2, 1536, 256], P(None, 'shard'), may hold values from -0.15625 to 0.15625
- value_matrix: bfloat16 [2, 1536, 256], P(None, 'shard'), may hold values from -0.15625 to 0.15625
- out_weight: bfloat16 [2, 1536, 1536], P(None, 'shard'), may hold values from -2.5 to 2.5
- router_weight: bfloat16 [2, 1536, 8], P(None, 'shard'), may hold values from -0.078125 to 0.078125
- attn_gain: bfloat16 [2, 1536], P(None, 'shard'), may hold values from 0.099609375 to 1.8984375
- ffn_gain: bfloat16 [2, 1536], P(None, 'shard'), may hold values from 0.099609375 to 1.8984375
- gate_weight: bfloat16 [2, 8, 1536, 768], P(None, 'expert'), may hold values from -0.15625 to 0.15625
- up_weight: bfloat16 [2, 8, 1536, 768], P(None, 'expert'), may hold values from -0.15625 to 0.15625
- down_weight: bfloat16 [2, 8, 768, 1536], P(None, 'expert'), may hold values from -0.21875 to 0.21875
Outputs:
- output: bfloat16 [8192, 1536], P(('expert', 'shard'))
- input_grad: bfloat16 [8192, 1536], P(('expert', 'shard'))
- q_grad: float32 [2, 1536, 1536], P(None, 'shard')
- key_grad: float32 [2, 1536, 256], P(None, 'shard')
- value_grad: float32 [2, 1536, 256], P(None, 'shard')
- out_grad: float32 [2, 1536, 1536], P(None, 'shard')
- router_grad: float32 [2, 1536, 8], P(None, 'shard')
- attn_gain_grad: float32 [2, 1536], P(None, 'shard')
- ffn_gain_grad: float32 [2, 1536], P(None, 'shard')
- gate_grad: float32 [2, 8, 1536, 768], P(None, 'expert', 'shard')
- up_grad: float32 [2, 8, 1536, 768], P(None, 'expert', 'shard')
- down_grad: float32 [2, 8, 768, 1536], P(None, 'expert', 'shard')
The draws below stay inside these ranges and needn't reach their ends.
Inputs may be any that keep to these rules, and one draw needn't show every extreme that they name: `routes`: each row names 4 different experts. `slot_order`: each row orders the 1024 pairs of one device, each once. Row s gives the lengths of the 4 documents of sequence s in order; they sum to 1024.
All inputs are finite; a program needn't handle non-finite values.
Results may differ from the reference program's by a relative error of at most 0.025.
Values may be sent and summed in bfloat16 or wider, within the bound.
No kernel may reach another device: no remote copies, remote signals or barrier semaphores. Data moves between devices by JAX's collectives and lax.ppermute only.
A program may use at most 320 MiB of HBM per device.

```python
import math
import jax
import jax.numpy as jnp
import numpy as np
from jax import lax

MODEL_WIDTH = 1536
QUERY_HEADS = 12
KEY_VALUE_HEADS = 2
HEAD_SIZE = 128
F = 768
TOP = 4
LAYER_COUNT = 2
DOCS = 4
TOK_DEV = 256
EXPERTS = 8
SOURCES = 32
SEQUENCE_COUNT = 8
SEQUENCE_TOKENS = 1024
TOKENS = 8192
PAIRS = 1024
CAP = 160


def shard_levels(rng, dims, split, least, top_value):
    loudness = 1.0
    for dim, parts in split:
        steps = jax.random.uniform(jax.random.fold_in(jax.random.fold_in(rng, 6), dim), (parts,), jnp.float32, least / len(split), top_value / len(split))
        loudness = loudness * jnp.repeat(jnp.exp(steps), dims[dim] // parts).reshape((-1,) + (1,) * (len(dims) - 1 - dim))
    return loudness


def picks_of(key, rows, count, top, lift):
    ranking = jax.random.permutation(jax.random.fold_in(key, 1), count)
    boost = ranking
    for power in range(3):
        boost = boost * boost // count
    boost = boost * lift // count
    tickets = jax.random.randint(jax.random.fold_in(key, 2), (rows, count), 0, 4096) + boost
    sure = jax.random.permutation(jax.random.fold_in(key, 3), rows)[jnp.arange(count) % rows]
    tickets = jnp.where(jnp.arange(rows)[:, None] == sure[None, :], 1 << 14, tickets)
    score = tickets * count + jnp.arange(count)
    return lax.top_k(score.astype(jnp.int32), top)[1].astype(jnp.int32)


def split_up(number_of, total, limit, slope):
    weights = [(1 << 20) // math.isqrt(standing ** slope) + 1 for standing in range(2, number_of + 1)]
    spare, holding = total - limit - (number_of - 1), [1] * (number_of - 1)
    while spare > 0:
        movable = [i for i in range(number_of - 1) if holding[i] < limit]
        mass, remaining = sum([weights[i] for i in movable]), spare
        for i in movable:
            addition = min(limit - holding[i], max(1, remaining * weights[i] // mass), spare)
            holding[i] = holding[i] + addition
            spare = spare - addition
    return np.array([limit] + holding)


def uneven_parts(key, amount, total, most, lean):
    if amount == 2:
        one = jax.random.randint(key, (), max(1, total - most), min(most, total - 1) + 1)
        return jnp.stack([one, total - one])
    sizes = jnp.asarray(split_up(amount, total, most, lean), jnp.int32)
    couples = (amount - 1) // 2
    source_of, sink = sizes[1:1 + 2 * couples:2], sizes[2:2 + 2 * couples:2]
    slack = jnp.minimum(source_of - 1, most - sink)
    passed = jax.random.randint(jax.random.fold_in(key, 1), (couples,), 0, 1 << 20) % (slack + 1)
    sizes = sizes.at[1:1 + 2 * couples:2].set(source_of - passed).at[2:2 + 2 * couples:2].set(sink + passed)
    return sizes[jax.random.permutation(jax.random.fold_in(key, 2), amount)]


def normal_values(stream_key, extent, scale, limit, split=(), kind=jnp.bfloat16):
    values = jax.random.normal(stream_key, extent, jnp.float32) * scale
    if len(split) > 0:
        values = shard_levels(stream_key, extent, split, -0.22, 0.18) * values
    return jnp.clip(values, min=-limit, max=limit).astype(kind)


def setup_inputs(seed: int = 0) -> dict:
    seeds = jax.random.split(jax.random.key(seed), 16)
    tokens = normal_values(seeds[0], (TOKENS, MODEL_WIDTH), 1.0, 6.0, ((0, 32),))
    lengths = jax.vmap(lambda own: uneven_parts(own, DOCS, SEQUENCE_TOKENS, SEQUENCE_TOKENS - TOK_DEV + 2, 1))(jax.random.split(seeds[1], SEQUENCE_COUNT)).reshape((SEQUENCE_COUNT, DOCS)).astype(jnp.int32)
    routes = picks_of(seeds[2], TOKENS, EXPERTS, TOP, 4096)
    slot_order = jax.vmap(lambda own: jax.random.permutation(own, PAIRS))(jax.random.split(seeds[3], SOURCES)).reshape((SOURCES, PAIRS)).astype(jnp.int32)
    cotangent = normal_values(seeds[4], (TOKENS, MODEL_WIDTH), 1.0, 6.0, ((0, 32),))
    q_weight = normal_values(seeds[5], (LAYER_COUNT, MODEL_WIDTH, QUERY_HEADS * HEAD_SIZE), MODEL_WIDTH ** -0.5, 0.15625, ((1, 4),))
    key_matrix = normal_values(seeds[6], (LAYER_COUNT, MODEL_WIDTH, KEY_VALUE_HEADS * HEAD_SIZE), MODEL_WIDTH ** -0.5, 0.15625, ((1, 4),))
    value_matrix = normal_values(seeds[7], (LAYER_COUNT, MODEL_WIDTH, KEY_VALUE_HEADS * HEAD_SIZE), MODEL_WIDTH ** -0.5, 0.15625, ((1, 4),))
    out_weight = normal_values(seeds[8], (LAYER_COUNT, QUERY_HEADS * HEAD_SIZE, MODEL_WIDTH), (max(1, 4 * QUERY_HEADS * HEAD_SIZE // SEQUENCE_TOKENS)) ** -0.5, 2.5, ((1, 4),))
    router_weight = normal_values(seeds[9], (LAYER_COUNT, MODEL_WIDTH, EXPERTS), (4 * MODEL_WIDTH) ** -0.5, 0.078125, ((1, 4),))
    attn_gain = jnp.clip(1.0 + 0.18 * jax.random.normal(seeds[10], (LAYER_COUNT, MODEL_WIDTH), jnp.float32), 0.099609375, 1.8984375).astype(jnp.bfloat16)
    ffn_gain = jnp.clip(1.0 + 0.18 * jax.random.normal(seeds[11], (LAYER_COUNT, MODEL_WIDTH), jnp.float32), 0.099609375, 1.8984375).astype(jnp.bfloat16)
    gate_weight = normal_values(seeds[12], (LAYER_COUNT, EXPERTS, MODEL_WIDTH, F), MODEL_WIDTH ** -0.5, 0.15625, ((1, 8),))
    up_weight = normal_values(seeds[13], (LAYER_COUNT, EXPERTS, MODEL_WIDTH, F), MODEL_WIDTH ** -0.5, 0.15625, ((1, 8),))
    down_weight = normal_values(seeds[14], (LAYER_COUNT, EXPERTS, F, MODEL_WIDTH), F ** -0.5, 0.21875, ((1, 8),))
    return dict(tokens=tokens, lengths=lengths, routes=routes, slot_order=slot_order, cotangent=cotangent, q_weight=q_weight, key_matrix=key_matrix, value_matrix=value_matrix, out_weight=out_weight, router_weight=router_weight, attn_gain=attn_gain, ffn_gain=ffn_gain, gate_weight=gate_weight, up_weight=up_weight, down_weight=down_weight)


@jax.custom_vjp
def lower_half(v):
    return lax.optimization_barrier(v.astype(jnp.bfloat16)).astype(jnp.float32)

@jax.custom_vjp
def low_back(v):
    return v

def low_keep(v):
    return (lower_half(v), None)

def low_pass(kept, grad):
    return (grad,)

def back_keep(v):
    return (v, None)

def back_low(kept, grad):
    return (lower_half(grad),)
lower_half.defvjp(low_keep, low_pass)
low_back.defvjp(back_keep, back_low)
norm_eps = 1e-06
rope_base = 10000.0
masked_score = -1e+30
highest = lax.Precision.HIGHEST

def product(left, right):
    return jnp.dot(left, right, precision=highest)

def norm_rows(values, norm_gain):
    inverse = lax.rsqrt(lax.optimization_barrier(jnp.mean(values * values, axis=-1, keepdims=True)) + norm_eps)
    return values * inverse * norm_gain

def rotary_apply(values, position, head_count, direction):
    head_width = values.shape[1] // head_count
    half_width = head_width // 2
    frequency = rope_base ** (-(jnp.arange(half_width).astype(jnp.float32) * 2.0 / head_width))
    angles = position.astype(jnp.float32)[:, None] * frequency[None, :]
    cosine = jnp.cos(angles)[:, None, :]
    sine_part = direction * jnp.sin(angles)[:, None, :]
    split_rows = values.reshape(values.shape[0], head_count, head_width)
    first_half = split_rows[:, :, :half_width]
    second_half = split_rows[:, :, half_width:]
    turned = jnp.concatenate([first_half * cosine - second_half * sine_part, second_half * cosine + first_half * sine_part], axis=-1)
    return turned.reshape(values.shape[0], head_count * head_width)

def documents(lengths_row, position):
    doc_ends = jnp.cumsum(lengths_row).astype(jnp.int32)
    doc_starts = doc_ends - lengths_row
    document_index = lax.optimization_barrier(jnp.sum((position[:, None] >= doc_ends[None, :]).astype(jnp.int32), axis=1))
    doc_first = lax.optimization_barrier(jnp.max(jnp.where(doc_starts[None, :] <= position[:, None], doc_starts[None, :], 0), axis=1))
    return (document_index, position - doc_first)

def router_gates(logits, route_rows, experts):
    probability = jax.nn.softmax(logits, axis=-1)
    picked = (route_rows[:, :, None] == jnp.arange(experts, dtype=jnp.int32)[None, None, :]).astype(logits.dtype)
    chosen = lax.optimization_barrier(jnp.sum(probability[:, None, :] * picked, axis=-1))
    return chosen / lax.optimization_barrier(jnp.sum(chosen, axis=-1, keepdims=True))

def gated_unit(gate_pre, up_pre):
    return jax.nn.gelu(gate_pre, approximate=True) * up_pre

def route_slots(route_flat, order_row, experts, capacity):
    ranked = route_flat[order_row]
    matches = (ranked[:, None] == jnp.arange(experts, dtype=jnp.int32)[None, :]).astype(jnp.int32)
    before = jnp.cumsum(matches, axis=0) - matches
    slot_index = lax.optimization_barrier(jnp.sum(before * matches, axis=1))
    target = jnp.where(slot_index < capacity, ranked * capacity + slot_index, experts * capacity)
    return jnp.zeros_like(route_flat).at[order_row].set(target)

def slot_tables(routes, slot_order):
    sources = slot_order.shape[0]
    pair_count = TOK_DEV * TOP
    targets = jax.vmap(lambda route_row, order_row: route_slots(route_row, order_row, EXPERTS, CAP))(routes.reshape(sources, pair_count), slot_order)
    source_index = jnp.arange(sources, dtype=jnp.int32)[:, None]
    pair_index = jnp.arange(pair_count, dtype=jnp.int32)[None, :]
    total_slots = EXPERTS * sources * CAP
    place = targets // CAP * (sources * CAP) + source_index * CAP + targets % CAP
    place = jnp.where(targets < EXPERTS * CAP, place, total_slots).reshape(-1)
    token_global = (source_index * TOK_DEV + pair_index // TOP).reshape(-1)
    pair_global = (source_index * pair_count + pair_index).reshape(-1)
    slot_token = jnp.full((total_slots,), TOKENS, jnp.int32).at[place].set(token_global, mode='drop')
    slot_pair = jnp.full((total_slots,), TOKENS * TOP, jnp.int32).at[place].set(pair_global, mode='drop')
    return (slot_token.reshape(EXPERTS, sources * CAP), slot_pair.reshape(EXPERTS, sources * CAP))

def attend_heads(query_rows, key_rows, value_rows, document_index):
    seq_index = jnp.arange(SEQUENCE_TOKENS, dtype=jnp.int32)
    query_head_rows = query_rows.reshape(SEQUENCE_TOKENS, KEY_VALUE_HEADS, QUERY_HEADS // KEY_VALUE_HEADS, HEAD_SIZE)
    key_head_rows = key_rows.reshape(SEQUENCE_TOKENS, KEY_VALUE_HEADS, HEAD_SIZE)
    value_head_rows = value_rows.reshape(SEQUENCE_TOKENS, KEY_VALUE_HEADS, HEAD_SIZE)
    visible = (document_index[:, None] == document_index[None, :]) & (seq_index[None, :] <= seq_index[:, None])
    raw_scores = jnp.einsum('qhgd,khd->hgqk', query_head_rows, key_head_rows, precision=highest)
    scores = low_back(jnp.where(visible, raw_scores * HEAD_SIZE ** (-0.5), masked_score))
    probability = jax.nn.softmax(scores, axis=-1)
    mixed_heads = jnp.einsum('hgqk,khd->qhgd', lower_half(probability), value_head_rows, precision=highest)
    return mixed_heads.reshape(SEQUENCE_TOKENS, QUERY_HEADS * HEAD_SIZE)

def block(stream, weights, document_index, document_place, routes, slot_token, slot_pair):
    w_query, w_key, w_value, w_out, w_router, gain_attn, gain_ffn, w_gate, w_up, w_down = weights
    hidden = lower_half(norm_rows(stream, gain_attn))
    q_pre = low_back(product(hidden, w_query))
    key_before_rotation = low_back(product(hidden, w_key))
    value_rows = lower_half(low_back(product(hidden, w_value)))
    query_rotated = lower_half(rotary_apply(q_pre, document_place, QUERY_HEADS, 1.0))
    key_rotated = lower_half(rotary_apply(key_before_rotation, document_place, KEY_VALUE_HEADS, 1.0))
    attended_rows = lax.map(jax.checkpoint(lambda group_input: attend_heads(*group_input)), (query_rotated.reshape(SEQUENCE_COUNT, SEQUENCE_TOKENS, QUERY_HEADS * HEAD_SIZE), key_rotated.reshape(SEQUENCE_COUNT, SEQUENCE_TOKENS, KEY_VALUE_HEADS * HEAD_SIZE), value_rows.reshape(SEQUENCE_COUNT, SEQUENCE_TOKENS, KEY_VALUE_HEADS * HEAD_SIZE), document_index.reshape(SEQUENCE_COUNT, SEQUENCE_TOKENS)))
    mixed_heads = lower_half(low_back(attended_rows.reshape(TOKENS, QUERY_HEADS * HEAD_SIZE)))
    stream = stream + low_back(product(mixed_heads, w_out))
    routed = lower_half(norm_rows(stream, gain_ffn))
    logits = low_back(product(routed, w_router))
    gate_values = router_gates(logits, routes, EXPERTS)
    padded = jnp.concatenate([routed, jnp.zeros((1, MODEL_WIDTH), jnp.float32)], axis=0)
    gate_flat = jnp.concatenate([gate_values.reshape(-1), jnp.zeros((1,), jnp.float32)], axis=0)

    def expert_work(expert_in):
        token_ids, pair_ids, expert_gate, expert_up, expert_down = expert_in
        arrived = low_back(padded[token_ids])
        gate_pre = low_back(product(arrived, expert_gate))
        up_pre = low_back(product(arrived, expert_up))
        active = lower_half(low_back(gated_unit(gate_pre, up_pre)))
        produced = lower_half(low_back(product(active, expert_down)))
        return gate_flat[pair_ids][:, None] * produced
    spread = lax.map(jax.checkpoint(expert_work), (slot_token, slot_pair, w_gate, w_up, w_down))
    combined = jnp.zeros((TOKENS, MODEL_WIDTH), jnp.float32).at[slot_token.reshape(-1)].add(spread.reshape(-1, MODEL_WIDTH), mode='drop')
    return stream + combined

def reference(tokens, lengths, routes, slot_order, cotangent, q_weight, key_matrix, value_matrix, out_weight, router_weight, attn_gain, ffn_gain, gate_weight, up_weight, down_weight):
    seq_index = jnp.arange(SEQUENCE_TOKENS, dtype=jnp.int32)
    document_index, document_place = jax.vmap(lambda lengths_row: documents(lengths_row, seq_index))(lengths)
    document_index = document_index.reshape(TOKENS)
    document_place = document_place.reshape(TOKENS)
    slot_token, slot_pair = slot_tables(routes, slot_order)
    weights = tuple((weight.astype(jnp.float32) for weight in (q_weight, key_matrix, value_matrix, out_weight, router_weight, attn_gain, ffn_gain, gate_weight, up_weight, down_weight)))

    def forward(stream, *layer_weights):
        for layer_index in range(LAYER_COUNT):
            stream = block(stream, tuple((weight[layer_index] for weight in layer_weights)), document_index, document_place, routes, slot_token, slot_pair)
        return stream
    result, pullback = jax.vjp(forward, tokens.astype(jnp.float32), *weights)
    gradients = pullback(cotangent.astype(jnp.float32))
    return (result.astype(jnp.bfloat16), gradients[0].astype(jnp.bfloat16), gradients[1], gradients[2], gradients[3], gradients[4], gradients[5], gradients[6], gradients[7], gradients[8], gradients[9], gradients[10])
```

```python
import jax
import jax.numpy as jnp
from jax import lax
from jax.sharding import PartitionSpec as P

QUERY_HEADS = 12
KEY_VALUE_HEADS = 2
HEAD_SIZE = 128

norm_eps = 1e-06
rope_base = 10000.0
masked_score = -1e30

bf16 = jnp.bfloat16
f32 = jnp.float32


def mm(left, right):
    return jnp.dot(left, right, preferred_element_type=f32)


def mm_tn(left, right):
    return lax.dot_general(left, right, (((0,), (0,)), ((), ())), preferred_element_type=f32)


def mm_nt(left, right):
    return lax.dot_general(left, right, (((1,), (1,)), ((), ())), preferred_element_type=f32)


def norm_forward(values, gain):
    inverse = lax.rsqrt(jnp.mean(values * values, axis=-1, keepdims=True) + norm_eps)
    return values * inverse * gain, inverse


def norm_backward(values, inverse, gain, grad):
    scaled = grad * gain
    mean_part = jnp.mean(values * scaled, axis=-1, keepdims=True)
    d_values = inverse * scaled - values * (inverse * inverse * inverse * mean_part)
    d_gain = jnp.sum(grad * values * inverse, axis=0)
    return d_values, d_gain


def rotary_tables(position):
    half_width = HEAD_SIZE // 2
    frequency = rope_base ** (-(jnp.arange(half_width).astype(f32) * 2.0 / HEAD_SIZE))
    angles = position.astype(f32)[:, None] * frequency[None, :]
    return jnp.cos(angles)[:, None, :], jnp.sin(angles)[:, None, :]


def rotary_apply(values, tables, head_count, direction):
    cosine, sine = tables
    sine = direction * sine
    half_width = HEAD_SIZE // 2
    split_rows = values.reshape(values.shape[0], head_count, HEAD_SIZE)
    first_half = split_rows[:, :, :half_width]
    second_half = split_rows[:, :, half_width:]
    turned = jnp.concatenate(
        [first_half * cosine - second_half * sine, second_half * cosine + first_half * sine],
        axis=-1,
    )
    return turned.reshape(values.shape[0], head_count * HEAD_SIZE)


def documents(lengths_row, position):
    doc_ends = jnp.cumsum(lengths_row)
    doc_starts = doc_ends - lengths_row
    document_index = jnp.sum((position[:, None] >= doc_ends[None, :]).astype(jnp.int32), axis=1)
    doc_first = jnp.max(
        jnp.where(doc_starts[None, :] <= position[:, None], doc_starts[None, :], 0), axis=1
    )
    return (document_index, position - doc_first)


def slot_table(routes, order_row, experts, capacity):
    token_rows, top_count = routes.shape
    pair_count = token_rows * top_count
    pairs = jnp.arange(pair_count, dtype=jnp.int32)
    named = (order_row[:, None] == pairs[None, :]).astype(bf16)
    of_pair = (
        routes.reshape(pair_count)[:, None] == jnp.arange(experts, dtype=jnp.int32)[None, :]
    ).astype(bf16)
    ranked = mm(named, of_pair)
    earlier = (pairs[None, :] < pairs[:, None]).astype(bf16)
    before = mm(earlier, ranked.astype(bf16))
    code = jnp.where(before < capacity, before + 1.0, -1.0) * ranked
    back = mm_tn(code.astype(bf16), named)
    return jnp.sum(back.reshape(experts, token_rows, top_count), axis=2)


def chosen_softmax(logits, chosen):
    top = jnp.max(jnp.where(chosen, logits, masked_score), axis=-1, keepdims=True)
    weight = jnp.where(chosen, jnp.exp(jnp.where(chosen, logits - top, 0.0)), 0.0)
    total = jnp.sum(weight, axis=-1, keepdims=True)
    return weight / jnp.where(total > 0.0, total, 1.0)


class Lines:
    def __init__(self):
        self.experts = lax.axis_size("expert")
        self.count = self.experts // 2
        self.index = lax.axis_index("expert")
        self.line = self.index // 2
        self.side = self.index % 2

    def source(self, slot):
        count, line = self.count, self.line
        low = jnp.where(line + slot < count, line + slot, count - 1 - slot)
        mirror = count - 1 - line
        high = count - 1 - jnp.where(mirror + slot < count, mirror + slot, count - 1 - slot)
        return jnp.where(line < count // 2, low, high)

    def swap(self, values):
        return lax.ppermute(values, "expert", [(i, i ^ 1) for i in range(self.experts)])

    def shift(self, values, lines, delta):
        pairs = [(2 * i + k, 2 * (i + delta) + k) for i in lines for k in range(2)]
        return lax.ppermute(values, "expert", pairs)

    def gather(self, values):
        count = self.count
        above, below = {0: values}, {0: values}
        for step in range(1, count):
            below[step] = self.shift(below[step - 1], range(step - 1, count - 1), 1)
            above[step] = self.shift(above[step - 1], range(1, count - step + 1), -1)
        slots = [values]
        for slot in range(1, count):
            parts = {}
            for line in range(count):
                near = line if line < count // 2 else count - 1 - line
                toward = near + slot < count
                distance = slot if toward else near + slot + 1 - count
                up = toward == (line < count // 2)
                parts.setdefault((up, distance), []).append(line)
            chosen = None
            for (up, distance), lines in parts.items():
                block = above[distance] if up else below[distance]
                if chosen is None:
                    chosen = block
                else:
                    here = jnp.any(self.line == jnp.array(lines))
                    chosen = jnp.where(here, block, chosen)
            slots.append(chosen)
        return slots

    def reduce(self, blocks):
        count, line = self.count, self.line
        half = count // 2

        def pick(distance, up):
            near = {}
            for at in range(count):
                if up and at + distance >= count or not up and at - distance < 0:
                    continue
                if up:
                    slot = distance if at < half else at + distance
                else:
                    slot = distance if at >= half else count - 1 - at + distance
                near.setdefault(slot, []).append(at)
            value = None
            for slot, lines in near.items():
                if value is None:
                    value = blocks[slot]
                else:
                    value = jnp.where(jnp.any(line == jnp.array(lines)), blocks[slot], value)
            return value

        from_below = from_above = None
        for step in range(count - 1):
            distance = count - 1 - step
            up, down = pick(distance, True), pick(distance, False)
            if from_below is not None:
                up = up + from_below.astype(f32)
                down = down + from_above.astype(f32)
            from_below = self.shift(up.astype(bf16), range(0, step + 1), 1)
            from_above = self.shift(down.astype(bf16), range(count - 1 - step, count), -1)
        return blocks[0] + from_below.astype(f32) + from_above.astype(f32)


def core_swap(values):
    return lax.ppermute(values, "shard", [(i, i ^ 1) for i in range(lax.axis_size("shard"))])


def row_swap(values):
    return lax.ppermute(values, "shard", [(i, i ^ 2) for i in range(lax.axis_size("shard"))])


def gather_weight(shard_rows):
    mine = lax.axis_index("shard")
    rows = shard_rows.shape[0]
    across = row_swap(shard_rows)
    beside = core_swap(shard_rows)
    diagonal = core_swap(across)
    whole = jnp.zeros((4 * rows, shard_rows.shape[1]), shard_rows.dtype)
    for mask, block in ((0, shard_rows), (2, across), (1, beside), (3, diagonal)):
        whole = lax.dynamic_update_slice(whole, block, ((mine ^ mask) * rows, 0))
    return whole


def split_columns(values):
    mine = lax.axis_index("shard")
    width = values.shape[1] // 4
    return [
        lax.dynamic_slice(values, (0, (mine ^ mask) * width), (values.shape[0], width))
        for mask in range(4)
    ]


def scattered_product(columns, right):
    width = columns[0].shape[1]
    sent = mm_tn(jnp.concatenate([columns[3], columns[1]], axis=1), right).astype(bf16)
    arrived = core_swap(sent).astype(f32)
    across = mm_tn(columns[2], right) + arrived[:width]
    crossed = row_swap(across.astype(bf16)).astype(f32)
    return mm_tn(columns[0], right) + arrived[width:] + crossed


def sum_over_experts(lines, part):
    rows, width = part.shape
    half = rows // 2
    block = half // lines.count
    low = part.astype(bf16)
    given = lax.dynamic_slice(low, ((1 - lines.side) * half, 0), (half, width))
    kept = lax.dynamic_slice(part, (lines.side * half, 0), (half, width))
    kept = kept + lines.swap(given).astype(f32)
    blocks = [
        lax.dynamic_slice(kept, (lines.source(slot) * block, 0), (block, width))
        for slot in range(lines.count)
    ]
    own = lines.reduce(blocks).astype(bf16)
    slots = lines.gather(own)
    mine = jnp.zeros((half, width), bf16)
    for slot in range(lines.count):
        mine = lax.dynamic_update_slice(mine, slots[slot], (lines.source(slot) * block, 0))
    other = lines.swap(mine)
    whole = jnp.zeros((rows, width), bf16)
    whole = lax.dynamic_update_slice(whole, mine, (lines.side * half, 0))
    whole = lax.dynamic_update_slice(whole, other, ((1 - lines.side) * half, 0))
    return whole.astype(f32)


def per_device(
    tokens,
    lengths,
    routes,
    slot_order,
    cotangent,
    q_weight,
    key_matrix,
    value_matrix,
    out_weight,
    router_weight,
    attn_gain,
    ffn_gain,
    gate_weight,
    up_weight,
    down_weight,
):
    lines = Lines()
    layer_count = q_weight.shape[0]
    shard_count = lax.axis_size("shard")
    mine = lax.axis_index("shard")
    token_rows, model_width = tokens.shape
    top_count = routes.shape[1]
    pair_count = token_rows * top_count
    experts = router_weight.shape[2]
    assert shard_count == 4 and experts == lines.experts and gate_weight.shape[1] == 1
    hidden_units = gate_weight.shape[3]
    capacity = (pair_count * 5 + 4 * experts - 1) // (4 * experts)
    assert capacity < 256
    sequence_length = token_rows * shard_count
    group_width = QUERY_HEADS // KEY_VALUE_HEADS
    kv_width = KEY_VALUE_HEADS * HEAD_SIZE
    score_scale = HEAD_SIZE ** (-0.5)

    own_rows = jnp.arange(token_rows, dtype=jnp.int32)
    position = mine * token_rows + own_rows
    key_position = jnp.concatenate([(mine ^ mask) * token_rows + own_rows for mask in (0, 2, 1, 3)])
    query_doc, query_position = documents(lengths[0], position)
    key_doc = documents(lengths[0], key_position)[0]
    visible = (query_doc[:, None] == key_doc[None, :]) & (
        key_position[None, :] <= position[:, None]
    )
    tables = rotary_tables(query_position)

    qkv_shards = [
        (q_weight[i], jnp.concatenate([key_matrix[i], value_matrix[i]], axis=1))
        for i in range(layer_count)
    ]
    gathered = []
    for i in range(layer_count):
        if i == 0:
            w_kv, w_query = gather_weight(qkv_shards[i][1]), gather_weight(qkv_shards[i][0])
        else:
            w_kv = lax.all_gather(qkv_shards[i][1], "shard", axis=0, tiled=True)
            w_query = lax.all_gather(qkv_shards[i][0], "shard", axis=0, tiled=True)
        w_out = lax.all_gather(out_weight[i], "shard", axis=0, tiled=True)
        gathered.append((w_query, w_kv, w_out))
    small = jnp.concatenate(
        [
            router_weight.transpose(0, 2, 1),
            attn_gain[:, None, :],
            ffn_gain[:, None, :],
        ],
        axis=1,
    )
    small = lax.all_gather(small, "shard", axis=2, tiled=True)
    routers = [small[i, :experts] for i in range(layer_count)]
    attn_gains = [small[i, experts].astype(f32)[None, :] for i in range(layer_count)]
    ffn_gains = [small[i, experts + 1].astype(f32)[None, :] for i in range(layer_count)]

    own_table = slot_table(routes, slot_order[0], experts, capacity)
    chosen_here = own_table.T != 0.0
    all_tables = lax.all_gather(own_table, "expert", axis=0)
    slot_code = jnp.arange(1, capacity + 1, dtype=jnp.int32).astype(f32)[:, None]
    mates = []
    own_hot, mate_hot, row_chosen = [], [], []
    for column in range(2):
        for slot in range(lines.count):
            source = lines.source(slot) * 2 + (lines.side ^ column)
            at_source = lax.dynamic_index_in_dim(all_tables, source, 0, keepdims=False)
            for_own = lax.dynamic_index_in_dim(at_source, lines.index, 0, keepdims=True)
            hot = (for_own == slot_code).astype(bf16)
            row_chosen.append(mm_nt(hot, (at_source != 0.0).astype(bf16)))
            if column == 0:
                own_hot.append(hot)
                for_mate = lax.dynamic_index_in_dim(at_source, lines.index ^ 1, 0, keepdims=True)
                mate_hot.append((for_mate == slot_code).astype(bf16))
            mates.append((source, hot))
    row_chosen = jnp.concatenate(row_chosen, axis=0) > 0.5

    def dispatch(values):
        slots = lines.gather(values)
        far = [lines.swap(mm(mate_hot[j], slots[j]).astype(bf16)) for j in range(lines.count)]
        near = [mm(own_hot[j], slots[j]).astype(bf16) for j in range(lines.count)]
        return jnp.concatenate(near + far, axis=0)

    def give_back(rows):
        blocks = [rows[i * capacity : (i + 1) * capacity] for i in range(2 * lines.count)]
        parts = [None] * lines.count
        for j in reversed(range(lines.count)):
            arrived = lines.swap(blocks[lines.count + j])
            parts[j] = mm_tn(own_hot[j], blocks[j]) + mm_tn(mate_hot[j], arrived)
        return lines.reduce(parts)

    def gate_grads_back(row_values):
        blocks = row_values.reshape(2 * lines.count, capacity)
        spread = jnp.zeros((experts, token_rows), f32)
        for i, (source, hot) in enumerate(mates):
            dense = jnp.sum(hot.astype(f32) * blocks[i][:, None], axis=0, keepdims=True)
            spread = lax.dynamic_update_slice(spread, dense, (source, 0))
        return lax.all_to_all(spread, "expert", split_axis=0, concat_axis=0, tiled=True).T

    def expert_forward(i, arrived):
        logits = mm_nt(arrived, routers[i])
        gates = chosen_softmax(logits, row_chosen)
        own_gate = lax.dynamic_slice(gates, (0, lines.index), (gates.shape[0], 1))
        gate_pre = mm(arrived, gate_weight[i, 0])
        up_pre = mm(arrived, up_weight[i, 0])
        active = jax.nn.gelu(gate_pre, approximate=True) * up_pre
        gated = (own_gate * active).astype(bf16)
        produced = mm(gated, down_weight[i, 0]).astype(bf16)
        return produced, dict(gate=own_gate, gate_pre=gate_pre, up_pre=up_pre, gated=gated)

    def expert_backward(i, arrived, kept, d_arrived):
        du = mm_nt(d_arrived, down_weight[i, 0])
        unit, pull = jax.vjp(
            lambda a, b: jax.nn.gelu(a, approximate=True) * b, kept["gate_pre"], kept["up_pre"]
        )
        d_gate_rows = jnp.sum(du * unit, axis=1)
        d_active = (kept["gate"] * du).astype(bf16).astype(f32)
        d_gate_pre, d_up_pre = pull(d_active)
        d_both = jnp.concatenate([d_gate_pre.astype(bf16), d_up_pre.astype(bf16)], axis=1)
        both_weight = jnp.concatenate([gate_weight[i, 0], up_weight[i, 0]], axis=1)
        d_rows = mm_nt(d_both, both_weight).astype(bf16)
        both_grad = scattered_product(split_columns(arrived), d_both)
        down_grad = scattered_product(split_columns(kept["gated"]), d_arrived)
        return d_rows, d_gate_rows, both_grad, down_grad

    stream = tokens.astype(f32)
    stored = []
    d_arrived_last = dispatch(cotangent)
    for i in range(layer_count):
        w_query, w_kv, w_out = gathered[i]
        normed, attn_inverse = norm_forward(stream, attn_gains[i])
        hidden = normed.astype(bf16)
        kv_pre = mm(hidden, w_kv)
        keys = rotary_apply(kv_pre[:, :kv_width], tables, KEY_VALUE_HEADS, 1.0)
        kv_own = jnp.concatenate([keys, kv_pre[:, kv_width:]], axis=1).astype(bf16)
        kv_pair = jnp.concatenate([kv_own, row_swap(kv_own)], axis=0)
        kv_all = jnp.concatenate([kv_pair, core_swap(kv_pair)], axis=0)
        q_pre = mm(hidden, w_query)
        query_heads = rotary_apply(q_pre, tables, QUERY_HEADS, 1.0).astype(bf16)
        query_heads = query_heads.reshape(token_rows, KEY_VALUE_HEADS, group_width, HEAD_SIZE)
        key_heads = kv_all[:, :kv_width].reshape(sequence_length, KEY_VALUE_HEADS, HEAD_SIZE)
        value_heads = kv_all[:, kv_width:].reshape(sequence_length, KEY_VALUE_HEADS, HEAD_SIZE)
        raw_scores = jnp.einsum(
            "qhgd,khd->hgqk", query_heads, key_heads, preferred_element_type=f32
        )
        scores = jnp.where(visible, raw_scores * score_scale, masked_score)
        row_peak = jnp.max(scores, axis=-1, keepdims=True)
        exponent = jnp.exp(scores - row_peak)
        row_total = jnp.sum(exponent, axis=-1, keepdims=True)
        probs_low = (exponent / row_total).astype(bf16)
        log_total = row_peak + jnp.log(row_total)
        mixed = (
            jnp.einsum("hgqk,khd->qhgd", probs_low, value_heads, preferred_element_type=f32)
            .reshape(token_rows, QUERY_HEADS * HEAD_SIZE)
            .astype(bf16)
        )
        stream_mid = stream + mm(mixed, w_out)
        normed_ffn, ffn_inverse = norm_forward(stream_mid, ffn_gains[i])
        routed = normed_ffn.astype(bf16)
        gates = chosen_softmax(mm_nt(routed, routers[i]), chosen_here)
        arrived = dispatch(routed)
        produced, kept = expert_forward(i, arrived)
        stored.append(
            dict(
                stream=stream,
                attn_inverse=attn_inverse,
                hidden=hidden,
                query_heads=query_heads,
                key_heads=key_heads,
                value_heads=value_heads,
                log_total=log_total,
                mixed=mixed,
                stream_mid=stream_mid,
                ffn_inverse=ffn_inverse,
                routed=routed,
                gates=gates,
                arrived=arrived,
                kept=kept,
            )
        )
        stream = stream_mid + give_back(produced)
    output = stream.astype(bf16)

    upstream = cotangent.astype(f32)
    d_arrived = d_arrived_last
    grads = [None] * layer_count
    for i in reversed(range(layer_count)):
        w_query, w_kv, w_out = gathered[i]
        saved = stored[i]
        if i < layer_count - 1:
            d_arrived = dispatch(upstream.astype(bf16))
        d_rows, d_gate_rows, both_grad, down_grad = expert_backward(
            i, saved["arrived"], saved["kept"], d_arrived
        )
        d_gates = gate_grads_back(d_gate_rows)
        gates = saved["gates"]
        d_logits = gates * (d_gates - jnp.sum(gates * d_gates, axis=1, keepdims=True))
        d_logits = d_logits.astype(bf16)
        router_grad = mm_tn(d_logits, saved["routed"])
        d_routed = give_back(d_rows) + mm(d_logits, routers[i])
        d_stream, ffn_gain_grad = norm_backward(
            saved["stream_mid"], saved["ffn_inverse"], ffn_gains[i], d_routed
        )
        upstream = upstream + d_stream
        d_branch = upstream.astype(bf16)
        mixed = saved["mixed"]
        d_mixed = (
            mm_nt(d_branch, w_out)
            .astype(bf16)
            .reshape(token_rows, KEY_VALUE_HEADS, group_width, HEAD_SIZE)
        )
        out_grad = scattered_product(split_columns(mixed), d_branch)
        out_grad = sum_over_experts(lines, out_grad)
        query_heads, key_heads = saved["query_heads"], saved["key_heads"]
        value_heads = saved["value_heads"]
        raw_scores = jnp.einsum(
            "qhgd,khd->hgqk", query_heads, key_heads, preferred_element_type=f32
        )
        scores = jnp.where(visible, raw_scores * score_scale, masked_score)
        probs_full = jnp.exp(scores - saved["log_total"])
        d_probs = jnp.einsum("qhgd,khd->hgqk", d_mixed, value_heads, preferred_element_type=f32)
        d_scores = (
            probs_full * (d_probs - jnp.sum(probs_full * d_probs, axis=-1, keepdims=True))
        ).astype(bf16)
        probs_low = probs_full.astype(bf16)
        d_value_all = jnp.einsum(
            "hgqk,qhgd->khd", probs_low, d_mixed, preferred_element_type=f32
        ).reshape(sequence_length, kv_width)
        d_key_all = (
            jnp.einsum("hgqk,qhgd->khd", d_scores, query_heads, preferred_element_type=f32)
            * score_scale
        ).reshape(sequence_length, kv_width)
        d_kv = jnp.concatenate([d_key_all, d_value_all], axis=1)
        pair_rows = 2 * token_rows
        d_kv_pair = d_kv[:pair_rows] + core_swap(d_kv[pair_rows:].astype(bf16)).astype(f32)
        d_kv_own = d_kv_pair[:token_rows] + row_swap(d_kv_pair[token_rows:].astype(bf16)).astype(
            f32
        )
        d_query = (
            jnp.einsum("hgqk,khd->qhgd", d_scores, key_heads, preferred_element_type=f32)
            * score_scale
        ).reshape(token_rows, QUERY_HEADS * HEAD_SIZE)
        d_q_low = rotary_apply(d_query, tables, QUERY_HEADS, -1.0).astype(bf16)
        d_kv_low = jnp.concatenate(
            [
                rotary_apply(d_kv_own[:, :kv_width], tables, KEY_VALUE_HEADS, -1.0),
                d_kv_own[:, kv_width:],
            ],
            axis=1,
        ).astype(bf16)
        d_hidden = mm_nt(d_q_low, w_query) + mm_nt(d_kv_low, w_kv)
        d_stream, attn_gain_grad = norm_backward(
            saved["stream"], saved["attn_inverse"], attn_gains[i], d_hidden
        )
        upstream = upstream + d_stream
        hidden_columns = split_columns(saved["hidden"])
        q_grad = sum_over_experts(lines, scattered_product(hidden_columns, d_q_low))
        kv_grad = sum_over_experts(lines, scattered_product(hidden_columns, d_kv_low))
        small_grad = jnp.concatenate(
            [router_grad, attn_gain_grad[None, :], ffn_gain_grad[None, :]], axis=0
        )
        grads[i] = (
            q_grad,
            kv_grad[:, :kv_width],
            kv_grad[:, kv_width:],
            out_grad,
            small_grad,
            both_grad[:, :hidden_units],
            both_grad[:, hidden_units:],
            down_grad,
        )
    input_grad = upstream.astype(bf16)
    stacked = [jnp.stack([grads[i][k] for i in range(layer_count)], axis=0) for k in range(8)]
    small_sum = lax.psum(stacked[4], ("expert", "shard"))
    own_width = model_width // shard_count
    small_sum = lax.dynamic_slice(
        small_sum, (0, 0, mine * own_width), (layer_count, experts + 2, own_width)
    )
    return (
        output,
        input_grad,
        stacked[0],
        stacked[1],
        stacked[2],
        stacked[3],
        small_sum[:, :experts].transpose(0, 2, 1),
        small_sum[:, experts],
        small_sum[:, experts + 1],
        stacked[5][:, None],
        stacked[6][:, None],
        stacked[7][:, None],
    )


def solution(mesh):
    tokens_spec = P(("expert", "shard"), None)
    shard_spec = P(None, "shard", None)
    expert_spec = P(None, "expert", None, None)
    expert_grad_spec = P(None, "expert", "shard", None)
    return jax.shard_map(
        per_device,
        mesh=mesh,
        in_specs=(
            tokens_spec,
            P("expert", None),
            tokens_spec,
            tokens_spec,
            tokens_spec,
            shard_spec,
            shard_spec,
            shard_spec,
            shard_spec,
            shard_spec,
            P(None, "shard"),
            P(None, "shard"),
            expert_spec,
            expert_spec,
            expert_spec,
        ),
        out_specs=(
            tokens_spec,
            tokens_spec,
            shard_spec,
            shard_spec,
            shard_spec,
            shard_spec,
            shard_spec,
            P(None, "shard"),
            P(None, "shard"),
            expert_grad_spec,
            expert_grad_spec,
            expert_grad_spec,
        ),
        check_vma=False,
    )
```

```python
import jax
import jax.numpy as jnp
from jax import lax
from jax.experimental import pallas as pl
from jax.experimental.pallas import tpu as pltpu
from jax.sharding import PartitionSpec as P

QUERY_HEADS = 12
KEY_VALUE_HEADS = 2
HEAD_SIZE = 128

norm_eps = 1e-06
rope_base = 10000.0
masked_score = -1e30

bf16 = jnp.bfloat16
f32 = jnp.float32


def mm(left, right):
    return jnp.dot(left, right, preferred_element_type=f32)


def mm_tn(left, right):
    return lax.dot_general(left, right, (((0,), (0,)), ((), ())), preferred_element_type=f32)


def mm_nt(left, right):
    return lax.dot_general(left, right, (((1,), (1,)), ((), ())), preferred_element_type=f32)


def norm_forward(values, gain):
    inverse = lax.rsqrt(jnp.mean(values * values, axis=-1, keepdims=True) + norm_eps)
    return values * inverse * gain, inverse


def norm_backward(values, inverse, gain, grad):
    scaled = grad * gain
    mean_part = jnp.mean(values * scaled, axis=-1, keepdims=True)
    d_values = inverse * scaled - values * (inverse * inverse * inverse * mean_part)
    d_gain = jnp.sum(grad * values * inverse, axis=0)
    return d_values, d_gain


def sync(*values):
    return lax.optimization_barrier(values)


def rotary_tables(position):
    half_width = HEAD_SIZE // 2
    frequency = rope_base ** (-(jnp.arange(half_width).astype(f32) * 2.0 / HEAD_SIZE))
    angles = position.astype(f32)[:, None] * frequency[None, :]
    cosine, sine = jnp.cos(angles), jnp.sin(angles)
    return jnp.concatenate([cosine, cosine], axis=1), jnp.concatenate([-sine, sine], axis=1)


def turned(values, cosine, sine):
    return values * cosine + pltpu.roll(values, HEAD_SIZE // 2, 1) * sine


def kernel_params():
    return pltpu.CompilerParams(vmem_limit_bytes=40 * 1024 * 1024)


def project_kv(hidden, w_kv, tables):
    rows, width = hidden.shape[0], w_kv.shape[1]

    def kernel(hidden_ref, w_ref, cos_ref, sin_ref, out_ref):
        value = jnp.dot(hidden_ref[...], w_ref[...], preferred_element_type=f32)
        for at in range(0, width, HEAD_SIZE):
            part = value[:, at : at + HEAD_SIZE]
            if at // HEAD_SIZE % 2 == 0:
                part = turned(part, cos_ref[...], sin_ref[...])
            out_ref[:, at : at + HEAD_SIZE] = part.astype(bf16)

    return pl.pallas_call(
        kernel,
        out_shape=jax.ShapeDtypeStruct((rows, width), bf16),
        compiler_params=kernel_params(),
        cost_estimate=pl.CostEstimate(
            flops=2 * rows * width * hidden.shape[1],
            bytes_accessed=2 * hidden.size + 2 * w_kv.size,
            transcendentals=0,
        ),
    )(hidden, w_kv, *tables)


def turn_kv_back(first, second, tables):
    rows, width = first.shape

    def kernel(first_ref, second_ref, cos_ref, sin_ref, out_ref):
        for at in range(0, width, HEAD_SIZE):
            columns = slice(at, at + HEAD_SIZE)
            part = first_ref[:, columns].astype(f32) + second_ref[:, columns].astype(f32)
            if at // HEAD_SIZE % 2 == 0:
                part = turned(part, cos_ref[...], -sin_ref[...])
            out_ref[:, columns] = part.astype(bf16)

    return pl.pallas_call(
        kernel,
        out_shape=jax.ShapeDtypeStruct((rows, width), bf16),
        compiler_params=kernel_params(),
    )(first, second, *tables)


def attend(q_pre, kv_all, tables, query_marks, key_marks):
    rows, width = q_pre.shape
    keys = kv_all.shape[0]
    heads = width // HEAD_SIZE
    group = heads // KEY_VALUE_HEADS
    scale = HEAD_SIZE ** (-0.5)

    def kernel(
        q_ref, kv_ref, cos_ref, sin_ref, qd_ref, qp_ref, kd_ref, kp_ref, turned_ref, out_ref, bias
    ):
        @pl.when(pl.program_id(0) == 0)
        def _():
            seen = (qd_ref[...] == kd_ref[...]) & (kp_ref[...] <= qp_ref[...])
            bias[...] = jnp.where(seen, 0.0, masked_score)

        query = turned(q_ref[...], cos_ref[...], sin_ref[...]).astype(bf16)
        turned_ref[...] = query
        scores = mm_nt(query, kv_ref[:, :HEAD_SIZE]) * scale + bias[...]
        weight = jnp.exp(scores - jnp.max(scores, axis=1, keepdims=True))
        total = jnp.sum(weight, axis=1, keepdims=True)
        probs = (weight * (1.0 / total)).astype(bf16)
        out_ref[...] = mm(probs, kv_ref[:, HEAD_SIZE:]).astype(bf16)

    fixed = lambda shape: pl.BlockSpec(shape, lambda h: (0, 0))
    by_head = pl.BlockSpec((rows, HEAD_SIZE), lambda h: (0, h))
    return pl.pallas_call(
        kernel,
        grid=(heads,),
        in_specs=[
            by_head,
            pl.BlockSpec((keys, 2 * HEAD_SIZE), lambda h: (0, h // group)),
            fixed((rows, HEAD_SIZE)),
            fixed((rows, HEAD_SIZE)),
            fixed((rows, 1)),
            fixed((rows, 1)),
            fixed((1, keys)),
            fixed((1, keys)),
        ],
        out_specs=[by_head, by_head],
        out_shape=[jax.ShapeDtypeStruct((rows, width), bf16)] * 2,
        scratch_shapes=[pltpu.VMEM((rows, keys), f32)],
        compiler_params=kernel_params(),
        cost_estimate=pl.CostEstimate(
            flops=8 * rows * keys * width,
            bytes_accessed=8 * rows * width,
            transcendentals=rows * keys * heads,
        ),
    )(
        q_pre,
        kv_all,
        *tables,
        query_marks[0][:, None],
        query_marks[1][:, None],
        key_marks[0][None, :],
        key_marks[1][None, :],
    )


def attend_back(query, kv_all, d_mixed, tables, query_marks, key_marks):
    rows, width = query.shape
    keys = kv_all.shape[0]
    heads = width // HEAD_SIZE
    group = heads // KEY_VALUE_HEADS
    scale = HEAD_SIZE ** (-0.5)

    def kernel(
        q_ref, kv_ref, dm_ref, cos_ref, sin_ref, qd_ref, qp_ref, kd_ref, kp_ref, dq_ref, dkv_ref,
        bias, dkv,
    ):
        head = pl.program_id(0)

        @pl.when(head == 0)
        def _():
            seen = (qd_ref[...] == kd_ref[...]) & (kp_ref[...] <= qp_ref[...])
            bias[...] = jnp.where(seen, 0.0, masked_score)

        query, key, value = q_ref[...], kv_ref[:, :HEAD_SIZE], kv_ref[:, HEAD_SIZE:]
        d_out = dm_ref[...]
        scores = mm_nt(key, query) * scale + bias[...]
        weight = jnp.exp(scores - jnp.max(scores, axis=0, keepdims=True))
        probs = weight * (1.0 / jnp.sum(weight, axis=0, keepdims=True))
        d_probs = mm_nt(value, d_out)
        mean = jnp.sum(probs * d_probs, axis=0, keepdims=True)
        d_scores = (probs * (d_probs - mean)).astype(bf16)
        d_value = mm(probs.astype(bf16), d_out)
        d_key = mm(d_scores, query) * scale
        d_query = mm_tn(d_scores, key) * scale
        dq_ref[...] = turned(d_query, cos_ref[...], -sin_ref[...]).astype(bf16)

        @pl.when(head % group == 0)
        def _():
            dkv[:, :HEAD_SIZE] = d_key
            dkv[:, HEAD_SIZE:] = d_value

        @pl.when(head % group != 0)
        def _():
            dkv[:, :HEAD_SIZE] += d_key
            dkv[:, HEAD_SIZE:] += d_value

        @pl.when(head % group == group - 1)
        def _():
            dkv_ref[...] = dkv[...].astype(bf16)

    fixed = lambda shape: pl.BlockSpec(shape, lambda h: (0, 0))
    by_head = pl.BlockSpec((rows, HEAD_SIZE), lambda h: (0, h))
    by_group = pl.BlockSpec((keys, 2 * HEAD_SIZE), lambda h: (0, h // group))
    return pl.pallas_call(
        kernel,
        grid=(heads,),
        in_specs=[
            by_head,
            by_group,
            by_head,
            fixed((rows, HEAD_SIZE)),
            fixed((rows, HEAD_SIZE)),
            fixed((1, rows)),
            fixed((1, rows)),
            fixed((keys, 1)),
            fixed((keys, 1)),
        ],
        out_specs=[by_head, by_group],
        out_shape=[
            jax.ShapeDtypeStruct((rows, width), bf16),
            jax.ShapeDtypeStruct(kv_all.shape, bf16),
        ],
        scratch_shapes=[pltpu.VMEM((keys, rows), f32), pltpu.VMEM((keys, 2 * HEAD_SIZE), f32)],
        compiler_params=kernel_params(),
        cost_estimate=pl.CostEstimate(
            flops=20 * rows * keys * width,
            bytes_accessed=8 * rows * width,
            transcendentals=rows * keys * heads,
        ),
    )(
        query,
        kv_all,
        d_mixed,
        *tables,
        query_marks[0][None, :],
        query_marks[1][None, :],
        key_marks[0][:, None],
        key_marks[1][:, None],
    )


def documents(lengths_row, position):
    doc_ends = jnp.cumsum(lengths_row)
    doc_starts = doc_ends - lengths_row
    document_index = jnp.sum((position[:, None] >= doc_ends[None, :]).astype(jnp.int32), axis=1)
    doc_first = jnp.max(
        jnp.where(doc_starts[None, :] <= position[:, None], doc_starts[None, :], 0), axis=1
    )
    return (document_index, position - doc_first)


def slot_table(routes, order_row, experts, capacity):
    token_rows, top_count = routes.shape
    pair_count = token_rows * top_count
    pairs = jnp.arange(pair_count, dtype=jnp.int32)
    named = (order_row[:, None] == pairs[None, :]).astype(bf16)
    of_pair = (
        routes.reshape(pair_count)[:, None] == jnp.arange(experts, dtype=jnp.int32)[None, :]
    ).astype(bf16)
    ranked = mm(named, of_pair)
    earlier = (pairs[None, :] < pairs[:, None]).astype(bf16)
    before = mm(earlier, ranked.astype(bf16))
    code = jnp.where(before < capacity, before + 1.0, -1.0) * ranked
    back = mm_tn(code.astype(bf16), named)
    return jnp.sum(back.reshape(experts, token_rows, top_count), axis=2)


def chosen_softmax(logits, chosen):
    top = jnp.max(jnp.where(chosen, logits, masked_score), axis=-1, keepdims=True)
    weight = jnp.where(chosen, jnp.exp(jnp.where(chosen, logits - top, 0.0)), 0.0)
    total = jnp.sum(weight, axis=-1, keepdims=True)
    return weight / jnp.where(total > 0.0, total, 1.0)


class Lines:
    def __init__(self):
        self.experts = lax.axis_size("expert")
        self.count = self.experts // 2
        self.index = lax.axis_index("expert")
        self.line = self.index // 2
        self.side = self.index % 2

    def source(self, slot):
        count, line = self.count, self.line
        low = jnp.where(line + slot < count, line + slot, count - 1 - slot)
        mirror = count - 1 - line
        high = count - 1 - jnp.where(mirror + slot < count, mirror + slot, count - 1 - slot)
        return jnp.where(line < count // 2, low, high)

    def swap(self, values):
        return lax.ppermute(values, "expert", [(i, i ^ 1) for i in range(self.experts)])

    def even(self, values):
        return lax.ppermute(values, "expert", [(i, i ^ 2) for i in range(self.experts)])

    def odd(self, values):
        count, shards = self.count, lax.axis_size("shard")
        pairs = []
        for i in range(count):
            end = i in (0, count - 1)
            other = i if end else i + 1 if i % 2 else i - 1
            for k in range(2):
                for j in range(shards):
                    to = (2 * other + k) * shards + (j ^ 1 if end else j)
                    pairs.append(((2 * i + k) * shards + j, to))
        return lax.ppermute(values, ("expert", "shard"), pairs)

    def choose(self, table):
        value, seen = None, {}
        for line, array in table.items():
            seen.setdefault(id(array), (array, []))[1].append(line)
        for array, lines in seen.values():
            if value is None:
                value = array
            else:
                here = jnp.any(self.line == jnp.array(lines))
                value = jnp.where(here, array, value)
        return value

    def step_gather(self, held):
        last = len(held) == self.count - 1
        even, odd = held[-1]
        return held + [(self.even(odd), None if last else self.odd(even))]

    def slot(self, held, slot):
        count = self.count
        table = {}
        for line in range(count):
            near = line if line < count // 2 else count - 1 - line
            toward = near + slot < count
            distance = slot if toward else near + slot + 1 - count
            above = toward == (line < count // 2)
            table[line] = held[distance][0 if above == (line % 2 == 0) else 1]
        return self.choose(table)

    def pick(self, blocks, distance, even):
        count, half = self.count, self.count // 2
        table = {}
        for line in range(count):
            up = even == (line % 2 == 0)
            if not 0 <= (line + distance if up else line - distance) < count:
                continue
            if up:
                slot = distance if line < half else line + distance
            else:
                slot = distance if line >= half else count - 1 - line + distance
            table[line] = blocks[slot]
        return self.choose(table) if table else None

    def step_reduce(self, step, blocks, arrived):
        distance = self.count - 1 - step
        even, odd = self.pick(blocks, distance, True), self.pick(blocks, distance, False)
        if arrived is not None:
            from_even, from_odd = self.inward(arrived)
            even = even + from_odd
            odd = odd + from_even
        sent = None if odd is None else self.odd(odd.astype(bf16))
        return self.even(even.astype(bf16)), sent

    def inward(self, arrived):
        even, odd = arrived
        if odd is None:
            return even.astype(f32), 0.0
        end = (self.line == 0) | (self.line == self.count - 1)
        return even.astype(f32), jnp.where(end, 0.0, odd.astype(f32))

    def turn(self, values, steps):
        pairs = [
            (2 * i + k, 2 * ((i + steps) % self.count) + k)
            for i in range(self.count)
            for k in range(2)
        ]
        return lax.ppermute(values, "expert", pairs)


def core_swap(values):
    return lax.ppermute(values, "shard", [(i, i ^ 1) for i in range(lax.axis_size("shard"))])


def row_swap(values):
    return lax.ppermute(values, "shard", [(i, i ^ 2) for i in range(lax.axis_size("shard"))])


def column_units(lines):
    mine = lax.axis_index("shard")
    units = []
    for mask in (0, 1, 2, 3):
        first = lines.side if mask >= 2 else 0
        units += [(mine ^ mask) * 2 + first, (mine ^ mask) * 2 + 1 - first]
    return units


def ordered_columns(values, units):
    width = values.shape[1] // 8
    return jnp.concatenate(
        [lax.dynamic_slice(values, (0, unit * width), (values.shape[0], width)) for unit in units],
        axis=1,
    )


def ordered_small(blocks):
    mine = lax.axis_index("shard")
    shape = blocks[0].shape
    whole = jnp.zeros(shape[:-1] + (4 * shape[-1],), blocks[0].dtype)
    for mask, block in blocks.items():
        at = (0,) * (len(shape) - 1) + ((mine ^ mask) * shape[-1],)
        whole = lax.dynamic_update_slice(whole, block, at)
    return whole


def split_columns(values):
    mine = lax.axis_index("shard")
    width = values.shape[1] // 4
    return [
        lax.dynamic_slice(values, (0, (mine ^ mask) * width), (values.shape[0], width))
        for mask in range(4)
    ]


def shard_rows_of(values):
    return jnp.concatenate([values, row_swap(values)], axis=0)


def shard_rows_all(pair):
    return jnp.concatenate([pair, core_swap(pair)], axis=0)


def exchange_blocks(blocks):
    pairs = lambda mask: [(i, i ^ mask) for i in range(lax.axis_size("shard"))]
    return [blocks[0]] + [lax.ppermute(blocks[r], "shard", pairs(r)) for r in (2, 1, 3)]


def own_columns(values):
    return jnp.concatenate(exchange_blocks(split_columns(values)), axis=0)


class Summed:
    def __init__(self, lines, part):
        self.lines = lines
        self.part = part
        self.value = ()

    def side(self):
        part = self.part
        half = part.shape[0] // 2
        lines = self.lines
        given = lax.dynamic_slice(part, ((1 - lines.side) * half, 0), (half, part.shape[1]))
        self.kept = lax.dynamic_slice(part, (lines.side * half, 0), (half, part.shape[1]))
        self.value = lines.swap(given.astype(bf16))

    def place(self, steps):
        return (self.lines.line + steps) % self.lines.count

    def scatter(self):
        lines = self.lines
        part = (self.kept + self.value.astype(f32)).reshape(lines.count, -1, self.kept.shape[1])
        low = part.astype(bf16)
        take = lambda steps, x: lax.dynamic_index_in_dim(x, self.place(steps), 0, keepdims=False)
        self.kept = take(0, part)
        self.value = tuple(
            lines.turn(take(steps, low), steps) for steps in range(1, lines.count)
        )

    def spread(self):
        own = self.kept
        for came in self.value:
            own = own + came.astype(f32)
        self.kept = own.astype(bf16)
        self.value = tuple(
            self.lines.turn(self.kept, -steps) for steps in range(1, self.lines.count)
        )

    def join(self):
        lines = self.lines
        blocks = jnp.zeros((lines.count,) + self.kept.shape, bf16)
        for steps, block in enumerate((self.kept,) + self.value):
            blocks = lax.dynamic_update_slice(blocks, block[None], (self.place(steps), 0, 0))
        self.kept = blocks.reshape(-1, self.kept.shape[1])
        self.value = lines.swap(self.kept)

    def whole(self):
        low = self.lines.side == 0
        first = jnp.where(low, self.kept, self.value)
        second = jnp.where(low, self.value, self.kept)
        return jnp.concatenate([first, second], axis=0).astype(f32)


class Sent:
    def __init__(self, routing, values):
        self.routing = routing
        self.held = [(values, values)]
        rows = 2 * routing.lines.count * routing.capacity
        self.buffer = jnp.zeros((rows, values.shape[1]), values.dtype)
        self.far = None

    @property
    def value(self):
        return self.held[-1], self.buffer, self.far

    @value.setter
    def value(self, value):
        self.held[-1], self.buffer, self.far = value

    def step(self):
        self.held = self.routing.lines.step_gather(self.held)

    def put(self, rows, block):
        at = block * self.routing.capacity
        self.buffer = lax.dynamic_update_slice(self.buffer, rows, (at, 0))

    def pack(self, j):
        routing = self.routing
        block = routing.lines.slot(self.held, j)
        arrived = self.far
        self.far = routing.lines.swap(mm(routing.mate_hot[j], block).astype(bf16))
        if arrived is not None:
            self.put(arrived, routing.lines.count + j - 1)
        self.put(mm(routing.own_hot[j], block).astype(bf16), j)

    def total(self):
        if self.far is not None:
            self.put(self.far, 2 * self.routing.lines.count - 1)
            self.far = None
        return self.buffer


class Returned:
    def __init__(self, routing, rows):
        self.routing = routing
        count, capacity = routing.lines.count, routing.capacity
        self.blocks = [rows[i * capacity : (i + 1) * capacity] for i in range(2 * count)]
        self.parts = [None] * count
        self.round = 0
        self.value = (None, None)

    def spread(self, j):
        own, far = self.routing.own_hot[j], self.routing.mate_hot[j]
        self.parts[j] = mm_tn(own, self.blocks[j]) + mm_tn(far, self.value[0])

    def advance(self):
        lines = self.routing.lines
        j = lines.count - 1 - self.round
        arrived = self.value[1]
        if self.round > 0:
            self.spread(j + 1)
            arrived = lines.step_reduce(self.round - 1, self.parts, arrived)
        self.value = (lines.swap(self.blocks[lines.count + j]), arrived)
        self.round += 1

    def total(self):
        self.spread(0)
        from_even, from_odd = self.routing.lines.inward(self.value[1])
        return self.parts[0] + from_even + from_odd


def settle(moving, *values):
    arrived, values = sync([m.value for m in moving], values)
    for m, value in zip(moving, arrived, strict=True):
        m.value = value
    return values


class Routing:
    pass


def per_device(
    tokens,
    lengths,
    routes,
    slot_order,
    cotangent,
    q_weight,
    key_matrix,
    value_matrix,
    out_weight,
    router_weight,
    attn_gain,
    ffn_gain,
    gate_weight,
    up_weight,
    down_weight,
):
    lines = Lines()
    layer_count = q_weight.shape[0]
    shard_count = lax.axis_size("shard")
    mine = lax.axis_index("shard")
    token_rows, model_width = tokens.shape
    pair_count = token_rows * routes.shape[1]
    experts = router_weight.shape[2]
    assert shard_count == 4 and experts == lines.experts and gate_weight.shape[1] == 1
    hidden_units = gate_weight.shape[3]
    capacity = (pair_count * 5 + 4 * experts - 1) // (4 * experts)
    assert capacity < 256
    sequence_length = token_rows * shard_count
    kv_width = KEY_VALUE_HEADS * HEAD_SIZE

    own_rows = jnp.arange(token_rows, dtype=jnp.int32)
    position = mine * token_rows + own_rows
    key_position = jnp.concatenate([(mine ^ mask) * token_rows + own_rows for mask in (0, 2, 1, 3)])
    query_doc, query_position = documents(lengths[0], position)
    key_doc = documents(lengths[0], key_position)[0]
    tables = rotary_tables(query_position)
    query_marks, key_marks = (query_doc, position), (key_doc, key_position)

    def paired(i):
        parts = []
        for at in range(0, kv_width, HEAD_SIZE):
            parts += [key_matrix[i, :, at : at + HEAD_SIZE], value_matrix[i, :, at : at + HEAD_SIZE]]
        return jnp.concatenate(parts, axis=1)

    kv_shards = [paired(i) for i in range(layer_count)]
    small = jnp.concatenate(
        [router_weight.transpose(0, 2, 1), attn_gain[:, None, :], ffn_gain[:, None, :]], axis=1
    )
    routing = Routing()
    routing.lines, routing.capacity = lines, capacity
    late = Sent(routing, cotangent)
    units = column_units(lines)

    def side_half(shard):
        half = shard.shape[0] // 2
        return lax.dynamic_slice(shard, (lines.side * half, 0), (half, shard.shape[1]))

    def joined(shard, beside, across, crossed):
        far = jnp.concatenate([across, crossed], axis=0)
        return jnp.concatenate([shard, beside, far, core_swap(far)], axis=0)

    small_across, small_beside = row_swap(small), core_swap(small)
    kv_across, kv_beside = row_swap(side_half(kv_shards[0])), core_swap(kv_shards[0])
    own_table = slot_table(routes, slot_order[0], experts, capacity)
    first_query = q_weight[0]
    small_across, small_beside, kv_across, kv_beside, own_table, first_query = sync(
        small_across, small_beside, kv_across, kv_beside, own_table, first_query
    )

    query_across, query_beside = row_swap(side_half(first_query)), core_swap(first_query)
    kv_crossed = lines.swap(kv_across)
    late.step()
    small_diagonal = core_swap(small_across)
    small = ordered_small({0: small, 1: small_beside, 2: small_across, 3: small_diagonal})
    routers = [small[i, :experts] for i in range(layer_count)]
    attn_gains = [small[i, experts].astype(f32)[None, :] for i in range(layer_count)]
    ffn_gains = [small[i, experts + 1].astype(f32)[None, :] for i in range(layer_count)]
    stream = tokens.astype(f32)
    normed, attn_inverse = norm_forward(stream, attn_gains[0])
    hidden = normed.astype(bf16)
    matched = ordered_columns(hidden, units)
    first_out = out_weight[0]
    query_across, query_beside, kv_crossed, matched, own_table, first_out = settle(
        [late], query_across, query_beside, kv_crossed, matched, own_table, first_out
    )

    query_crossed = lines.swap(query_across)
    first_kv = joined(kv_shards[0], kv_beside, kv_across, kv_crossed)
    first_pair = shard_rows_of(project_kv(matched, first_kv, tables))
    held_tables = [(own_table, own_table)]
    for _ in range(lines.count - 1):
        held_tables = lines.step_gather(held_tables)
    near_tables = jnp.stack([lines.slot(held_tables, j) for j in range(lines.count)], axis=0)
    later = [q_weight[0], kv_shards[0]]
    for i in range(1, layer_count):
        later += [kv_shards[i], q_weight[i], out_weight[i]]
    query_crossed, first_pair, near_tables, later = sync(
        query_crossed, first_pair, near_tables, later
    )
    first_query = joined(first_query, query_beside, query_across, query_crossed)

    whole = [lax.all_gather(part, "shard", axis=0, tiled=True) for part in [first_out] + later]
    gathered = [(whole[1], whole[2], whole[0])]
    for i in range(1, layer_count):
        gathered.append((whole[3 * i + 1], whole[3 * i], whole[3 * i + 2]))

    chosen_here = own_table.T != 0.0
    far_tables = lines.swap(near_tables)
    slot_code = jnp.arange(1, capacity + 1, dtype=jnp.int32).astype(f32)[:, None]

    def hot_rows(codes, expert):
        code = lax.dynamic_index_in_dim(codes, expert, 1, keepdims=True)
        return (code == slot_code).astype(bf16)

    routing.own_hot = hot_rows(near_tables, lines.index)
    routing.mate_hot = hot_rows(near_tables, lines.index ^ 1)
    all_hot = jnp.concatenate([routing.own_hot, hot_rows(far_tables, lines.index)], axis=0)
    all_tables = jnp.concatenate([near_tables, far_tables], axis=0)
    row_chosen = jnp.einsum(
        "sct,set->sce", all_hot, (all_tables != 0.0).astype(bf16), preferred_element_type=f32
    ).reshape(2 * lines.count * capacity, experts)
    row_chosen = row_chosen > 0.5
    sources = [
        lines.source(slot) * 2 + (lines.side ^ column)
        for column in range(2)
        for slot in range(lines.count)
    ]

    def gate_grads_back(row_values):
        blocks = row_values.reshape(2 * lines.count, capacity)
        spread = jnp.zeros((experts, token_rows), f32)
        rows = jnp.sum(all_hot.astype(f32) * blocks[:, :, None], axis=1)
        for i, source in enumerate(sources):
            spread = lax.dynamic_update_slice(spread, rows[i : i + 1], (source, 0))
        return lax.all_to_all(spread, "expert", split_axis=0, concat_axis=0, tiled=True).T

    def expert_forward(i, arrived):
        gates = chosen_softmax(mm_nt(arrived, routers[i]), row_chosen)
        own_gate = lax.dynamic_slice(gates, (0, lines.index), (gates.shape[0], 1))
        gate_pre = mm(arrived, gate_weight[i, 0])
        up_pre = mm(arrived, up_weight[i, 0])
        active = jax.nn.gelu(gate_pre, approximate=True) * up_pre
        gated = (own_gate * active).astype(bf16)
        produced = mm(gated, down_weight[i, 0]).astype(bf16)
        return produced, dict(gate=own_gate, gate_pre=gate_pre, up_pre=up_pre, gated=gated)

    def expert_backward(i, kept, d_arrived):
        du = mm_nt(d_arrived, down_weight[i, 0])
        unit, pull = jax.vjp(
            lambda a, b: jax.nn.gelu(a, approximate=True) * b, kept["gate_pre"], kept["up_pre"]
        )
        d_gate_rows = jnp.sum(du * unit, axis=1)
        d_active = (kept["gate"] * du).astype(bf16).astype(f32)
        d_gate_pre, d_up_pre = pull(d_active)
        d_both = jnp.concatenate([d_gate_pre.astype(bf16), d_up_pre.astype(bf16)], axis=1)
        return d_gate_rows, d_both

    def expert_rows(i, d_both):
        d_rows = mm_nt(d_both[:, :hidden_units], gate_weight[i, 0])
        return (d_rows + mm_nt(d_both[:, hidden_units:], up_weight[i, 0])).astype(bf16)

    def shard_sum(part):
        return lax.psum_scatter(part, "shard", scatter_dimension=0, tiled=True)

    def small_sum(part):
        own = sum(exchange_blocks(split_columns(part)))
        return jnp.pad(own, ((0, -own.shape[0] % 128), (0, 0))).T

    last = layer_count - 1
    stored = []
    for i in range(layer_count):
        w_query, w_kv, w_out = gathered[i]
        if i == 0:
            late.step()
            late.pack(0)
            kv_pair = first_pair
            q_pre = mm(matched, first_query)
        else:
            if i == last:
                late.pack(2)
            normed, attn_inverse = norm_forward(stream, attn_gains[i])
            hidden = normed.astype(bf16)
            kv_pair = shard_rows_of(project_kv(hidden, w_kv, tables))
            q_pre = mm(hidden, w_query)
            kv_pair, q_pre = settle([late], kv_pair, q_pre)
            if i == last:
                late.pack(3)
        kv_all = shard_rows_all(kv_pair)
        query, mixed = attend(q_pre, kv_all, tables, query_marks, key_marks)
        stream_mid = stream + mm(mixed, w_out)
        normed_ffn, ffn_inverse = norm_forward(stream_mid, ffn_gains[i])
        routed = normed_ffn.astype(bf16)
        (routed,) = settle([late], routed)
        gates = chosen_softmax(mm_nt(routed, routers[i]), chosen_here)
        sent = Sent(routing, routed)
        for j in range(lines.count):
            if j < lines.count - 1:
                sent.step()
            sent.pack(j)
            if i == last and j == 0:
                late.total()
            hidden, mixed = settle([sent, late], hidden, mixed)
        columns = [own_columns(hidden), own_columns(mixed)]
        arrived = sent.total()
        if i == 0:
            (arrived,) = settle([late], arrived)
            late.step()
            late.pack(1)
        produced, kept = expert_forward(i, arrived)
        produced, kept = settle([late], produced, kept)
        stored.append(
            dict(
                stream=stream,
                attn_inverse=attn_inverse,
                hidden_columns=columns[0],
                query=query,
                kv_all=kv_all,
                mixed_columns=columns[1],
                stream_mid=stream_mid,
                ffn_inverse=ffn_inverse,
                routed=routed,
                gates=gates,
                arrived=arrived,
                kept=kept,
            )
        )
        back = Returned(routing, produced)
        if i < last:
            for _ in range(lines.count):
                back.advance()
                settle([back])
            stream = stream_mid + back.total()

    output_back = back
    output_back.advance()
    d_arrived = late.total()
    upstream = cotangent.astype(f32)
    grads = [None] * layer_count
    for i in reversed(range(layer_count)):
        w_query, w_kv, w_out = gathered[i]
        saved = stored[i]
        if i < last:
            sent = Sent(routing, upstream.astype(bf16))
            above = stored[i + 1]
            d_branch, d_query, d_kv_low = waiting
            for j in range(lines.count):
                if j < lines.count - 1:
                    sent.step()
                sent.pack(j)
                if j == 0:
                    d_branch = shard_rows_of(d_branch)
                    small_part = small_sum(small_grad)
                if j == 1:
                    d_query = shard_rows_of(d_query)
                    d_branch = shard_rows_all(d_branch)
                if j == 2:
                    out_part = mm_tn(above["mixed_columns"], d_branch).astype(bf16)
                    d_kv_low = shard_rows_of(d_kv_low)
                    d_query = shard_rows_all(d_query)
                if j == 3:
                    d_kv_low = shard_rows_all(d_kv_low)
                    q_part = mm_tn(above["hidden_columns"], d_query).astype(bf16)
                d_branch, d_query, d_kv_low = settle([sent], d_branch, d_query, d_kv_low)
            kv_part = mm_tn(above["hidden_columns"], d_kv_low).astype(bf16)
            part = jnp.concatenate([q_part, out_part, kv_part, small_part.astype(bf16)], axis=1)
            last_sum = Summed(lines, part)
            last_sum.side()
            last_experts = expert_grads
            d_arrived = sent.total()
        d_gate_rows, d_both = expert_backward(i, saved["kept"], d_arrived)
        if i == last:
            d_gate_rows, d_both = settle([output_back], d_gate_rows, d_both)
            output_back.advance()
            d_rows = expert_rows(i, d_both)
            d_rows, d_gate_rows, d_both = settle([output_back], d_rows, d_gate_rows, d_both)
        else:
            d_rows = expert_rows(i, d_both)
            d_rows, d_gate_rows, d_both = settle([last_sum], d_rows, d_gate_rows, d_both)
        d_gates = gate_grads_back(d_gate_rows)
        back = Returned(routing, d_rows)
        arrived, gated = saved["arrived"], saved["kept"]["gated"]
        for j in range(lines.count):
            back.advance()
            extra = ()
            if j == 0:
                extra = mm_tn(arrived, d_both).astype(bf16)
            if j == 1:
                extra = mm_tn(gated, d_arrived).astype(bf16)
            extra, d_gates, arrived, gated, d_both, d_arrived = settle(
                [back], extra, d_gates, arrived, gated, d_both, d_arrived
            )
            if j == 0:
                both_grad = shard_sum(extra).astype(f32)
            if j == 1:
                down_grad = shard_sum(extra).astype(f32)
        expert_grads = (both_grad, down_grad)
        gates = saved["gates"]
        d_logits = gates * (d_gates - jnp.sum(gates * d_gates, axis=1, keepdims=True))
        d_logits = d_logits.astype(bf16)
        router_grad = mm_tn(d_logits, saved["routed"])
        d_routed = back.total() + mm(d_logits, routers[i])
        d_stream, ffn_gain_grad = norm_backward(
            saved["stream_mid"], saved["ffn_inverse"], ffn_gains[i], d_routed
        )
        upstream = upstream + d_stream
        d_branch = upstream.astype(bf16)
        d_mixed = mm_nt(d_branch, w_out).astype(bf16)
        if i == last:
            output_back.advance()
            moving = [output_back]
            d_branch_all = ()
        else:
            last_sum.scatter()
            moving = [last_sum]
            d_branch_all = shard_rows_all(shard_rows_of(d_branch))
        d_query, d_kv = attend_back(
            saved["query"], saved["kv_all"], d_mixed, tables, query_marks, key_marks
        )
        d_query, d_kv, d_branch_all = settle(moving, d_query, d_kv, d_branch_all)
        if i == last:
            output_back.advance()
            sums = [output_back]
        else:
            out_sum = Summed(lines, mm_tn(saved["mixed_columns"], d_branch_all))
            out_sum.side()
            last_sum.spread()
            sums = [out_sum, last_sum]
        pair_rows = 2 * token_rows
        d_kv_pair = d_kv[:pair_rows].astype(f32) + core_swap(d_kv[pair_rows:]).astype(f32)
        d_hidden = mm_nt(d_query, w_query)
        d_kv_pair, d_hidden, d_query = sync(d_kv_pair, d_hidden, d_query)
        d_kv_crossed = row_swap(d_kv_pair[token_rows:].astype(bf16))
        if i < last:
            d_query_pair = shard_rows_of(d_query)
        d_kv_low = turn_kv_back(d_kv_pair[:token_rows], d_kv_crossed, tables)
        d_hidden = d_hidden + mm_nt(d_kv_low, w_kv)
        d_stream, attn_gain_grad = norm_backward(
            saved["stream"], saved["attn_inverse"], attn_gains[i], d_hidden
        )
        upstream = upstream + d_stream
        small_grad = jnp.concatenate(
            [router_grad, attn_gain_grad[None, :], ffn_gain_grad[None, :]], axis=0
        )
        if i == last:
            upstream, d_kv_low, small_grad = settle(sums, upstream, d_kv_low, small_grad)
            output = (saved["stream_mid"] + output_back.total()).astype(bf16)
            waiting = (d_branch, d_query, d_kv_low)
            upstream, output, waiting = sync(upstream, output, waiting)
        else:
            d_query_pair, d_kv_low, small_grad, upstream = settle(
                sums, d_query_pair, d_kv_low, small_grad, upstream
            )
            out_sum.scatter()
            d_kv_pair = shard_rows_of(d_kv_low)
            small_part = small_sum(small_grad)
            hidden_columns = saved["hidden_columns"]
            q_sum = Summed(lines, mm_tn(hidden_columns, shard_rows_all(d_query_pair)))
            q_sum.side()
            d_kv_pair, small_part = settle([q_sum, out_sum], d_kv_pair, small_part)
            kv_part = mm_tn(hidden_columns, shard_rows_all(d_kv_pair))
            kv_sum = Summed(lines, jnp.concatenate([kv_part, small_part], axis=1))
            for sends in (
                (q_sum.scatter, kv_sum.side, last_sum.join),
                (q_sum.spread, kv_sum.scatter, out_sum.spread),
                (q_sum.join, kv_sum.spread, out_sum.join),
                (kv_sum.join,),
            ):
                for send in sends:
                    send()
                settle([q_sum, kv_sum, out_sum, last_sum])
            grads[i] = (q_sum.whole(), kv_sum.whole(), out_sum.whole()) + expert_grads
            above = last_sum.whole()
            width = model_width
            grads[last] = (above[:, :width], above[:, 2 * width :], above[:, width : 2 * width])
            grads[last] += last_experts
    input_grad = upstream.astype(bf16)
    stacked = [jnp.stack([grads[i][k] for i in range(layer_count)], axis=0) for k in range(5)]
    q_grad, kv_grad, out_grad, both_grad, down_grad = stacked
    kv_parts = [kv_grad[:, :, at : at + HEAD_SIZE] for at in range(0, 2 * kv_width, HEAD_SIZE)]
    small_grad = kv_grad[:, :, 2 * kv_width :]
    return (
        output,
        input_grad,
        q_grad,
        jnp.concatenate(kv_parts[0::2], axis=2),
        jnp.concatenate(kv_parts[1::2], axis=2),
        out_grad,
        small_grad[:, :, :experts],
        small_grad[:, :, experts],
        small_grad[:, :, experts + 1],
        both_grad[:, None, :, :hidden_units],
        both_grad[:, None, :, hidden_units:],
        down_grad[:, None],
    )


def solution(mesh):
    tokens_spec = P(("expert", "shard"), None)
    shard_spec = P(None, "shard", None)
    expert_spec = P(None, "expert", None, None)
    expert_grad_spec = P(None, "expert", "shard", None)
    return jax.shard_map(
        per_device,
        mesh=mesh,
        in_specs=(
            tokens_spec,
            P("expert", None),
            tokens_spec,
            tokens_spec,
            tokens_spec,
            shard_spec,
            shard_spec,
            shard_spec,
            shard_spec,
            shard_spec,
            P(None, "shard"),
            P(None, "shard"),
            expert_spec,
            expert_spec,
            expert_spec,
        ),
        out_specs=(
            tokens_spec,
            tokens_spec,
            shard_spec,
            shard_spec,
            shard_spec,
            shard_spec,
            shard_spec,
            P(None, "shard"),
            P(None, "shard"),
            expert_grad_spec,
            expert_grad_spec,
            expert_grad_spec,
        ),
        check_vma=False,
    )
```

```python
import math

import jax
import jax.numpy as jnp
from jax import lax
from jax.experimental import pallas as pl
from jax.experimental.pallas import tpu as pltpu
from jax.sharding import PartitionSpec as P

QUERY_HEADS = 12
KEY_VALUE_HEADS = 2
HEAD_SIZE = 128

norm_eps = 1e-06
rope_base = 10000.0
masked_score = -1e30

bf16 = jnp.bfloat16
f32 = jnp.float32


def mm(left, right):
    return jnp.dot(left, right, preferred_element_type=f32)


def mm_tn(left, right):
    return lax.dot_general(left, right, (((0,), (0,)), ((), ())), preferred_element_type=f32)


def mm_nt(left, right):
    return lax.dot_general(left, right, (((1,), (1,)), ((), ())), preferred_element_type=f32)


def norm_forward(values, gain):
    inverse = lax.rsqrt(jnp.mean(values * values, axis=-1, keepdims=True) + norm_eps)
    return values * inverse * gain, inverse


def norm_backward(values, inverse, gain, grad):
    scaled = grad * gain
    mean_part = jnp.mean(values * scaled, axis=-1, keepdims=True)
    d_values = inverse * scaled - values * (inverse * inverse * inverse * mean_part)
    d_gain = jnp.sum(grad * values * inverse, axis=0)
    return d_values, d_gain


def sync(*values):
    return lax.optimization_barrier(values)


def rotary_tables(position):
    half_width = HEAD_SIZE // 2
    frequency = rope_base ** (-(jnp.arange(half_width).astype(f32) * 2.0 / HEAD_SIZE))
    angles = position.astype(f32)[:, None] * frequency[None, :]
    cosine, sine = jnp.cos(angles), jnp.sin(angles)
    return jnp.concatenate([cosine, cosine], axis=1), jnp.concatenate([-sine, sine], axis=1)


def turned(values, cosine, sine):
    return values * cosine + pltpu.roll(values, HEAD_SIZE // 2, 1) * sine


def kernel_params():
    return pltpu.CompilerParams(vmem_limit_bytes=40 * 1024 * 1024)


def project(parts, weights, tables=None):
    rows, width = parts[0].shape[0], weights[0].shape[1]
    tile = width if tables else width // 3
    count = len(parts)

    def kernel(*refs):
        out_ref = refs[-1]
        value = mm(refs[0][...], refs[count][...])
        for k in range(1, count):
            value = value + mm(refs[k][...], refs[count + k][...])
        if tables is None:
            out_ref[...] = value
            return
        for at in range(0, width, HEAD_SIZE):
            part = value[:, at : at + HEAD_SIZE]
            if at // HEAD_SIZE % 2 == 0:
                part = turned(part, refs[2 * count][...], refs[2 * count + 1][...])
            out_ref[:, at : at + HEAD_SIZE] = part.astype(bf16)

    fixed = lambda x: pl.BlockSpec(x.shape, lambda t: (0, 0))
    columns = lambda x: pl.BlockSpec((x.shape[0], tile), lambda t: (0, t))
    extra = list(tables) if tables else []
    return pl.pallas_call(
        kernel,
        grid=(width // tile,),
        in_specs=[fixed(x) for x in parts]
        + [columns(x) for x in weights]
        + [fixed(x) for x in extra],
        out_specs=pl.BlockSpec((rows, tile), lambda t: (0, t)),
        out_shape=jax.ShapeDtypeStruct((rows, width), bf16 if tables else f32),
        compiler_params=kernel_params(),
        cost_estimate=pl.CostEstimate(
            flops=2 * rows * width * sum(x.shape[0] for x in weights),
            bytes_accessed=2 * sum(x.size for x in parts + weights),
            transcendentals=0,
        ),
    )(*parts, *weights, *extra)


def turn_kv_back(first, second, tables):
    rows, width = first.shape

    def kernel(first_ref, second_ref, cos_ref, sin_ref, out_ref):
        for at in range(0, width, HEAD_SIZE):
            columns = slice(at, at + HEAD_SIZE)
            part = first_ref[:, columns].astype(f32) + second_ref[:, columns].astype(f32)
            if at // HEAD_SIZE % 2 == 0:
                part = turned(part, cos_ref[...], -sin_ref[...])
            out_ref[:, columns] = part.astype(bf16)

    return pl.pallas_call(
        kernel,
        out_shape=jax.ShapeDtypeStruct((rows, width), bf16),
        compiler_params=kernel_params(),
    )(first, second, *tables)


def attend(q_pre, kv_all, tables, query_marks, key_marks):
    rows, width = q_pre.shape
    keys = kv_all.shape[0]
    heads = width // HEAD_SIZE
    group = heads // KEY_VALUE_HEADS
    scale = HEAD_SIZE ** (-0.5)

    def kernel(
        q_ref, kv_ref, cos_ref, sin_ref, qd_ref, qp_ref, kd_ref, kp_ref, turned_ref, out_ref, bias
    ):
        @pl.when(pl.program_id(0) == 0)
        def _():
            seen = (qd_ref[...] == kd_ref[...]) & (kp_ref[...] <= qp_ref[...])
            bias[...] = jnp.where(seen, 0.0, masked_score)

        query = turned(q_ref[...], cos_ref[...], sin_ref[...]).astype(bf16)
        turned_ref[...] = query
        scores = mm_nt(query, kv_ref[:, :HEAD_SIZE]) * scale + bias[...]
        weight = jnp.exp(scores - jnp.max(scores, axis=1, keepdims=True))
        total = jnp.sum(weight, axis=1, keepdims=True)
        probs = (weight * (1.0 / total)).astype(bf16)
        out_ref[...] = mm(probs, kv_ref[:, HEAD_SIZE:]).astype(bf16)

    fixed = lambda shape: pl.BlockSpec(shape, lambda h: (0, 0))
    by_head = pl.BlockSpec((rows, HEAD_SIZE), lambda h: (0, h))
    return pl.pallas_call(
        kernel,
        grid=(heads,),
        in_specs=[
            by_head,
            pl.BlockSpec((keys, 2 * HEAD_SIZE), lambda h: (0, h // group)),
            fixed((rows, HEAD_SIZE)),
            fixed((rows, HEAD_SIZE)),
            fixed((rows, 1)),
            fixed((rows, 1)),
            fixed((1, keys)),
            fixed((1, keys)),
        ],
        out_specs=[by_head, by_head],
        out_shape=[jax.ShapeDtypeStruct((rows, width), bf16)] * 2,
        scratch_shapes=[pltpu.VMEM((rows, keys), f32)],
        compiler_params=kernel_params(),
        cost_estimate=pl.CostEstimate(
            flops=8 * rows * keys * width,
            bytes_accessed=8 * rows * width,
            transcendentals=rows * keys * heads,
        ),
    )(
        q_pre,
        kv_all,
        *tables,
        *query_marks,
        *key_marks,
    )


def attend_back(query, kv_all, d_mixed, tables, query_marks, key_marks):
    rows, width = query.shape
    keys = kv_all.shape[0]
    heads = width // HEAD_SIZE
    group = heads // KEY_VALUE_HEADS
    scale = HEAD_SIZE ** (-0.5)

    def kernel(
        q_ref, kv_ref, dm_ref, cos_ref, sin_ref, qd_ref, qp_ref, kd_ref, kp_ref, dq_ref, dkv_ref,
        bias, dkv,
    ):
        head = pl.program_id(0)

        @pl.when(head == 0)
        def _():
            seen = (qd_ref[...] == kd_ref[...]) & (kp_ref[...] <= qp_ref[...])
            bias[...] = jnp.where(seen, 0.0, masked_score)

        query, key, value = q_ref[...], kv_ref[:, :HEAD_SIZE], kv_ref[:, HEAD_SIZE:]
        d_out = dm_ref[...]
        scores = mm_nt(key, query) * scale + bias[...]
        weight = jnp.exp(scores - jnp.max(scores, axis=0, keepdims=True))
        probs = weight * (1.0 / jnp.sum(weight, axis=0, keepdims=True))
        d_probs = mm_nt(value, d_out)
        mean = jnp.sum(probs * d_probs, axis=0, keepdims=True)
        d_scores = (probs * (d_probs - mean)).astype(bf16)
        d_value = mm(probs.astype(bf16), d_out)
        d_key = mm(d_scores, query) * scale
        d_query = mm_tn(d_scores, key) * scale
        dq_ref[...] = turned(d_query, cos_ref[...], -sin_ref[...]).astype(bf16)

        @pl.when(head % group == 0)
        def _():
            dkv[:, :HEAD_SIZE] = d_key
            dkv[:, HEAD_SIZE:] = d_value

        @pl.when(head % group != 0)
        def _():
            dkv[:, :HEAD_SIZE] += d_key
            dkv[:, HEAD_SIZE:] += d_value

        @pl.when(head % group == group - 1)
        def _():
            dkv_ref[...] = dkv[...].astype(bf16)

    fixed = lambda shape: pl.BlockSpec(shape, lambda h: (0, 0))
    by_head = pl.BlockSpec((rows, HEAD_SIZE), lambda h: (0, h))
    by_group = pl.BlockSpec((keys, 2 * HEAD_SIZE), lambda h: (0, h // group))
    return pl.pallas_call(
        kernel,
        grid=(heads,),
        in_specs=[
            by_head,
            by_group,
            by_head,
            fixed((rows, HEAD_SIZE)),
            fixed((rows, HEAD_SIZE)),
            fixed((1, rows)),
            fixed((1, rows)),
            fixed((keys, 1)),
            fixed((keys, 1)),
        ],
        out_specs=[by_head, by_group],
        out_shape=[
            jax.ShapeDtypeStruct((rows, width), bf16),
            jax.ShapeDtypeStruct(kv_all.shape, bf16),
        ],
        scratch_shapes=[pltpu.VMEM((keys, rows), f32), pltpu.VMEM((keys, 2 * HEAD_SIZE), f32)],
        compiler_params=kernel_params(),
        cost_estimate=pl.CostEstimate(
            flops=20 * rows * keys * width,
            bytes_accessed=8 * rows * width,
            transcendentals=rows * keys * heads,
        ),
    )(
        query,
        kv_all,
        d_mixed,
        *tables,
        query_marks[0][None, :],
        query_marks[1][None, :],
        key_marks[0][:, None],
        key_marks[1][:, None],
    )


gelu_scale = (2.0 / math.pi) ** 0.5
gelu_cube = 0.044715


def weight_block(weight, layer):
    return pl.BlockSpec((None, None) + weight.shape[2:], lambda t: (layer, 0, 0, 0))


def expert_forward(layer, part, arrived, router, chosen, own, weights, into=None):
    rows, width = arrived.shape
    hidden = weights[0].shape[3]
    tile = rows // 4
    kept = () if into is None else tuple(into)

    def kernel(
        x_ref, router_ref, chosen_ref, own_ref, wg_ref, wu_ref, wd_ref, *others
    ):
        out_ref, pre_ref, up_ref, gated_ref, gate_ref = others[len(kept) :]
        x = x_ref[...]
        logits = mm_nt(x, router_ref[...])
        among = chosen_ref[...] > 0.5
        weight = jnp.exp(
            jnp.where(among, logits, masked_score)
            - jnp.max(jnp.where(among, logits, masked_score), axis=1, keepdims=True)
        )
        weight = jnp.where(among, weight, 0.0)
        total = jnp.sum(weight, axis=1, keepdims=True)
        gate = jnp.sum(weight * own_ref[...], axis=1, keepdims=True)
        gate = gate / jnp.where(total > 0.0, total, 1.0)
        gate_ref[...] = gate
        for at in range(0, hidden, 256):
            part = slice(at, at + 256)
            gate_pre = mm(x, wg_ref[:, part])
            up_pre = mm(x, wu_ref[:, part])
            turn = jnp.tanh(gelu_scale * gate_pre * (1.0 + gelu_cube * gate_pre * gate_pre))
            active = 0.5 * gate_pre * (1.0 + turn) * up_pre
            gated_ref[:, part] = (gate * active).astype(bf16)
            pre_ref[:, part] = gate_pre
            up_ref[:, part] = up_pre
        out_ref[...] = mm(gated_ref[...], wd_ref[...]).astype(bf16)

    by_row = lambda columns: pl.BlockSpec((tile, columns), lambda t: (2 * part + t, 0))
    fixed = lambda x: pl.BlockSpec(x.shape, lambda t: (0, 0))
    produced, *results = pl.pallas_call(
        kernel,
        grid=(2,),
        in_specs=[by_row(width), fixed(router), by_row(chosen.shape[1]), fixed(own)]
        + [weight_block(w, layer) for w in weights]
        + [pl.BlockSpec(memory_space=pl.ANY)] * len(kept),
        out_specs=[pl.BlockSpec((tile, width), lambda t: (t, 0))]
        + [by_row(hidden), by_row(hidden), by_row(hidden), by_row(1)],
        out_shape=[
            jax.ShapeDtypeStruct((rows // 2, width), bf16),
            jax.ShapeDtypeStruct((rows, hidden), f32),
            jax.ShapeDtypeStruct((rows, hidden), f32),
            jax.ShapeDtypeStruct((rows, hidden), bf16),
            jax.ShapeDtypeStruct((rows, 1), f32),
        ],
        input_output_aliases={7 + k: 1 + k for k in range(len(kept))},
        compiler_params=kernel_params(),
        cost_estimate=pl.CostEstimate(
            flops=3 * rows * width * hidden,
            bytes_accessed=2 * rows * width + 6 * rows * hidden + 6 * width * hidden,
            transcendentals=rows * hidden // 2,
        ),
    )(arrived, router, chosen, own, *weights, *kept)
    return produced, results


def expert_backward(layer, part, d_arrived, gate_pre, up_pre, gate, marks, weights, into=None):
    rows, width = d_arrived.shape
    hidden = weights[0].shape[3]
    tile = rows // 4
    kept = () if into is None else (into,)

    def kernel(
        d_ref, pre_ref, up_ref, gate_ref, marks_ref, wg_ref, wu_ref, wd_ref, *others
    ):
        rows_ref, both_ref = others[len(kept) :]
        d_rows, gate = d_ref[...], gate_ref[...]
        d_gate_sum = jnp.zeros((tile, 1), f32)
        for at in range(0, hidden, 256):
            part = slice(at, at + 256)
            du = mm_nt(d_rows, wd_ref[part, :])
            v, up_value = pre_ref[:, part], up_ref[:, part]
            square = v * v
            turn = jnp.tanh(gelu_scale * v * (1.0 + gelu_cube * square))
            half = 0.5 * (1.0 + turn)
            unit = v * half
            slope = half + 0.5 * v * (1.0 - turn * turn) * (
                gelu_scale * (1.0 + 3.0 * gelu_cube * square)
            )
            d_gate_sum += jnp.sum(du * unit * up_value, axis=1, keepdims=True)
            d_active = (gate * du).astype(bf16).astype(f32)
            both_ref[:, part] = (d_active * slope * up_value).astype(bf16)
            both_ref[:, hidden + at : hidden + at + 256] = (d_active * unit).astype(bf16)
        coarse = d_gate_sum.astype(bf16).astype(f32)
        beside = coarse * marks_ref[0:1, :] + (d_gate_sum - coarse) * marks_ref[1:2, :]
        rows_ref[:, width:] = beside.astype(bf16)
        d_pre = mm_nt(both_ref[:, :hidden], wg_ref[...]) + mm_nt(both_ref[:, hidden:], wu_ref[...])
        rows_ref[:, :width] = d_pre.astype(bf16)

    by_row = lambda columns: pl.BlockSpec((tile, columns), lambda t: (2 * part + t, 0))
    return pl.pallas_call(
        kernel,
        grid=(2,),
        in_specs=[by_row(width), by_row(hidden), by_row(hidden), by_row(1)]
        + [pl.BlockSpec(marks.shape, lambda t: (0, 0))]
        + [weight_block(w, layer) for w in weights]
        + [pl.BlockSpec(memory_space=pl.ANY)] * len(kept),
        out_specs=[
            pl.BlockSpec((tile, width + marks.shape[1]), lambda t: (t, 0)),
            by_row(2 * hidden),
        ],
        out_shape=[
            jax.ShapeDtypeStruct((rows // 2, width + marks.shape[1]), bf16),
            jax.ShapeDtypeStruct((rows, 2 * hidden), bf16),
        ],
        input_output_aliases={8 + k: 1 + k for k in range(len(kept))},
        compiler_params=kernel_params(),
        cost_estimate=pl.CostEstimate(
            flops=3 * rows * width * hidden,
            bytes_accessed=2 * rows * width + 6 * rows * hidden + 6 * width * hidden,
            transcendentals=rows * hidden // 2,
        ),
    )(d_arrived, gate_pre, up_pre, gate, marks, *weights, *kept)


def documents(lengths_row, position):
    doc_ends = jnp.cumsum(lengths_row)
    doc_starts = doc_ends - lengths_row
    document_index = jnp.sum((position[:, None] >= doc_ends[None, :]).astype(jnp.int32), axis=1)
    doc_first = jnp.max(
        jnp.where(doc_starts[None, :] <= position[:, None], doc_starts[None, :], 0), axis=1
    )
    return (document_index, position - doc_first)


def slot_table(routes, order_row, experts, capacity):
    token_rows, top_count = routes.shape
    pair_count = token_rows * top_count
    pairs = jnp.arange(pair_count, dtype=jnp.int32)
    named = (order_row[:, None] == pairs[None, :]).astype(bf16)
    of_pair = (
        routes.reshape(pair_count)[:, None] == jnp.arange(experts, dtype=jnp.int32)[None, :]
    ).astype(bf16)
    ranked = mm(named, of_pair)
    earlier = (pairs[None, :] < pairs[:, None]).astype(bf16)
    before = mm(earlier, ranked.astype(bf16))
    code = jnp.where(before < capacity, before + 1.0, -1.0) * ranked
    back = mm_tn(code.astype(bf16), named)
    return jnp.sum(back.reshape(experts, token_rows, top_count), axis=2)


def chosen_softmax(logits, chosen):
    top = jnp.max(jnp.where(chosen, logits, masked_score), axis=-1, keepdims=True)
    weight = jnp.where(chosen, jnp.exp(jnp.where(chosen, logits - top, 0.0)), 0.0)
    total = jnp.sum(weight, axis=-1, keepdims=True)
    return weight / jnp.where(total > 0.0, total, 1.0)


class Lines:
    def __init__(self):
        self.experts = lax.axis_size("expert")
        self.count = self.experts // 2
        self.index = lax.axis_index("expert")
        self.line = self.index // 2
        self.side = self.index % 2

    def source(self, slot):
        count, line = self.count, self.line
        low = jnp.where(line + slot < count, line + slot, count - 1 - slot)
        mirror = count - 1 - line
        high = count - 1 - jnp.where(mirror + slot < count, mirror + slot, count - 1 - slot)
        return jnp.where(line < count // 2, low, high)

    def swap(self, values):
        return lax.ppermute(values, "expert", [(i, i ^ 1) for i in range(self.experts)])

    def even(self, values):
        return lax.ppermute(values, "expert", [(i, i ^ 2) for i in range(self.experts)])

    def odd(self, values):
        count, shards = self.count, lax.axis_size("shard")
        pairs = []
        for i in range(count):
            end = i in (0, count - 1)
            other = i if end else i + 1 if i % 2 else i - 1
            for k in range(2):
                for j in range(shards):
                    to = (2 * other + k) * shards + (j ^ 1 if end else j)
                    pairs.append(((2 * i + k) * shards + j, to))
        return lax.ppermute(values, ("expert", "shard"), pairs)

    def choose(self, table):
        value, seen = None, {}
        for line, array in table.items():
            seen.setdefault(id(array), (array, []))[1].append(line)
        for array, lines in seen.values():
            if value is None:
                value = array
            else:
                here = jnp.any(self.line == jnp.array(lines))
                value = jnp.where(here, array, value)
        return value

    def step_gather(self, held):
        last = len(held) == self.count - 1
        even, odd = held[-1]
        return held + [(self.even(odd), None if last else self.odd(even))]

    def slot(self, held, slot):
        count = self.count
        table = {}
        for line in range(count):
            near = line if line < count // 2 else count - 1 - line
            toward = near + slot < count
            distance = slot if toward else near + slot + 1 - count
            above = toward == (line < count // 2)
            table[line] = held[distance][0 if above == (line % 2 == 0) else 1]
        return self.choose(table)

    def pick(self, blocks, distance, even):
        count, half = self.count, self.count // 2
        table = {}
        for line in range(count):
            up = even == (line % 2 == 0)
            if not 0 <= (line + distance if up else line - distance) < count:
                continue
            if up:
                slot = distance if line < half else line + distance
            else:
                slot = distance if line >= half else count - 1 - line + distance
            table[line] = blocks[slot]
        return self.choose(table) if table else None

    def step_reduce(self, step, blocks, arrived):
        distance = self.count - 1 - step
        even, odd = self.pick(blocks, distance, True), self.pick(blocks, distance, False)
        if arrived is not None:
            from_even, from_odd = self.inward(arrived)
            even = even + from_odd
            odd = odd + from_even
        sent = None if odd is None else self.odd(odd.astype(bf16))
        return self.even(even.astype(bf16)), sent

    def inward(self, arrived):
        even, odd = arrived
        if odd is None:
            return even.astype(f32), 0.0
        end = (self.line == 0) | (self.line == self.count - 1)
        return even.astype(f32), jnp.where(end, 0.0, odd.astype(f32))

    def turn(self, values, steps):
        pairs = [
            (2 * i + k, 2 * ((i + steps) % self.count) + k)
            for i in range(self.count)
            for k in range(2)
        ]
        return lax.ppermute(values, "expert", pairs)


def core_swap(values):
    return lax.ppermute(values, "shard", [(i, i ^ 1) for i in range(lax.axis_size("shard"))])


def row_swap(values):
    return lax.ppermute(values, "shard", [(i, i ^ 2) for i in range(lax.axis_size("shard"))])


def column_units(lines):
    mine = lax.axis_index("shard")
    units = []
    for mask in (0, 1, 2, 3):
        first = lines.side if mask >= 2 else 0
        units += [(mine ^ mask) * 2 + first, (mine ^ mask) * 2 + 1 - first]
    return units


def column_parts(values, units):
    width = values.shape[1] // 8
    rows = values.shape[0]
    parts = [
        lax.dynamic_slice(values, (0, units[at] * width), (rows, 2 * width)) for at in (0, 2)
    ]
    return parts + [
        lax.dynamic_slice(values, (0, units[at] * width), (rows, width)) for at in range(4, 8)
    ]


def ordered_small(blocks):
    mine = lax.axis_index("shard")
    shape = blocks[0].shape
    whole = jnp.zeros(shape[:-1] + (4 * shape[-1],), blocks[0].dtype)
    for mask, block in blocks.items():
        at = (0,) * (len(shape) - 1) + ((mine ^ mask) * shape[-1],)
        whole = lax.dynamic_update_slice(whole, block, at)
    return whole


def split_columns(values):
    mine = lax.axis_index("shard")
    width = values.shape[1] // 4
    return [
        lax.dynamic_slice(values, (0, (mine ^ mask) * width), (values.shape[0], width))
        for mask in range(4)
    ]


def shard_rows_of(values):
    return jnp.concatenate([values, row_swap(values)], axis=0)


def shard_rows_all(pair):
    return jnp.concatenate([pair, core_swap(pair)], axis=0)


def exchange_blocks(blocks):
    pairs = lambda mask: [(i, i ^ mask) for i in range(lax.axis_size("shard"))]
    return [blocks[0]] + [lax.ppermute(blocks[r], "shard", pairs(r)) for r in (2, 1, 3)]


def own_columns(values):
    return jnp.concatenate(exchange_blocks(split_columns(values)), axis=0)


class ShardSummed:
    def __init__(self, columns, right):
        self.columns, self.right = columns, right
        self.width = columns[0].shape[1]
        self.moving = ()

    @property
    def value(self):
        return self.moving, self.columns, self.right

    @value.setter
    def value(self, value):
        self.moving, self.columns, self.right = value

    def product(self, k):
        return mm_tn(self.columns[k], self.right)

    def core(self):
        sent = [self.product(k).astype(bf16) for k in (3, 1)]
        self.moving = core_swap(jnp.concatenate(sent, axis=0))

    def row(self):
        self.came = self.moving
        across = self.product(2) + self.came[: self.width].astype(f32)
        self.moving = row_swap(across.astype(bf16))

    def keep(self):
        self.kept = self.product(0) + self.came[self.width :].astype(f32)

    def total(self):
        return self.kept + self.moving.astype(f32)


class Summed:
    def __init__(self, lines, part):
        self.lines = lines
        self.part = part
        self.value = ()

    def side(self):
        part = self.part
        half = part.shape[0] // 2
        lines = self.lines
        given = lax.dynamic_slice(part, ((1 - lines.side) * half, 0), (half, part.shape[1]))
        self.kept = lax.dynamic_slice(part, (lines.side * half, 0), (half, part.shape[1]))
        self.value = lines.swap(given.astype(bf16))

    def place(self, steps):
        return (self.lines.line + steps) % self.lines.count

    def scatter(self):
        lines = self.lines
        part = (self.kept + self.value.astype(f32)).reshape(lines.count, -1, self.kept.shape[1])
        low = part.astype(bf16)
        take = lambda steps, x: lax.dynamic_index_in_dim(x, self.place(steps), 0, keepdims=False)
        self.kept = take(0, part)
        self.value = tuple(
            lines.turn(take(steps, low), steps) for steps in range(1, lines.count)
        )

    def spread(self):
        own = self.kept
        for came in self.value:
            own = own + came.astype(f32)
        self.kept = own.astype(bf16)
        self.value = tuple(
            self.lines.turn(self.kept, -steps) for steps in range(1, self.lines.count)
        )

    def assembled(self):
        blocks = jnp.zeros((self.lines.count,) + self.kept.shape, bf16)
        for steps, block in enumerate((self.kept,) + self.value):
            blocks = lax.dynamic_update_slice(blocks, block[None], (self.place(steps), 0, 0))
        return blocks.reshape(-1, self.kept.shape[1])


def merged(sums):
    one = Summed(sums[0].lines, None)
    one.kept = jnp.concatenate([s.kept for s in sums], axis=1)
    one.value = jnp.concatenate([s.value for s in sums], axis=1)
    return one


class Joined:
    def __init__(self, lines, kept):
        self.lines, self.kept = lines, kept
        self.value = lines.swap(kept)

    def whole(self, take):
        low = self.lines.side == 0
        kept, value = take(self.kept), take(self.value)
        pair = (jnp.where(low, kept, value), jnp.where(low, value, kept))
        return jnp.concatenate(pair, axis=0).astype(f32)

    def put(self, whole, layer, take=lambda x: x):
        half = self.kept.shape[0]
        for rows, side in ((self.kept, self.lines.side), (self.value, 1 - self.lines.side)):
            block = take(rows).astype(f32)[None]
            whole = lax.dynamic_update_slice(whole, block, (layer, side * half, 0))
        return whole


class Sent:
    def __init__(self, routing, values):
        self.routing = routing
        self.held = [(values, values)]
        rows = 2 * routing.lines.count * routing.capacity
        self.buffer = jnp.zeros((rows, values.shape[1]), values.dtype)
        self.fars, self.ready = {}, {}

    @property
    def value(self):
        return self.held[-1], self.buffer, self.fars, self.ready

    @value.setter
    def value(self, value):
        self.held[-1], self.buffer, self.fars, self.ready = value

    def step(self):
        self.held = self.routing.lines.step_gather(self.held)

    def put(self, rows, block):
        at = block * self.routing.capacity
        self.buffer = lax.dynamic_update_slice(self.buffer, rows, (at, 0))

    def prepare(self, j):
        block = self.routing.lines.slot(self.held, j)
        self.ready[j] = mm(self.routing.mate_hot[j], block).astype(bf16)

    def send(self, j):
        if j not in self.ready:
            self.prepare(j)
        self.fars[j] = self.routing.lines.swap(self.ready.pop(j))

    def place(self, j):
        block = self.routing.lines.slot(self.held, j)
        self.put(mm(self.routing.own_hot[j], block).astype(bf16), j)

    def take(self, j):
        self.put(self.fars.pop(j), self.routing.lines.count + j)

    def round(self, j):
        if j < self.routing.lines.count - 1:
            self.step()
        self.send(j)
        if j > 0:
            self.take(j - 1)
        self.place(j)

    def total(self):
        for j in list(self.fars):
            self.take(j)
        return self.buffer


class Returned:
    def __init__(self, routing, far):
        self.routing = routing
        count = routing.lines.count
        self.blocks = [None] * count + self.cut(far)
        self.parts = [None] * count
        self.steps = 0
        self.came, self.arrived = {}, None

    @property
    def value(self):
        return self.came, self.arrived, self.blocks

    @value.setter
    def value(self, value):
        self.came, self.arrived, self.blocks = value

    def cut(self, rows):
        capacity = self.routing.capacity
        return [rows[at : at + capacity] for at in range(0, rows.shape[0], capacity)]

    def near(self, rows):
        self.blocks = self.cut(rows) + self.blocks[self.routing.lines.count :]

    def swap(self, j):
        lines = self.routing.lines
        self.came[j] = lines.swap(self.blocks[lines.count + j])

    def spread(self, j):
        own, far = self.routing.own_hot[j], self.routing.mate_hot[j]
        self.parts[j] = mm_tn(own, self.blocks[j]) + mm_tn(far, self.came.pop(j))

    def step(self):
        lines = self.routing.lines
        self.spread(lines.count - 1 - self.steps)
        self.arrived = lines.step_reduce(self.steps, self.parts, self.arrived)
        self.steps += 1

    def advance(self, stage):
        self.step()
        self.swap(self.routing.lines.count - 1 - stage)

    def total(self):
        self.spread(0)
        from_even, from_odd = self.routing.lines.inward(self.arrived)
        return self.parts[0] + from_even + from_odd


def settle(moving, *values):
    arrived, values = sync([m.value for m in moving], values)
    for m, value in zip(moving, arrived, strict=True):
        m.value = value
    return values


class Routing:
    pass


def per_device(
    tokens,
    lengths,
    routes,
    slot_order,
    cotangent,
    q_weight,
    key_matrix,
    value_matrix,
    out_weight,
    router_weight,
    attn_gain,
    ffn_gain,
    gate_weight,
    up_weight,
    down_weight,
):
    lines = Lines()
    layer_count = q_weight.shape[0]
    shard_count = lax.axis_size("shard")
    mine = lax.axis_index("shard")
    token_rows, model_width = tokens.shape
    pair_count = token_rows * routes.shape[1]
    experts = router_weight.shape[2]
    assert shard_count == 4 and experts == lines.experts and gate_weight.shape[1] == 1
    hidden_units = gate_weight.shape[3]
    capacity = (pair_count * 5 + 4 * experts - 1) // (4 * experts)
    assert capacity < 256
    sequence_length = token_rows * shard_count
    kv_width = KEY_VALUE_HEADS * HEAD_SIZE

    own_rows = jnp.arange(token_rows, dtype=jnp.int32)
    position = mine * token_rows + own_rows
    key_position = jnp.concatenate([(mine ^ mask) * token_rows + own_rows for mask in (0, 2, 1, 3)])
    query_doc, query_position = documents(lengths[0], position)
    key_doc = documents(lengths[0], key_position)[0]
    tables = rotary_tables(query_position)
    query_marks, key_marks = (query_doc, position), (key_doc, key_position)

    def paired(i):
        parts = []
        for at in range(0, kv_width, HEAD_SIZE):
            parts += [key_matrix[i, :, at : at + HEAD_SIZE], value_matrix[i, :, at : at + HEAD_SIZE]]
        return jnp.concatenate(parts, axis=1)

    small = jnp.concatenate(
        [router_weight.transpose(0, 2, 1), attn_gain[:, None, :], ffn_gain[:, None, :]], axis=1
    )
    routing = Routing()
    routing.lines, routing.capacity = lines, capacity
    late = Sent(routing, cotangent)
    units = column_units(lines)

    def side_half(shards, layer):
        half = shards.shape[1] // 2
        return lax.dynamic_slice(
            shards, (layer, lines.side * half, 0), (1, half, shards.shape[2])
        )[0]

    kv_first = paired(0)
    small_across, small_beside = row_swap(small), core_swap(small)
    kv_across, kv_beside = row_swap(side_half(kv_first[None], 0)), core_swap(kv_first)
    query_half = side_half(q_weight, 0)
    small_across, small_beside, kv_across, kv_beside, query_half, q_gated = sync(
        small_across, small_beside, kv_across, kv_beside, query_half, q_weight
    )
    slot_code = jnp.arange(1, capacity + 1, dtype=jnp.int32).astype(f32)[:, None]
    query_rows = tuple(mark[:, None] for mark in query_marks)
    key_rows = tuple(mark[None, :] for mark in key_marks)

    query_across = row_swap(query_half)
    query_own = q_gated[0]
    query_beside = core_swap(query_own)
    kv_crossed = lines.swap(kv_across)
    kv_across_beside = core_swap(kv_across)
    late.step()
    own_table = slot_table(routes, slot_order[0], experts, capacity)
    small_diagonal = core_swap(small_across)
    small = ordered_small({0: small, 1: small_beside, 2: small_across, 3: small_diagonal})
    routers = [small[i, :experts] for i in range(layer_count)]
    attn_gains = [small[i, experts].astype(f32)[None, :] for i in range(layer_count)]
    ffn_gains = [small[i, experts + 1].astype(f32)[None, :] for i in range(layer_count)]
    stream = tokens.astype(f32)
    normed, attn_inverse = norm_forward(stream, attn_gains[0])
    hidden = normed.astype(bf16)
    matched = column_parts(hidden, units)
    query_across, query_beside, kv_crossed, kv_across_beside, matched, own_table, later = settle(
        [late], query_across, query_beside, kv_crossed, kv_across_beside, matched, own_table,
        (out_weight, key_matrix, value_matrix),
    )
    every = lambda part: lax.all_gather(part, "shard", axis=0, tiled=True)
    gathered = [(None, None, every(later[0][0]))]
    tables, query_rows, key_rows, slot_code = sync(tables, query_rows, key_rows, slot_code)

    query_crossed = lines.swap(query_across)
    query_across_beside = core_swap(query_across)
    kv_pieces = [kv_first, kv_beside, kv_across, kv_crossed, kv_across_beside]
    kv_pieces.append(core_swap(kv_crossed))
    first_pair = shard_rows_of(project(matched, kv_pieces, tables))
    held_tables = [(own_table, own_table)]
    for _ in range(lines.count - 1):
        held_tables = lines.step_gather(held_tables)
    query_crossed, query_across_beside, first_pair, q_gated, later = settle(
        [late], query_crossed, query_across_beside, first_pair, q_gated, later
    )
    near_tables = jnp.stack([lines.slot(held_tables, j) for j in range(lines.count)], axis=0)
    query_pieces = [query_own, query_beside, query_across, query_crossed, query_across_beside]
    query_pieces.append(core_swap(query_crossed))

    def prepare_routing(near_tables, own_table):
        far_tables = lines.swap(near_tables)

        def hot_rows(codes, expert):
            code = lax.dynamic_index_in_dim(codes, expert, 1, keepdims=True)
            return (code == slot_code).astype(bf16)

        routing.own_hot = hot_rows(near_tables, lines.index)
        routing.mate_hot = hot_rows(near_tables, lines.index ^ 1)
        all_hot = jnp.concatenate([routing.own_hot, hot_rows(far_tables, lines.index)], axis=0)
        all_tables = jnp.concatenate([near_tables, far_tables], axis=0)
        row_chosen = jnp.einsum(
            "sct,set->sce", all_hot, (all_tables != 0.0).astype(bf16), preferred_element_type=f32
        ).reshape(2 * lines.count * capacity, experts)
        return own_table.T != 0.0, row_chosen

    own_expert = (jnp.arange(experts) == lines.index).astype(f32)[None, :]
    assert experts <= 64
    gate_marks = jnp.arange(128)[None, :] == lines.index + 64 * jnp.arange(2)[:, None]
    gate_marks = gate_marks.astype(f32)

    weights = (gate_weight, up_weight, down_weight)

    def small_sum(part):
        own = sum(exchange_blocks(split_columns(part)))
        return jnp.pad(own, ((0, -own.shape[0] % 128), (0, 0))).T

    last = layer_count - 1
    stored = []
    for i in range(layer_count):
        w_query, w_kv, w_out = gathered[i]
        if i == 0:
            late.step()
            kv_pair = first_pair
            q_pre = project(matched, query_pieces)
        else:
            if i == last:
                late.send(2)
            normed, attn_inverse = norm_forward(stream, attn_gains[i])
            hidden = normed.astype(bf16)
            kv_pair = shard_rows_of(project([hidden], [w_kv], tables))
            q_pre = mm(hidden, w_query)
            kv_pair, q_pre = settle([late], kv_pair, q_pre)
            if i == last:
                late.send(3)
                for k in range(4, lines.count):
                    late.step()
                    late.send(k)
        kv_all = shard_rows_all(kv_pair)
        query, mixed = attend(q_pre, kv_all, tables, query_rows, key_rows)
        stream_mid = stream + mm(mixed, w_out)
        normed_ffn, ffn_inverse = norm_forward(stream_mid, ffn_gains[i])
        routed = normed_ffn.astype(bf16)
        if i == last:
            (routed, gathered[0]) = settle([late], routed, gathered[0])
        else:
            routed, q_gated, later, near_tables = settle(
                [late], routed, q_gated, later, near_tables
            )
            chosen_here, row_chosen = prepare_routing(near_tables, own_table)
        if i == 0:

            def paired_of(k):
                parts = []
                for at in range(0, kv_width, HEAD_SIZE):
                    parts += [later[m][k, :, at : at + HEAD_SIZE] for m in (1, 2)]
                return jnp.concatenate(parts, axis=1)

            for k in range(1, layer_count):
                gathered.append((every(q_gated[k]), every(paired_of(k)), every(later[0][k])))
            gathered[0] = (every(q_gated[0]), every(paired_of(0)), w_out)
        gates = chosen_softmax(mm_nt(routed, routers[i]), chosen_here)
        sent = Sent(routing, routed)
        for j in range(lines.count):
            sent.round(j)
            if i == 0 and j < 2:
                late.prepare(j)
            if i == last:
                late.place(j)
                late.take(j)
            hidden, mixed = settle([sent, late], hidden, mixed)
        columns = [own_columns(hidden), own_columns(mixed)]
        arrived = sent.total()
        if i == 0:
            (arrived,) = settle([late], arrived)
        shared = (arrived, routers[i], row_chosen, own_expert, weights)
        produced, kept = expert_forward(i, 1, *shared)
        if i == 0:
            late.step()
            late.send(0)
        produced, kept = sync(produced, kept)
        back = Returned(routing, produced)
        back.swap(lines.count - 1)
        produced, kept = expert_forward(i, 0, *shared, into=kept)
        if i == 0:
            late.send(1)
        produced, kept = settle([late, back], produced, kept)
        back.near(produced)
        stored.append(
            dict(
                stream=stream,
                attn_inverse=attn_inverse,
                hidden_columns=columns[0],
                query=query,
                kv_all=kv_all,
                mixed_columns=columns[1],
                stream_mid=stream_mid,
                ffn_inverse=ffn_inverse,
                routed=routed,
                gates=gates,
                arrived=arrived,
                kept=kept,
            )
        )
        if i < last:
            for j in range(1, lines.count):
                back.advance(j)
                if i == last - 1 and j in (1, 2):
                    late.prepare(j + 1)
                settle([back, late])
            stream = stream_mid + back.total()

    own_width = model_width // shard_count
    results = dict(
        query=jnp.full((layer_count, own_width, model_width), 0.0, f32),
        out=jnp.full((layer_count, own_width, model_width), 1.0, f32),
        key=jnp.full((layer_count, own_width, kv_width), 0.0, f32),
        value=jnp.full((layer_count, own_width, kv_width), 1.0, f32),
        gate=jnp.full((layer_count, own_width, hidden_units), 0.0, f32),
        up=jnp.full((layer_count, own_width, hidden_units), 1.0, f32),
        down=jnp.full((layer_count, hidden_units // shard_count, model_width), 0.0, f32),
    )

    small_results = [None] * layer_count

    def put_experts(layer, both, down):
        for name, block in (
            ("gate", both[:, :hidden_units]),
            ("up", both[:, hidden_units:]),
            ("down", down),
        ):
            results[name] = lax.dynamic_update_slice(
                results[name], block.astype(f32)[None], (layer, 0, 0)
            )

    def put_kv(layer, joined, take):
        heads = lambda first: lambda x: jnp.concatenate(
            [take(x)[:, at : at + HEAD_SIZE] for at in range(first, 2 * kv_width, 2 * HEAD_SIZE)],
            axis=1,
        )
        results["key"] = joined.put(results["key"], layer, heads(0))
        results["value"] = joined.put(results["value"], layer, heads(HEAD_SIZE))
        rest = lambda x: take(x)[:, 2 * kv_width :]
        small_results[layer] = joined.whole(rest)

    output_back = back
    top = lines.count - 1
    d_arrived = late.total()
    upstream = cotangent.astype(f32)
    for i in reversed(range(layer_count)):
        w_query, w_kv, w_out = gathered[i]
        saved = stored[i]
        if i < last:
            sent = Sent(routing, upstream.astype(bf16))
            columns = stored[i + 1]["hidden_columns"]
            out_above, d_query, d_kv_low, small_grad = waiting
            small_part = small_grad
            for j in range(lines.count):
                sent.round(j)
                moving = []
                if j == 0:
                    d_kv_low = shard_rows_of(d_kv_low)
                if j == 1:
                    d_query = shard_rows_all(d_query)
                    d_kv_low = shard_rows_all(d_kv_low)
                    small_part = small_sum(small_grad)
                if j == 2:
                    query_above = Summed(lines, mm_tn(columns, d_query))
                    query_above.side()
                if j == 3:
                    kv_above = mm_tn(columns, d_kv_low)
                    kv_above = Summed(lines, jnp.concatenate([kv_above, small_part], axis=1))
                    kv_above.side()
                    moving = [query_above, kv_above]
                d_query, d_kv_low, small_part = settle(
                    [sent] + moving, d_query, d_kv_low, small_part
                )
                if j == 1:
                    results, d_query = sync(results, d_query)
                if j == lines.count - 1:
                    d_query, both_grad, down_grad = sync(d_query, both_grad, down_grad)
            put_experts(last, both_grad, down_grad)
            d_arrived = sent.total()
            above = merged([out_above, kv_above, query_above])
            above.scatter()
        gate_pre, up_pre, gated, own_gate = saved["kept"]
        shared = (d_arrived, gate_pre, up_pre, own_gate, gate_marks, weights)
        if i == last:
            output_back.step()
        d_rows, d_both = expert_backward(i, 1, *shared)
        d_rows, d_both = sync(d_rows, d_both)
        back = Returned(routing, d_rows)
        back.swap(top)
        d_rows, d_both = expert_backward(i, 0, *shared, into=d_both)
        moving = [back, output_back if i == last else above]
        d_rows, d_both = settle(moving, d_rows, d_both)
        back.near(d_rows)
        both = ShardSummed(split_columns(saved["arrived"]), d_both)
        down = ShardSummed(split_columns(gated), d_arrived)
        for j in range(1, lines.count):
            back.advance(j)
            moving = [back, both, down]
            if j == 1:
                both.core()
            if j == 2:
                both.row()
                down.core()
                if i == last:
                    for k in reversed(range(2, top)):
                        output_back.swap(k)
                    moving.append(output_back)
            if j == 3:
                both.keep()
                down.row()
                moving = [back, both] + ([output_back] if i == last else [])
            settle(moving)
        down.keep()
        returned = back.total()
        d_gates = returned[:, model_width : model_width + experts]
        d_gates = d_gates + returned[:, model_width + 64 : model_width + 64 + experts]
        gates = saved["gates"]
        d_logits = gates * (d_gates - jnp.sum(gates * d_gates, axis=1, keepdims=True))
        d_logits = d_logits.astype(bf16)
        router_grad = mm_tn(d_logits, saved["routed"])
        d_routed = returned[:, :model_width] + mm(d_logits, routers[i])
        d_stream, ffn_gain_grad = norm_backward(
            saved["stream_mid"], saved["ffn_inverse"], ffn_gains[i], d_routed
        )
        upstream = upstream + d_stream
        d_branch = upstream.astype(bf16)
        d_mixed = mm_nt(d_branch, w_out).astype(bf16)
        if i == last:
            while output_back.steps < top - 1:
                output_back.step()
            output_back.swap(1)
            output_back.swap(0)
            moving = [output_back]
        else:
            above.spread()
            moving = []
        d_branch_crossed = row_swap(d_branch)
        d_query, d_kv = attend_back(
            saved["query"], saved["kv_all"], d_mixed, tables, query_marks, key_marks
        )
        d_query, d_kv, d_branch_crossed = settle(
            moving + [down], d_query, d_kv, d_branch_crossed
        )
        d_branch_pair = jnp.concatenate([d_branch, d_branch_crossed], axis=0)
        both_grad, down_grad = both.total(), down.total()
        pair_rows = 2 * token_rows
        d_kv_pair = d_kv[:pair_rows].astype(f32) + core_swap(d_kv[pair_rows:]).astype(f32)
        d_branch_all = shard_rows_all(d_branch_pair)
        d_kv_pair, d_branch_all, d_query = sync(d_kv_pair, d_branch_all, d_query)
        d_kv_crossed = row_swap(d_kv_pair[token_rows:].astype(bf16))
        d_hidden = mm_nt(d_query, w_query)
        out_part = mm_tn(saved["mixed_columns"], d_branch_all)
        d_kv_crossed, d_query, d_hidden, out_part = sync(
            d_kv_crossed, d_query, d_hidden, out_part
        )
        out_sum = Summed(lines, out_part)
        out_sum.side()
        moving = [out_sum]
        if i == last:
            output_back.step()
            moving.append(output_back)
        else:
            moving.append(above)
        d_query_pair = shard_rows_of(d_query)
        d_kv_low = turn_kv_back(d_kv_pair[:token_rows], d_kv_crossed, tables)
        d_hidden = d_hidden + mm_nt(d_kv_low, w_kv)
        d_stream, attn_gain_grad = norm_backward(
            saved["stream"], saved["attn_inverse"], attn_gains[i], d_hidden
        )
        upstream = upstream + d_stream
        small_grad = jnp.concatenate(
            [router_grad, attn_gain_grad[None, :], ffn_gain_grad[None, :]], axis=0
        )
        upstream, d_kv_low, small_grad = settle(moving, upstream, d_kv_low, small_grad)
        if i == last:
            output = (saved["stream_mid"] + output_back.total()).astype(bf16)
            out_above = out_sum
            waiting = (out_above, d_query_pair, d_kv_low, small_grad)

    hidden_columns = stored[0]["hidden_columns"]
    out_sum.scatter()
    d_kv_pair = shard_rows_of(d_kv_low)
    small_part = small_sum(small_grad)
    q_sum = Summed(lines, mm_tn(hidden_columns, shard_rows_all(d_query_pair)))
    q_sum.side()
    d_kv_pair, small_part = settle([q_sum, out_sum], d_kv_pair, small_part)
    q_sum.scatter()
    kv_part = mm_tn(hidden_columns, shard_rows_all(d_kv_pair))
    kv_sum = Summed(lines, jnp.concatenate([kv_part, small_part], axis=1))
    kv_sum.side()
    half_result = above.assembled()
    split = half_result.shape[1] - model_width
    above_first = Joined(lines, half_result[:, :split])
    out_sum.spread()
    above_second_rows = half_result[:, split:]
    (above_second_rows,) = settle([q_sum, kv_sum, out_sum], above_second_rows)
    q_sum.spread()
    kv_sum.scatter()
    out_join = Joined(lines, out_sum.assembled())
    above_second = Joined(lines, above_second_rows)
    put_experts(0, both_grad, down_grad)
    (results,) = settle([q_sum, kv_sum, out_join, above_first], results)
    q_join = Joined(lines, q_sum.assembled())
    kv_sum.spread()
    results["out"] = above_first.put(results["out"], last, lambda x: x[:, :model_width])
    put_kv(last, above_first, lambda x: x[:, model_width:])
    results["out"] = out_join.put(results["out"], 0)
    (results,) = settle([q_join, kv_sum, above_second], results)
    kv_join = Joined(lines, kv_sum.assembled())
    results["query"] = above_second.put(results["query"], last)
    results["query"] = q_join.put(results["query"], 0)
    put_kv(0, kv_join, lambda x: x)
    small_result = jnp.stack(small_results, axis=0)
    return (
        output,
        upstream.astype(bf16),
        results["query"],
        results["key"],
        results["value"],
        results["out"],
        small_result[:, :, :experts],
        small_result[:, :, experts],
        small_result[:, :, experts + 1],
        results["gate"][:, None],
        results["up"][:, None],
        results["down"][:, None],
    )


def solution(mesh):
    tokens_spec = P(("expert", "shard"), None)
    shard_spec = P(None, "shard", None)
    expert_spec = P(None, "expert", None, None)
    expert_grad_spec = P(None, "expert", "shard", None)
    return jax.shard_map(
        per_device,
        mesh=mesh,
        in_specs=(
            tokens_spec,
            P("expert", None),
            tokens_spec,
            tokens_spec,
            tokens_spec,
            shard_spec,
            shard_spec,
            shard_spec,
            shard_spec,
            shard_spec,
            P(None, "shard"),
            P(None, "shard"),
            expert_spec,
            expert_spec,
            expert_spec,
        ),
        out_specs=(
            tokens_spec,
            tokens_spec,
            shard_spec,
            shard_spec,
            shard_spec,
            shard_spec,
            shard_spec,
            P(None, "shard"),
            P(None, "shard"),
            expert_grad_spec,
            expert_grad_spec,
            expert_grad_spec,
        ),
        check_vma=False,
    )
```

```python
import math

import jax
import jax.numpy as jnp
from jax import lax
from jax.experimental import pallas as pl
from jax.experimental.pallas import tpu as pltpu
from jax.sharding import PartitionSpec as P

QUERY_HEADS = 12
KEY_VALUE_HEADS = 2
HEAD_SIZE = 128

norm_eps = 1e-06
rope_base = 10000.0
masked_score = -1e30

bf16 = jnp.bfloat16
f32 = jnp.float32


def mm(left, right):
    return jnp.dot(left, right, preferred_element_type=f32)


def mm_tn(left, right):
    return lax.dot_general(left, right, (((0,), (0,)), ((), ())), preferred_element_type=f32)


def mm_nt(left, right):
    return lax.dot_general(left, right, (((1,), (1,)), ((), ())), preferred_element_type=f32)


def norm_forward(values, gain):
    inverse = lax.rsqrt(jnp.mean(values * values, axis=-1, keepdims=True) + norm_eps)
    return values * inverse * gain, inverse


def norm_backward(values, inverse, gain, grad):
    scaled = grad * gain
    mean_part = jnp.mean(values * scaled, axis=-1, keepdims=True)
    d_values = inverse * scaled - values * (inverse * inverse * inverse * mean_part)
    d_gain = jnp.sum(grad * values * inverse, axis=0)
    return d_values, d_gain


def sync(*values):
    return lax.optimization_barrier(values)


def rotary_tables(position):
    half_width = HEAD_SIZE // 2
    frequency = rope_base ** (-(jnp.arange(half_width).astype(f32) * 2.0 / HEAD_SIZE))
    angles = position.astype(f32)[:, None] * frequency[None, :]
    cosine, sine = jnp.cos(angles), jnp.sin(angles)
    return jnp.concatenate([cosine, cosine], axis=1), jnp.concatenate([-sine, sine], axis=1)


def turned(values, cosine, sine):
    return values * cosine + pltpu.roll(values, HEAD_SIZE // 2, 1) * sine


def kernel_params():
    return pltpu.CompilerParams(vmem_limit_bytes=40 * 1024 * 1024)


def project(parts, weights, tables=None):
    rows, width = parts[0].shape[0], weights[0].shape[1]
    tile = width if tables else width // 3
    count = len(parts)

    def kernel(*refs):
        out_ref = refs[-1]
        value = mm(refs[0][...], refs[count][...])
        for k in range(1, count):
            value = value + mm(refs[k][...], refs[count + k][...])
        if tables is None:
            out_ref[...] = value
            return
        for at in range(0, width, HEAD_SIZE):
            part = value[:, at : at + HEAD_SIZE]
            if at // HEAD_SIZE % 2 == 0:
                part = turned(part, refs[2 * count][...], refs[2 * count + 1][...])
            out_ref[:, at : at + HEAD_SIZE] = part.astype(bf16)

    fixed = lambda x: pl.BlockSpec(x.shape, lambda t: (0, 0))
    columns = lambda x: pl.BlockSpec((x.shape[0], tile), lambda t: (0, t))
    extra = list(tables) if tables else []
    return pl.pallas_call(
        kernel,
        grid=(width // tile,),
        in_specs=[fixed(x) for x in parts]
        + [columns(x) for x in weights]
        + [fixed(x) for x in extra],
        out_specs=pl.BlockSpec((rows, tile), lambda t: (0, t)),
        out_shape=jax.ShapeDtypeStruct((rows, width), bf16 if tables else f32),
        compiler_params=kernel_params(),
        cost_estimate=pl.CostEstimate(
            flops=2 * rows * width * sum(x.shape[0] for x in weights),
            bytes_accessed=2 * sum(x.size for x in parts + weights),
            transcendentals=0,
        ),
    )(*parts, *weights, *extra)


def turn_kv_back(first, second, tables):
    rows, width = first.shape

    def kernel(first_ref, second_ref, cos_ref, sin_ref, out_ref):
        for at in range(0, width, HEAD_SIZE):
            columns = slice(at, at + HEAD_SIZE)
            part = first_ref[:, columns].astype(f32) + second_ref[:, columns].astype(f32)
            if at // HEAD_SIZE % 2 == 0:
                part = turned(part, cos_ref[...], -sin_ref[...])
            out_ref[:, columns] = part.astype(bf16)

    return pl.pallas_call(
        kernel,
        out_shape=jax.ShapeDtypeStruct((rows, width), bf16),
        compiler_params=kernel_params(),
    )(first, second, *tables)


def attend(q_pre, kv_all, tables, query_marks, key_marks):
    rows, width = q_pre.shape
    keys = kv_all.shape[0]
    heads = width // HEAD_SIZE
    group = heads // KEY_VALUE_HEADS
    together = 3 if group % 3 == 0 else 1
    scale = HEAD_SIZE ** (-0.5)

    def kernel(
        q_ref, kv_ref, cos_ref, sin_ref, qd_ref, qp_ref, kd_ref, kp_ref, turned_ref, out_ref, bias
    ):
        @pl.when(pl.program_id(0) == 0)
        def _():
            seen = (qd_ref[...] == kd_ref[...]) & (kp_ref[...] <= qp_ref[...])
            bias[...] = jnp.where(seen, 0.0, masked_score)

        for at in range(0, together * HEAD_SIZE, HEAD_SIZE):
            head = slice(at, at + HEAD_SIZE)
            query = turned(q_ref[:, head], cos_ref[...], sin_ref[...]).astype(bf16)
            turned_ref[:, head] = query
            scores = mm_nt(query, kv_ref[:, :HEAD_SIZE]) * scale + bias[...]
            weight = jnp.exp(scores - jnp.max(scores, axis=1, keepdims=True))
            total = jnp.sum(weight, axis=1, keepdims=True)
            probs = (weight * (1.0 / total)).astype(bf16)
            out_ref[:, head] = mm(probs, kv_ref[:, HEAD_SIZE:]).astype(bf16)

    fixed = lambda shape: pl.BlockSpec(shape, lambda h: (0, 0))
    by_head = pl.BlockSpec((rows, together * HEAD_SIZE), lambda h: (0, h))
    return pl.pallas_call(
        kernel,
        grid=(heads // together,),
        in_specs=[
            by_head,
            pl.BlockSpec((keys, 2 * HEAD_SIZE), lambda h: (0, h * together // group)),
            fixed((rows, HEAD_SIZE)),
            fixed((rows, HEAD_SIZE)),
            fixed((rows, 1)),
            fixed((rows, 1)),
            fixed((1, keys)),
            fixed((1, keys)),
        ],
        out_specs=[by_head, by_head],
        out_shape=[jax.ShapeDtypeStruct((rows, width), bf16)] * 2,
        scratch_shapes=[pltpu.VMEM((rows, keys), f32)],
        compiler_params=kernel_params(),
        cost_estimate=pl.CostEstimate(
            flops=8 * rows * keys * width,
            bytes_accessed=8 * rows * width,
            transcendentals=rows * keys * heads,
        ),
    )(
        q_pre,
        kv_all,
        *tables,
        *query_marks,
        *key_marks,
    )


def attend_back(query, kv_all, d_mixed, tables, query_marks, key_marks):
    rows, width = query.shape
    keys = kv_all.shape[0]
    heads = width // HEAD_SIZE
    group = heads // KEY_VALUE_HEADS
    together = 3 if group % 3 == 0 else 1
    steps = group // together
    scale = HEAD_SIZE ** (-0.5)

    def kernel(
        q_ref, kv_ref, dm_ref, cos_ref, sin_ref, qd_ref, qp_ref, kd_ref, kp_ref, dq_ref, dkv_ref,
        bias, dkv,
    ):
        head = pl.program_id(0)

        @pl.when(head == 0)
        def _():
            seen = (qd_ref[...] == kd_ref[...]) & (kp_ref[...] <= qp_ref[...])
            bias[...] = jnp.where(seen, 0.0, masked_score)

        key, value = kv_ref[:, :HEAD_SIZE], kv_ref[:, HEAD_SIZE:]
        d_key = d_value = 0.0
        for at in range(0, together * HEAD_SIZE, HEAD_SIZE):
            own = slice(at, at + HEAD_SIZE)
            query, d_out = q_ref[:, own], dm_ref[:, own]
            scores = mm_nt(key, query) * scale + bias[...]
            weight = jnp.exp(scores - jnp.max(scores, axis=0, keepdims=True))
            probs = weight * (1.0 / jnp.sum(weight, axis=0, keepdims=True))
            d_probs = mm_nt(value, d_out)
            mean = jnp.sum(probs * d_probs, axis=0, keepdims=True)
            d_scores = (probs * (d_probs - mean)).astype(bf16)
            d_value = d_value + mm(probs.astype(bf16), d_out)
            d_key = d_key + mm(d_scores, query) * scale
            d_query = mm_tn(d_scores, key) * scale
            dq_ref[:, own] = turned(d_query, cos_ref[...], -sin_ref[...]).astype(bf16)

        @pl.when(head % steps == 0)
        def _():
            dkv[:, :HEAD_SIZE] = d_key
            dkv[:, HEAD_SIZE:] = d_value

        @pl.when(head % steps != 0)
        def _():
            dkv[:, :HEAD_SIZE] += d_key
            dkv[:, HEAD_SIZE:] += d_value

        @pl.when(head % steps == steps - 1)
        def _():
            dkv_ref[...] = dkv[...].astype(bf16)

    fixed = lambda shape: pl.BlockSpec(shape, lambda h: (0, 0))
    by_head = pl.BlockSpec((rows, together * HEAD_SIZE), lambda h: (0, h))
    by_group = pl.BlockSpec((keys, 2 * HEAD_SIZE), lambda h: (0, h // steps))
    return pl.pallas_call(
        kernel,
        grid=(heads // together,),
        in_specs=[
            by_head,
            by_group,
            by_head,
            fixed((rows, HEAD_SIZE)),
            fixed((rows, HEAD_SIZE)),
            fixed((1, rows)),
            fixed((1, rows)),
            fixed((keys, 1)),
            fixed((keys, 1)),
        ],
        out_specs=[by_head, by_group],
        out_shape=[
            jax.ShapeDtypeStruct((rows, width), bf16),
            jax.ShapeDtypeStruct(kv_all.shape, bf16),
        ],
        scratch_shapes=[pltpu.VMEM((keys, rows), f32), pltpu.VMEM((keys, 2 * HEAD_SIZE), f32)],
        compiler_params=kernel_params(),
        cost_estimate=pl.CostEstimate(
            flops=20 * rows * keys * width,
            bytes_accessed=8 * rows * width,
            transcendentals=rows * keys * heads,
        ),
    )(
        query,
        kv_all,
        d_mixed,
        *tables,
        query_marks[0][None, :],
        query_marks[1][None, :],
        key_marks[0][:, None],
        key_marks[1][:, None],
    )


gelu_scale = (2.0 / math.pi) ** 0.5
gelu_cube = 0.044715


def weight_block(weight, layer):
    return pl.BlockSpec((None, None) + weight.shape[2:], lambda t: (layer, 0, 0, 0))


def expert_forward(layer, part, arrived, router, chosen, own, weights, into=None):
    rows, width = arrived.shape
    hidden = weights[0].shape[3]
    tile = rows // 4
    kept = () if into is None else tuple(into)

    def kernel(
        x_ref, router_ref, chosen_ref, own_ref, wg_ref, wu_ref, wd_ref, *others
    ):
        out_ref, pre_ref, up_ref, gated_ref, gate_ref = others[len(kept) :]
        x = x_ref[...]
        logits = mm_nt(x, router_ref[...])
        among = chosen_ref[...] > 0.5
        weight = jnp.exp(
            jnp.where(among, logits, masked_score)
            - jnp.max(jnp.where(among, logits, masked_score), axis=1, keepdims=True)
        )
        weight = jnp.where(among, weight, 0.0)
        total = jnp.sum(weight, axis=1, keepdims=True)
        gate = jnp.sum(weight * own_ref[...], axis=1, keepdims=True)
        gate = gate / jnp.where(total > 0.0, total, 1.0)
        gate_ref[...] = gate
        for at in range(0, hidden, 256):
            part = slice(at, at + 256)
            gate_pre = mm(x, wg_ref[:, part])
            up_pre = mm(x, wu_ref[:, part])
            turn = jnp.tanh(gelu_scale * gate_pre * (1.0 + gelu_cube * gate_pre * gate_pre))
            active = 0.5 * gate_pre * (1.0 + turn) * up_pre
            gated_ref[:, part] = (gate * active).astype(bf16)
            pre_ref[:, part] = gate_pre.astype(bf16)
            up_ref[:, part] = up_pre.astype(bf16)
        out_ref[...] = mm(gated_ref[...], wd_ref[...]).astype(bf16)

    by_row = lambda columns: pl.BlockSpec((tile, columns), lambda t: (2 * part + t, 0))
    fixed = lambda x: pl.BlockSpec(x.shape, lambda t: (0, 0))
    produced, *results = pl.pallas_call(
        kernel,
        grid=(2,),
        in_specs=[by_row(width), fixed(router), by_row(chosen.shape[1]), fixed(own)]
        + [weight_block(w, layer) for w in weights]
        + [pl.BlockSpec(memory_space=pl.ANY)] * len(kept),
        out_specs=[pl.BlockSpec((tile, width), lambda t: (t, 0))]
        + [by_row(hidden), by_row(hidden), by_row(hidden), by_row(1)],
        out_shape=[
            jax.ShapeDtypeStruct((rows // 2, width), bf16),
            jax.ShapeDtypeStruct((rows, hidden), bf16),
            jax.ShapeDtypeStruct((rows, hidden), bf16),
            jax.ShapeDtypeStruct((rows, hidden), bf16),
            jax.ShapeDtypeStruct((rows, 1), f32),
        ],
        input_output_aliases={7 + k: 1 + k for k in range(len(kept))},
        compiler_params=kernel_params(),
        cost_estimate=pl.CostEstimate(
            flops=3 * rows * width * hidden,
            bytes_accessed=2 * rows * width + 6 * rows * hidden + 6 * width * hidden,
            transcendentals=rows * hidden // 2,
        ),
    )(arrived, router, chosen, own, *weights, *kept)
    return produced, results


def expert_backward(layer, part, d_arrived, gate_pre, up_pre, gate, marks, weights, into=None):
    rows, width = d_arrived.shape
    hidden = weights[0].shape[3]
    tile = rows // 4
    kept = () if into is None else (into,)

    def kernel(
        d_ref, pre_ref, up_ref, gate_ref, marks_ref, wg_ref, wu_ref, wd_ref, *others
    ):
        rows_ref, both_ref = others[len(kept) :]
        d_rows, gate = d_ref[...], gate_ref[...]
        d_gate_sum = jnp.zeros((tile, 1), f32)
        for at in range(0, hidden, 256):
            part = slice(at, at + 256)
            du = mm_nt(d_rows, wd_ref[part, :])
            v, up_value = pre_ref[:, part].astype(f32), up_ref[:, part].astype(f32)
            square = v * v
            turn = jnp.tanh(gelu_scale * v * (1.0 + gelu_cube * square))
            half = 0.5 * (1.0 + turn)
            unit = v * half
            slope = half + 0.5 * v * (1.0 - turn * turn) * (
                gelu_scale * (1.0 + 3.0 * gelu_cube * square)
            )
            d_gate_sum += jnp.sum(du * unit * up_value, axis=1, keepdims=True)
            d_active = (gate * du).astype(bf16).astype(f32)
            both_ref[:, part] = (d_active * slope * up_value).astype(bf16)
            both_ref[:, hidden + at : hidden + at + 256] = (d_active * unit).astype(bf16)
        coarse = d_gate_sum.astype(bf16).astype(f32)
        beside = coarse * marks_ref[0:1, :] + (d_gate_sum - coarse) * marks_ref[1:2, :]
        rows_ref[:, width:] = beside.astype(bf16)
        d_pre = mm_nt(both_ref[:, :hidden], wg_ref[...]) + mm_nt(both_ref[:, hidden:], wu_ref[...])
        rows_ref[:, :width] = d_pre.astype(bf16)

    by_row = lambda columns: pl.BlockSpec((tile, columns), lambda t: (2 * part + t, 0))
    return pl.pallas_call(
        kernel,
        grid=(2,),
        in_specs=[by_row(width), by_row(hidden), by_row(hidden), by_row(1)]
        + [pl.BlockSpec(marks.shape, lambda t: (0, 0))]
        + [weight_block(w, layer) for w in weights]
        + [pl.BlockSpec(memory_space=pl.ANY)] * len(kept),
        out_specs=[
            pl.BlockSpec((tile, width + marks.shape[1]), lambda t: (t, 0)),
            by_row(2 * hidden),
        ],
        out_shape=[
            jax.ShapeDtypeStruct((rows // 2, width + marks.shape[1]), bf16),
            jax.ShapeDtypeStruct((rows, 2 * hidden), bf16),
        ],
        input_output_aliases={8 + k: 1 + k for k in range(len(kept))},
        compiler_params=kernel_params(),
        cost_estimate=pl.CostEstimate(
            flops=3 * rows * width * hidden,
            bytes_accessed=2 * rows * width + 6 * rows * hidden + 6 * width * hidden,
            transcendentals=rows * hidden // 2,
        ),
    )(d_arrived, gate_pre, up_pre, gate, marks, *weights, *kept)


def documents(lengths_row, position):
    doc_ends = jnp.cumsum(lengths_row)
    doc_starts = doc_ends - lengths_row
    document_index = jnp.sum((position[:, None] >= doc_ends[None, :]).astype(jnp.int32), axis=1)
    doc_first = jnp.max(
        jnp.where(doc_starts[None, :] <= position[:, None], doc_starts[None, :], 0), axis=1
    )
    return (document_index, position - doc_first)


def slot_table(routes, order_row, experts, capacity):
    token_rows, top_count = routes.shape
    pair_count = token_rows * top_count
    pairs = jnp.arange(pair_count, dtype=jnp.int32)
    named = (order_row[:, None] == pairs[None, :]).astype(bf16)
    of_pair = (
        routes.reshape(pair_count)[:, None] == jnp.arange(experts, dtype=jnp.int32)[None, :]
    ).astype(bf16)
    ranked = mm(named, of_pair)
    earlier = (pairs[None, :] < pairs[:, None]).astype(bf16)
    before = mm(earlier, ranked.astype(bf16))
    code = jnp.where(before < capacity, before + 1.0, -1.0) * ranked
    back = mm_tn(code.astype(bf16), named)
    return jnp.sum(back.reshape(experts, token_rows, top_count), axis=2)


def chosen_softmax(logits, chosen):
    top = jnp.max(jnp.where(chosen, logits, masked_score), axis=-1, keepdims=True)
    weight = jnp.where(chosen, jnp.exp(jnp.where(chosen, logits - top, 0.0)), 0.0)
    total = jnp.sum(weight, axis=-1, keepdims=True)
    return weight / jnp.where(total > 0.0, total, 1.0)


class Lines:
    def __init__(self):
        self.experts = lax.axis_size("expert")
        self.count = self.experts // 2
        self.index = lax.axis_index("expert")
        self.line = self.index // 2
        self.side = self.index % 2

    def source(self, slot):
        count, line = self.count, self.line
        low = jnp.where(line + slot < count, line + slot, count - 1 - slot)
        mirror = count - 1 - line
        high = count - 1 - jnp.where(mirror + slot < count, mirror + slot, count - 1 - slot)
        return jnp.where(line < count // 2, low, high)

    def swap(self, values):
        return lax.ppermute(values, "expert", [(i, i ^ 1) for i in range(self.experts)])

    def even(self, values):
        return lax.ppermute(values, "expert", [(i, i ^ 2) for i in range(self.experts)])

    def odd(self, values):
        count, shards = self.count, lax.axis_size("shard")
        pairs = []
        for i in range(count):
            end = i in (0, count - 1)
            other = i if end else i + 1 if i % 2 else i - 1
            for k in range(2):
                for j in range(shards):
                    to = (2 * other + k) * shards + (j ^ 1 if end else j)
                    pairs.append(((2 * i + k) * shards + j, to))
        return lax.ppermute(values, ("expert", "shard"), pairs)

    def choose(self, table):
        value, seen = None, {}
        for line, array in table.items():
            seen.setdefault(id(array), (array, []))[1].append(line)
        for array, lines in seen.values():
            if value is None:
                value = array
            else:
                here = jnp.any(self.line == jnp.array(lines))
                value = jnp.where(here, array, value)
        return value

    def step_gather(self, held):
        last = len(held) == self.count - 1
        even, odd = held[-1]
        return held + [(self.even(odd), None if last else self.odd(even))]

    def slot(self, held, slot):
        count = self.count
        table = {}
        for line in range(count):
            near = line if line < count // 2 else count - 1 - line
            toward = near + slot < count
            distance = slot if toward else near + slot + 1 - count
            above = toward == (line < count // 2)
            table[line] = held[distance][0 if above == (line % 2 == 0) else 1]
        return self.choose(table)

    def pick(self, blocks, distance, even):
        count, half = self.count, self.count // 2
        table = {}
        for line in range(count):
            up = even == (line % 2 == 0)
            if not 0 <= (line + distance if up else line - distance) < count:
                continue
            if up:
                slot = distance if line < half else line + distance
            else:
                slot = distance if line >= half else count - 1 - line + distance
            table[line] = blocks[slot]
        return self.choose(table) if table else None

    def step_reduce(self, step, blocks, arrived):
        distance = self.count - 1 - step
        even, odd = self.pick(blocks, distance, True), self.pick(blocks, distance, False)
        if arrived is not None:
            from_even, from_odd = self.inward(arrived)
            even = even + from_odd
            odd = odd + from_even
        sent = None if odd is None else self.odd(odd.astype(bf16))
        return self.even(even.astype(bf16)), sent

    def inward(self, arrived):
        even, odd = arrived
        if odd is None:
            return even.astype(f32), 0.0
        end = (self.line == 0) | (self.line == self.count - 1)
        return even.astype(f32), jnp.where(end, 0.0, odd.astype(f32))

    def turn(self, values, steps):
        pairs = [
            (2 * i + k, 2 * ((i + steps) % self.count) + k)
            for i in range(self.count)
            for k in range(2)
        ]
        return lax.ppermute(values, "expert", pairs)


def core_swap(values):
    return lax.ppermute(values, "shard", [(i, i ^ 1) for i in range(lax.axis_size("shard"))])


def row_swap(values):
    return lax.ppermute(values, "shard", [(i, i ^ 2) for i in range(lax.axis_size("shard"))])


def column_units(lines):
    mine = lax.axis_index("shard")
    units = []
    for mask in (0, 1, 2, 3):
        first = lines.side if mask >= 2 else 0
        units += [(mine ^ mask) * 2 + first, (mine ^ mask) * 2 + 1 - first]
    return units


def column_parts(values, units):
    width = values.shape[1] // 8
    rows = values.shape[0]
    parts = [
        lax.dynamic_slice(values, (0, units[at] * width), (rows, 2 * width)) for at in (0, 2)
    ]
    return parts + [
        lax.dynamic_slice(values, (0, units[at] * width), (rows, width)) for at in range(4, 8)
    ]


def ordered_small(blocks):
    mine = lax.axis_index("shard")
    shape = blocks[0].shape
    whole = jnp.zeros(shape[:-1] + (4 * shape[-1],), blocks[0].dtype)
    for mask, block in blocks.items():
        at = (0,) * (len(shape) - 1) + ((mine ^ mask) * shape[-1],)
        whole = lax.dynamic_update_slice(whole, block, at)
    return whole


def split_columns(values):
    mine = lax.axis_index("shard")
    width = values.shape[1] // 4
    return [
        lax.dynamic_slice(values, (0, (mine ^ mask) * width), (values.shape[0], width))
        for mask in range(4)
    ]


def shard_rows_of(values):
    return jnp.concatenate([values, row_swap(values)], axis=0)


def shard_rows_all(pair):
    return jnp.concatenate([pair, core_swap(pair)], axis=0)


def exchange_blocks(blocks):
    pairs = lambda mask: [(i, i ^ mask) for i in range(lax.axis_size("shard"))]
    return [blocks[0]] + [lax.ppermute(blocks[r], "shard", pairs(r)) for r in (2, 1, 3)]


def own_columns(values):
    return jnp.concatenate(exchange_blocks(split_columns(values)), axis=0)


class ShardSummed:
    def __init__(self, columns, right):
        self.columns, self.right = columns, right
        self.width = columns[0].shape[1]
        self.moving = ()

    @property
    def value(self):
        return self.moving, self.columns, self.right

    @value.setter
    def value(self, value):
        self.moving, self.columns, self.right = value

    def product(self, k):
        return mm_tn(self.columns[k], self.right)

    def core(self):
        sent = [self.product(k).astype(bf16) for k in (3, 1)]
        self.moving = core_swap(jnp.concatenate(sent, axis=0))

    def row(self):
        self.came = self.moving
        across = self.product(2) + self.came[: self.width].astype(f32)
        self.moving = row_swap(across.astype(bf16))

    def keep(self):
        self.kept = self.product(0) + self.came[self.width :].astype(f32)

    def total(self):
        return self.kept + self.moving.astype(f32)


class Summed:
    def __init__(self, lines, part):
        self.lines = lines
        self.part = part
        self.value = ()

    def side(self):
        part = self.part
        half = part.shape[0] // 2
        lines = self.lines
        given = lax.dynamic_slice(part, ((1 - lines.side) * half, 0), (half, part.shape[1]))
        self.kept = lax.dynamic_slice(part, (lines.side * half, 0), (half, part.shape[1]))
        self.value = lines.swap(given.astype(bf16))

    def place(self, steps):
        return (self.lines.line + steps) % self.lines.count

    def scatter(self):
        lines = self.lines
        part = (self.kept + self.value.astype(f32)).reshape(lines.count, -1, self.kept.shape[1])
        low = part.astype(bf16)
        take = lambda steps, x: lax.dynamic_index_in_dim(x, self.place(steps), 0, keepdims=False)
        self.kept = take(0, part)
        self.value = tuple(
            lines.turn(take(steps, low), steps) for steps in range(1, lines.count)
        )

    def spread(self):
        own = self.kept
        for came in self.value:
            own = own + came.astype(f32)
        self.kept = own.astype(bf16)
        self.value = tuple(
            self.lines.turn(self.kept, -steps) for steps in range(1, self.lines.count)
        )

    def assembled(self):
        blocks = jnp.zeros((self.lines.count,) + self.kept.shape, bf16)
        for steps, block in enumerate((self.kept,) + self.value):
            blocks = lax.dynamic_update_slice(blocks, block[None], (self.place(steps), 0, 0))
        return blocks.reshape(-1, self.kept.shape[1])


def merged(sums):
    one = Summed(sums[0].lines, None)
    one.kept = jnp.concatenate([s.kept for s in sums], axis=1)
    one.value = jnp.concatenate([s.value for s in sums], axis=1)
    return one


class Joined:
    def __init__(self, lines, kept):
        self.lines, self.kept = lines, kept
        self.value = lines.swap(kept)

    def whole(self, take):
        low = self.lines.side == 0
        kept, value = take(self.kept), take(self.value)
        pair = (jnp.where(low, kept, value), jnp.where(low, value, kept))
        return jnp.concatenate(pair, axis=0).astype(f32)

    def put(self, whole, layer, take=lambda x: x):
        half = self.kept.shape[0]
        for rows, side in ((self.kept, self.lines.side), (self.value, 1 - self.lines.side)):
            block = take(rows).astype(f32)[None]
            whole = lax.dynamic_update_slice(whole, block, (layer, side * half, 0))
        return whole


class Sent:
    def __init__(self, routing, values):
        self.routing = routing
        self.held = [(values, values)]
        rows = 2 * routing.lines.count * routing.capacity
        self.buffer = jnp.zeros((rows, values.shape[1]), values.dtype)
        self.fars, self.ready = {}, {}

    @property
    def value(self):
        return self.held[-1], self.buffer, self.fars, self.ready

    @value.setter
    def value(self, value):
        self.held[-1], self.buffer, self.fars, self.ready = value

    def step(self):
        self.held = self.routing.lines.step_gather(self.held)

    def put(self, rows, block):
        at = block * self.routing.capacity
        self.buffer = lax.dynamic_update_slice(self.buffer, rows, (at, 0))

    def prepare(self, j):
        block = self.routing.lines.slot(self.held, j)
        self.ready[j] = mm(self.routing.mate_hot[j], block).astype(bf16)

    def send(self, j):
        if j not in self.ready:
            self.prepare(j)
        self.fars[j] = self.routing.lines.swap(self.ready.pop(j))

    def place(self, j):
        block = self.routing.lines.slot(self.held, j)
        self.put(mm(self.routing.own_hot[j], block).astype(bf16), j)

    def take(self, j):
        self.put(self.fars.pop(j), self.routing.lines.count + j)

    def round(self, j):
        if j < self.routing.lines.count - 1:
            self.step()
        self.send(j)
        if j > 0:
            self.take(j - 1)
        self.place(j)

    def total(self):
        for j in list(self.fars):
            self.take(j)
        return self.buffer


class Returned:
    def __init__(self, routing, far):
        self.routing = routing
        count = routing.lines.count
        self.blocks = [None] * count + self.cut(far)
        self.parts = [None] * count
        self.steps = 0
        self.came, self.arrived = {}, None

    @property
    def value(self):
        return self.came, self.arrived, self.blocks

    @value.setter
    def value(self, value):
        self.came, self.arrived, self.blocks = value

    def cut(self, rows):
        capacity = self.routing.capacity
        return [rows[at : at + capacity] for at in range(0, rows.shape[0], capacity)]

    def near(self, rows):
        self.blocks = self.cut(rows) + self.blocks[self.routing.lines.count :]

    def swap(self, j):
        lines = self.routing.lines
        self.came[j] = lines.swap(self.blocks[lines.count + j])

    def spread(self, j):
        own, far = self.routing.own_hot[j], self.routing.mate_hot[j]
        self.parts[j] = mm_tn(own, self.blocks[j]) + mm_tn(far, self.came.pop(j))

    def step(self):
        lines = self.routing.lines
        self.spread(lines.count - 1 - self.steps)
        self.arrived = lines.step_reduce(self.steps, self.parts, self.arrived)
        self.steps += 1

    def advance(self, stage):
        self.step()
        self.swap(self.routing.lines.count - 1 - stage)

    def total(self):
        self.spread(0)
        from_even, from_odd = self.routing.lines.inward(self.arrived)
        return self.parts[0] + from_even + from_odd


def settle(moving, *values):
    arrived, values = sync([m.value for m in moving], values)
    for m, value in zip(moving, arrived, strict=True):
        m.value = value
    return values


class Routing:
    pass


def per_device(
    tokens,
    lengths,
    routes,
    slot_order,
    cotangent,
    q_weight,
    key_matrix,
    value_matrix,
    out_weight,
    router_weight,
    attn_gain,
    ffn_gain,
    gate_weight,
    up_weight,
    down_weight,
):
    lines = Lines()
    layer_count = q_weight.shape[0]
    shard_count = lax.axis_size("shard")
    mine = lax.axis_index("shard")
    token_rows, model_width = tokens.shape
    pair_count = token_rows * routes.shape[1]
    experts = router_weight.shape[2]
    assert shard_count == 4 and experts == lines.experts and gate_weight.shape[1] == 1
    hidden_units = gate_weight.shape[3]
    capacity = (pair_count * 5 + 4 * experts - 1) // (4 * experts)
    assert capacity < 256
    sequence_length = token_rows * shard_count
    kv_width = KEY_VALUE_HEADS * HEAD_SIZE

    own_rows = jnp.arange(token_rows, dtype=jnp.int32)
    position = mine * token_rows + own_rows
    key_position = jnp.concatenate([(mine ^ mask) * token_rows + own_rows for mask in (0, 2, 1, 3)])
    query_doc, query_position = documents(lengths[0], position)
    key_doc = documents(lengths[0], key_position)[0]
    tables = rotary_tables(query_position)
    query_marks, key_marks = (query_doc, position), (key_doc, key_position)

    def paired(i):
        parts = []
        for at in range(0, kv_width, HEAD_SIZE):
            parts += [key_matrix[i, :, at : at + HEAD_SIZE], value_matrix[i, :, at : at + HEAD_SIZE]]
        return jnp.concatenate(parts, axis=1)

    small = jnp.concatenate(
        [router_weight.transpose(0, 2, 1), attn_gain[:, None, :], ffn_gain[:, None, :]], axis=1
    )
    routing = Routing()
    routing.lines, routing.capacity = lines, capacity
    late = Sent(routing, cotangent)
    units = column_units(lines)

    def side_half(shards, layer):
        half = shards.shape[1] // 2
        return lax.dynamic_slice(
            shards, (layer, lines.side * half, 0), (1, half, shards.shape[2])
        )[0]

    kv_first = paired(0)
    small_across, small_beside = row_swap(small), core_swap(small)
    kv_across, kv_beside = row_swap(side_half(kv_first[None], 0)), core_swap(kv_first)
    query_half = side_half(q_weight, 0)
    small_across, small_beside, kv_across, kv_beside, query_half, q_gated = sync(
        small_across, small_beside, kv_across, kv_beside, query_half, q_weight
    )
    slot_code = jnp.arange(1, capacity + 1, dtype=jnp.int32).astype(f32)[:, None]
    query_rows = tuple(mark[:, None] for mark in query_marks)
    key_rows = tuple(mark[None, :] for mark in key_marks)

    query_across = row_swap(query_half)
    query_own = q_gated[0]
    query_beside = core_swap(query_own)
    kv_crossed = lines.swap(kv_across)
    kv_across_beside = core_swap(kv_across)
    late.step()
    own_table = slot_table(routes, slot_order[0], experts, capacity)
    small_diagonal = core_swap(small_across)
    small = ordered_small({0: small, 1: small_beside, 2: small_across, 3: small_diagonal})
    routers = [small[i, :experts] for i in range(layer_count)]
    attn_gains = [small[i, experts].astype(f32)[None, :] for i in range(layer_count)]
    ffn_gains = [small[i, experts + 1].astype(f32)[None, :] for i in range(layer_count)]
    stream = tokens.astype(f32)
    normed, attn_inverse = norm_forward(stream, attn_gains[0])
    hidden = normed.astype(bf16)
    matched = column_parts(hidden, units)
    query_across, query_beside, kv_crossed, kv_across_beside, matched, own_table, later = settle(
        [late], query_across, query_beside, kv_crossed, kv_across_beside, matched, own_table,
        (out_weight, key_matrix, value_matrix),
    )
    every = lambda part: lax.all_gather(part, "shard", axis=0, tiled=True)
    gathered = [(None, None, every(later[0][0]))]
    tables, query_rows, key_rows, slot_code = sync(tables, query_rows, key_rows, slot_code)

    query_crossed = lines.swap(query_across)
    query_across_beside = core_swap(query_across)
    kv_pieces = [kv_first, kv_beside, kv_across, kv_crossed, kv_across_beside]
    kv_pieces.append(core_swap(kv_crossed))
    first_pair = shard_rows_of(project(matched, kv_pieces, tables))
    held_tables = [(own_table, own_table)]
    for _ in range(lines.count - 1):
        held_tables = lines.step_gather(held_tables)
    query_crossed, query_across_beside, first_pair, q_gated, later = settle(
        [late], query_crossed, query_across_beside, first_pair, q_gated, later
    )
    near_tables = jnp.stack([lines.slot(held_tables, j) for j in range(lines.count)], axis=0)
    query_pieces = [query_own, query_beside, query_across, query_crossed, query_across_beside]
    query_pieces.append(core_swap(query_crossed))

    def prepare_routing(near_tables, own_table):
        far_tables = lines.swap(near_tables)

        def hot_rows(codes, expert):
            code = lax.dynamic_index_in_dim(codes, expert, 1, keepdims=True)
            return (code == slot_code).astype(bf16)

        routing.own_hot = hot_rows(near_tables, lines.index)
        routing.mate_hot = hot_rows(near_tables, lines.index ^ 1)
        all_hot = jnp.concatenate([routing.own_hot, hot_rows(far_tables, lines.index)], axis=0)
        all_tables = jnp.concatenate([near_tables, far_tables], axis=0)
        row_chosen = jnp.einsum(
            "sct,set->sce", all_hot, (all_tables != 0.0).astype(bf16), preferred_element_type=f32
        ).reshape(2 * lines.count * capacity, experts)
        return own_table.T != 0.0, row_chosen

    own_expert = (jnp.arange(experts) == lines.index).astype(f32)[None, :]
    assert experts <= 64
    gate_marks = jnp.arange(128)[None, :] == lines.index + 64 * jnp.arange(2)[:, None]
    gate_marks = gate_marks.astype(f32)

    weights = (gate_weight, up_weight, down_weight)

    def small_sum(part):
        own = sum(exchange_blocks(split_columns(part)))
        return jnp.pad(own, ((0, -own.shape[0] % 128), (0, 0))).T

    last = layer_count - 1
    stored = []
    for i in range(layer_count):
        w_query, w_kv, w_out = gathered[i]
        if i == 0:
            late.step()
            kv_pair = first_pair
            q_pre = project(matched, query_pieces)
        else:
            if i == last:
                late.send(2)
            normed, attn_inverse = norm_forward(stream, attn_gains[i])
            hidden = normed.astype(bf16)
            kv_own = project([hidden], [w_kv], tables)
            kv_crossed = row_swap(kv_own)
            q_pre = mm(hidden, w_query)
            kv_own, kv_crossed, q_pre = settle([late], kv_own, kv_crossed, q_pre)
            kv_pair = jnp.concatenate([kv_own, kv_crossed], axis=0)
            if i == last:
                late.send(3)
                for k in range(4, lines.count):
                    late.step()
                    late.send(k)
        kv_all = shard_rows_all(kv_pair)
        query, mixed = attend(q_pre, kv_all, tables, query_rows, key_rows)
        stream_mid = stream + mm(mixed, w_out)
        normed_ffn, ffn_inverse = norm_forward(stream_mid, ffn_gains[i])
        routed = normed_ffn.astype(bf16)
        if i == last:
            (routed, gathered[0]) = settle([late], routed, gathered[0])
        else:
            routed, q_gated, later, near_tables = settle(
                [late], routed, q_gated, later, near_tables
            )
            chosen_here, row_chosen = prepare_routing(near_tables, own_table)
        if i == 0:

            def paired_of(k):
                parts = []
                for at in range(0, kv_width, HEAD_SIZE):
                    parts += [later[m][k, :, at : at + HEAD_SIZE] for m in (1, 2)]
                return jnp.concatenate(parts, axis=1)

            for k in range(1, layer_count):
                gathered.append((every(q_gated[k]), every(paired_of(k)), every(later[0][k])))
            gathered[0] = (every(q_gated[0]), every(paired_of(0)), w_out)
        gates = chosen_softmax(mm_nt(routed, routers[i]), chosen_here)
        sent = Sent(routing, routed)
        for j in range(lines.count):
            sent.round(j)
            if i == 0 and j < 2:
                late.prepare(j)
            if i == last:
                late.place(j)
                late.take(j)
            hidden, mixed = settle([sent, late], hidden, mixed)
        columns = [own_columns(hidden), own_columns(mixed)]
        arrived = sent.total()
        if i == 0:
            (arrived,) = settle([late], arrived)
        shared = (arrived, routers[i], row_chosen, own_expert, weights)
        produced, kept = expert_forward(i, 1, *shared)
        if i == 0:
            late.step()
            late.send(0)
        produced, kept = sync(produced, kept)
        back = Returned(routing, produced)
        back.swap(lines.count - 1)
        produced, kept = expert_forward(i, 0, *shared, into=kept)
        if i == 0:
            late.send(1)
        produced, kept = settle([late, back], produced, kept)
        back.near(produced)
        stored.append(
            dict(
                stream=stream,
                attn_inverse=attn_inverse,
                hidden_columns=columns[0],
                query=query,
                kv_all=kv_all,
                mixed_columns=columns[1],
                stream_mid=stream_mid,
                ffn_inverse=ffn_inverse,
                routed=routed,
                gates=gates,
                arrived=arrived,
                kept=kept,
            )
        )
        if i < last:
            for j in range(1, lines.count):
                back.advance(j)
                if i == last - 1 and j in (1, 2):
                    late.prepare(j + 1)
                settle([back, late])
            stream = stream_mid + back.total()

    own_width = model_width // shard_count
    results = dict(
        query=jnp.full((layer_count, own_width, model_width), 0.0, f32),
        out=jnp.full((layer_count, own_width, model_width), 1.0, f32),
        key=jnp.full((layer_count, own_width, kv_width), 0.0, f32),
        value=jnp.full((layer_count, own_width, kv_width), 1.0, f32),
        gate=jnp.full((layer_count, own_width, hidden_units), 0.0, f32),
        up=jnp.full((layer_count, own_width, hidden_units), 1.0, f32),
        down=jnp.full((layer_count, hidden_units // shard_count, model_width), 0.0, f32),
    )

    small_results = [None] * layer_count

    def put_experts(layer, both, down):
        for name, block in (
            ("gate", both[:, :hidden_units]),
            ("up", both[:, hidden_units:]),
            ("down", down),
        ):
            results[name] = lax.dynamic_update_slice(
                results[name], block.astype(f32)[None], (layer, 0, 0)
            )

    def put_kv(layer, joined, take):
        heads = lambda first: lambda x: jnp.concatenate(
            [take(x)[:, at : at + HEAD_SIZE] for at in range(first, 2 * kv_width, 2 * HEAD_SIZE)],
            axis=1,
        )
        results["key"] = joined.put(results["key"], layer, heads(0))
        results["value"] = joined.put(results["value"], layer, heads(HEAD_SIZE))
        rest = lambda x: take(x)[:, 2 * kv_width :]
        small_results[layer] = joined.whole(rest)

    output_back = back
    top = lines.count - 1
    d_arrived = late.total()
    upstream = cotangent.astype(f32)
    for i in reversed(range(layer_count)):
        w_query, w_kv, w_out = gathered[i]
        saved = stored[i]
        if i < last:
            sent = Sent(routing, upstream.astype(bf16))
            columns = stored[i + 1]["hidden_columns"]
            out_above, d_query, d_kv_low, small_grad = waiting
            small_part = small_grad
            for j in range(lines.count):
                sent.round(j)
                moving = []
                if j == 0:
                    d_kv_low = shard_rows_of(d_kv_low)
                if j == 1:
                    d_query = shard_rows_all(d_query)
                    d_kv_low = shard_rows_all(d_kv_low)
                    small_part = small_sum(small_grad)
                if j == 2:
                    query_above = Summed(lines, mm_tn(columns, d_query))
                    query_above.side()
                if j == 3:
                    kv_above = mm_tn(columns, d_kv_low)
                    kv_above = Summed(lines, jnp.concatenate([kv_above, small_part], axis=1))
                    kv_above.side()
                    moving = [query_above, kv_above]
                d_query, d_kv_low, small_part = settle(
                    [sent] + moving, d_query, d_kv_low, small_part
                )
                if j == 1:
                    results, d_query = sync(results, d_query)
                if j == lines.count - 1:
                    d_query, both_grad, down_grad = sync(d_query, both_grad, down_grad)
            put_experts(last, both_grad, down_grad)
            d_arrived = sent.total()
            above = merged([out_above, kv_above, query_above])
            above.scatter()
        gate_pre, up_pre, gated, own_gate = saved["kept"]
        shared = (d_arrived, gate_pre, up_pre, own_gate, gate_marks, weights)
        if i == last:
            output_back.step()
        d_rows, d_both = expert_backward(i, 1, *shared)
        d_rows, d_both = sync(d_rows, d_both)
        back = Returned(routing, d_rows)
        back.swap(top)
        d_rows, d_both = expert_backward(i, 0, *shared, into=d_both)
        moving = [back, output_back if i == last else above]
        d_rows, d_both = settle(moving, d_rows, d_both)
        back.near(d_rows)
        both = ShardSummed(split_columns(saved["arrived"]), d_both)
        down = ShardSummed(split_columns(gated), d_arrived)
        for j in range(1, lines.count):
            back.advance(j)
            moving = [back, both, down]
            if j == 1:
                both.core()
            if j == 2:
                both.row()
                down.core()
                if i == last:
                    for k in reversed(range(2, top)):
                        output_back.swap(k)
                    moving.append(output_back)
            if j == 3:
                both.keep()
                down.row()
                moving = [back, both] + ([output_back] if i == last else [])
            settle(moving)
        down.keep()
        returned = back.total()
        d_gates = returned[:, model_width : model_width + experts]
        d_gates = d_gates + returned[:, model_width + 64 : model_width + 64 + experts]
        gates = saved["gates"]
        d_logits = gates * (d_gates - jnp.sum(gates * d_gates, axis=1, keepdims=True))
        d_logits = d_logits.astype(bf16)
        router_grad = mm_tn(d_logits, saved["routed"])
        d_routed = returned[:, :model_width] + mm(d_logits, routers[i])
        d_stream, ffn_gain_grad = norm_backward(
            saved["stream_mid"], saved["ffn_inverse"], ffn_gains[i], d_routed
        )
        upstream = upstream + d_stream
        d_branch = upstream.astype(bf16)
        d_mixed = mm_nt(d_branch, w_out).astype(bf16)
        if i == last:
            while output_back.steps < top - 1:
                output_back.step()
            output_back.swap(1)
            output_back.swap(0)
            moving = [output_back]
        else:
            above.spread()
            moving = []
        d_branch_crossed = row_swap(d_branch)
        d_query, d_kv = attend_back(
            saved["query"], saved["kv_all"], d_mixed, tables, query_marks, key_marks
        )
        d_query, d_kv, d_branch_crossed = settle(
            moving + [down], d_query, d_kv, d_branch_crossed
        )
        d_branch_pair = jnp.concatenate([d_branch, d_branch_crossed], axis=0)
        both_grad, down_grad = both.total(), down.total()
        pair_rows = 2 * token_rows
        d_kv_pair = d_kv[:pair_rows].astype(f32) + core_swap(d_kv[pair_rows:]).astype(f32)
        d_branch_all = shard_rows_all(d_branch_pair)
        d_kv_pair, d_branch_all, d_query = sync(d_kv_pair, d_branch_all, d_query)
        d_kv_crossed = row_swap(d_kv_pair[token_rows:].astype(bf16))
        d_hidden = mm_nt(d_query, w_query)
        out_part = mm_tn(saved["mixed_columns"], d_branch_all)
        d_kv_crossed, d_query, d_hidden, out_part = sync(
            d_kv_crossed, d_query, d_hidden, out_part
        )
        out_sum = Summed(lines, out_part)
        out_sum.side()
        moving = [out_sum]
        if i == last:
            output_back.step()
            moving.append(output_back)
        else:
            moving.append(above)
        d_query_pair = shard_rows_of(d_query)
        d_kv_low = turn_kv_back(d_kv_pair[:token_rows], d_kv_crossed, tables)
        d_hidden = d_hidden + mm_nt(d_kv_low, w_kv)
        d_stream, attn_gain_grad = norm_backward(
            saved["stream"], saved["attn_inverse"], attn_gains[i], d_hidden
        )
        upstream = upstream + d_stream
        small_grad = jnp.concatenate(
            [router_grad, attn_gain_grad[None, :], ffn_gain_grad[None, :]], axis=0
        )
        upstream, d_kv_low, small_grad = settle(moving, upstream, d_kv_low, small_grad)
        if i == last:
            output = (saved["stream_mid"] + output_back.total()).astype(bf16)
            out_above = out_sum
            waiting = (out_above, d_query_pair, d_kv_low, small_grad)

    hidden_columns = stored[0]["hidden_columns"]
    out_sum.scatter()
    d_kv_crossed = row_swap(d_kv_low)
    small_part = small_sum(small_grad)
    q_sum = Summed(lines, mm_tn(hidden_columns, shard_rows_all(d_query_pair)))
    q_sum.side()
    d_kv_crossed, small_part = settle([q_sum, out_sum], d_kv_crossed, small_part)
    d_kv_pair = jnp.concatenate([d_kv_low, d_kv_crossed], axis=0)
    q_sum.scatter()
    kv_part = mm_tn(hidden_columns, shard_rows_all(d_kv_pair))
    kv_sum = Summed(lines, jnp.concatenate([kv_part, small_part], axis=1))
    kv_sum.side()
    half_result = above.assembled()
    split = half_result.shape[1] - model_width
    above_first = Joined(lines, half_result[:, :split])
    out_sum.spread()
    above_second_rows = half_result[:, split:]
    (above_second_rows,) = settle([q_sum, kv_sum, out_sum], above_second_rows)
    q_sum.spread()
    kv_sum.scatter()
    out_join = Joined(lines, out_sum.assembled())
    above_second = Joined(lines, above_second_rows)
    put_experts(0, both_grad, down_grad)
    (results,) = settle([q_sum, kv_sum, out_join, above_first], results)
    q_join = Joined(lines, q_sum.assembled())
    kv_sum.spread()
    results["out"] = above_first.put(results["out"], last, lambda x: x[:, :model_width])
    put_kv(last, above_first, lambda x: x[:, model_width:])
    results["out"] = out_join.put(results["out"], 0)
    (results,) = settle([q_join, kv_sum, above_second], results)
    kv_join = Joined(lines, kv_sum.assembled())
    results["query"] = above_second.put(results["query"], last)
    results["query"] = q_join.put(results["query"], 0)
    put_kv(0, kv_join, lambda x: x)
    small_result = jnp.stack(small_results, axis=0)
    return (
        output,
        upstream.astype(bf16),
        results["query"],
        results["key"],
        results["value"],
        results["out"],
        small_result[:, :, :experts],
        small_result[:, :, experts],
        small_result[:, :, experts + 1],
        results["gate"][:, None],
        results["up"][:, None],
        results["down"][:, None],
    )


def solution(mesh):
    tokens_spec = P(("expert", "shard"), None)
    shard_spec = P(None, "shard", None)
    expert_spec = P(None, "expert", None, None)
    expert_grad_spec = P(None, "expert", "shard", None)
    return jax.shard_map(
        per_device,
        mesh=mesh,
        in_specs=(
            tokens_spec,
            P("expert", None),
            tokens_spec,
            tokens_spec,
            tokens_spec,
            shard_spec,
            shard_spec,
            shard_spec,
            shard_spec,
            shard_spec,
            P(None, "shard"),
            P(None, "shard"),
            expert_spec,
            expert_spec,
            expert_spec,
        ),
        out_specs=(
            tokens_spec,
            tokens_spec,
            shard_spec,
            shard_spec,
            shard_spec,
            shard_spec,
            shard_spec,
            P(None, "shard"),
            P(None, "shard"),
            expert_grad_spec,
            expert_grad_spec,
            expert_grad_spec,
        ),
        check_vma=False,
    )
```

```python
import math

import jax
import jax.numpy as jnp
from jax import lax
from jax.experimental import pallas as pl
from jax.experimental.pallas import tpu as pltpu
from jax.sharding import PartitionSpec as P

QUERY_HEADS = 12
KEY_VALUE_HEADS = 2
HEAD_SIZE = 128

norm_eps = 1e-06
rope_base = 10000.0
masked_score = -1e30

bf16 = jnp.bfloat16
f32 = jnp.float32


def mm(left, right):
    return jnp.dot(left, right, preferred_element_type=f32)


def mm_tn(left, right):
    return lax.dot_general(left, right, (((0,), (0,)), ((), ())), preferred_element_type=f32)


def mm_nt(left, right):
    return lax.dot_general(left, right, (((1,), (1,)), ((), ())), preferred_element_type=f32)


def norm_forward(values, gain):
    inverse = lax.rsqrt(jnp.mean(values * values, axis=-1, keepdims=True) + norm_eps)
    return values * inverse * gain, inverse


def norm_backward(values, inverse, gain, grad):
    scaled = grad * gain
    mean_part = jnp.mean(values * scaled, axis=-1, keepdims=True)
    d_values = inverse * scaled - values * (inverse * inverse * inverse * mean_part)
    d_gain = jnp.sum(grad * values * inverse, axis=0)
    return d_values, d_gain


def sync(*values):
    return lax.optimization_barrier(values)


def rotary_tables(position):
    half_width = HEAD_SIZE // 2
    frequency = rope_base ** (-(jnp.arange(half_width).astype(f32) * 2.0 / HEAD_SIZE))
    angles = position.astype(f32)[:, None] * frequency[None, :]
    cosine, sine = jnp.cos(angles), jnp.sin(angles)
    return jnp.concatenate([cosine, cosine], axis=1), jnp.concatenate([-sine, sine], axis=1)


def turned(values, cosine, sine):
    return values * cosine + pltpu.roll(values, HEAD_SIZE // 2, 1) * sine


def kernel_params():
    return pltpu.CompilerParams(vmem_limit_bytes=40 * 1024 * 1024)


def project(parts, weights, tables=None):
    rows, width = parts[0].shape[0], weights[0].shape[1]
    tile = width if tables else width // 3
    count = len(parts)

    def kernel(*refs):
        out_ref = refs[-1]
        value = mm(refs[0][...], refs[count][...])
        for k in range(1, count):
            value = value + mm(refs[k][...], refs[count + k][...])
        if tables is None:
            out_ref[...] = value
            return
        for at in range(0, width, HEAD_SIZE):
            part = value[:, at : at + HEAD_SIZE]
            if at // HEAD_SIZE % 2 == 0:
                part = turned(part, refs[2 * count][...], refs[2 * count + 1][...])
            out_ref[:, at : at + HEAD_SIZE] = part.astype(bf16)

    fixed = lambda x: pl.BlockSpec(x.shape, lambda t: (0, 0))
    columns = lambda x: pl.BlockSpec((x.shape[0], tile), lambda t: (0, t))
    extra = list(tables) if tables else []
    return pl.pallas_call(
        kernel,
        grid=(width // tile,),
        in_specs=[fixed(x) for x in parts]
        + [columns(x) for x in weights]
        + [fixed(x) for x in extra],
        out_specs=pl.BlockSpec((rows, tile), lambda t: (0, t)),
        out_shape=jax.ShapeDtypeStruct((rows, width), bf16 if tables else f32),
        compiler_params=kernel_params(),
        cost_estimate=pl.CostEstimate(
            flops=2 * rows * width * sum(x.shape[0] for x in weights),
            bytes_accessed=2 * sum(x.size for x in parts + weights),
            transcendentals=0,
        ),
    )(*parts, *weights, *extra)


def turn_kv_back(first, second, tables):
    rows, width = first.shape

    def kernel(first_ref, second_ref, cos_ref, sin_ref, out_ref):
        for at in range(0, width, HEAD_SIZE):
            columns = slice(at, at + HEAD_SIZE)
            part = first_ref[:, columns].astype(f32) + second_ref[:, columns].astype(f32)
            if at // HEAD_SIZE % 2 == 0:
                part = turned(part, cos_ref[...], -sin_ref[...])
            out_ref[:, columns] = part.astype(bf16)

    return pl.pallas_call(
        kernel,
        out_shape=jax.ShapeDtypeStruct((rows, width), bf16),
        compiler_params=kernel_params(),
    )(first, second, *tables)


def attend(q_pre, kv_all, tables, query_marks, key_marks):
    rows, width = q_pre.shape
    keys = kv_all.shape[0]
    heads = width // HEAD_SIZE
    group = heads // KEY_VALUE_HEADS
    together = 3 if group % 3 == 0 else 1
    scale = HEAD_SIZE ** (-0.5)

    def kernel(
        q_ref, kv_ref, cos_ref, sin_ref, qd_ref, qp_ref, kd_ref, kp_ref, turned_ref, out_ref, bias
    ):
        @pl.when(pl.program_id(0) == 0)
        def _():
            seen = (qd_ref[...] == kd_ref[...]) & (kp_ref[...] <= qp_ref[...])
            bias[...] = jnp.where(seen, 0.0, masked_score)

        for at in range(0, together * HEAD_SIZE, HEAD_SIZE):
            head = slice(at, at + HEAD_SIZE)
            query = turned(q_ref[:, head], cos_ref[...], sin_ref[...]).astype(bf16)
            turned_ref[:, head] = query
            scores = mm_nt(query, kv_ref[:, :HEAD_SIZE]) * scale + bias[...]
            weight = jnp.exp(scores - jnp.max(scores, axis=1, keepdims=True))
            total = jnp.sum(weight, axis=1, keepdims=True)
            probs = (weight * (1.0 / total)).astype(bf16)
            out_ref[:, head] = mm(probs, kv_ref[:, HEAD_SIZE:]).astype(bf16)

    fixed = lambda shape: pl.BlockSpec(shape, lambda h: (0, 0))
    by_head = pl.BlockSpec((rows, together * HEAD_SIZE), lambda h: (0, h))
    return pl.pallas_call(
        kernel,
        grid=(heads // together,),
        in_specs=[
            by_head,
            pl.BlockSpec((keys, 2 * HEAD_SIZE), lambda h: (0, h * together // group)),
            fixed((rows, HEAD_SIZE)),
            fixed((rows, HEAD_SIZE)),
            fixed((rows, 1)),
            fixed((rows, 1)),
            fixed((1, keys)),
            fixed((1, keys)),
        ],
        out_specs=[by_head, by_head],
        out_shape=[jax.ShapeDtypeStruct((rows, width), bf16)] * 2,
        scratch_shapes=[pltpu.VMEM((rows, keys), f32)],
        compiler_params=kernel_params(),
        cost_estimate=pl.CostEstimate(
            flops=8 * rows * keys * width,
            bytes_accessed=8 * rows * width,
            transcendentals=rows * keys * heads,
        ),
    )(
        q_pre,
        kv_all,
        *tables,
        *query_marks,
        *key_marks,
    )


def attend_back(query, kv_all, d_mixed, tables, query_marks, key_marks):
    rows, width = query.shape
    keys = kv_all.shape[0]
    heads = width // HEAD_SIZE
    group = heads // KEY_VALUE_HEADS
    together = 3 if group % 3 == 0 else 1
    steps = group // together
    scale = HEAD_SIZE ** (-0.5)

    def kernel(
        q_ref, kv_ref, dm_ref, cos_ref, sin_ref, qd_ref, qp_ref, kd_ref, kp_ref, dq_ref, dkv_ref,
        bias, dkv,
    ):
        head = pl.program_id(0)

        @pl.when(head == 0)
        def _():
            seen = (qd_ref[...] == kd_ref[...]) & (kp_ref[...] <= qp_ref[...])
            bias[...] = jnp.where(seen, 0.0, masked_score)

        key, value = kv_ref[:, :HEAD_SIZE], kv_ref[:, HEAD_SIZE:]
        d_key = d_value = 0.0
        for at in range(0, together * HEAD_SIZE, HEAD_SIZE):
            own = slice(at, at + HEAD_SIZE)
            query, d_out = q_ref[:, own], dm_ref[:, own]
            scores = mm_nt(key, query) * scale + bias[...]
            weight = jnp.exp(scores - jnp.max(scores, axis=0, keepdims=True))
            probs = weight * (1.0 / jnp.sum(weight, axis=0, keepdims=True))
            d_probs = mm_nt(value, d_out)
            mean = jnp.sum(probs * d_probs, axis=0, keepdims=True)
            d_scores = (probs * (d_probs - mean)).astype(bf16)
            d_value = d_value + mm(probs.astype(bf16), d_out)
            d_key = d_key + mm(d_scores, query) * scale
            d_query = mm_tn(d_scores, key) * scale
            dq_ref[:, own] = turned(d_query, cos_ref[...], -sin_ref[...]).astype(bf16)

        @pl.when(head % steps == 0)
        def _():
            dkv[:, :HEAD_SIZE] = d_key
            dkv[:, HEAD_SIZE:] = d_value

        @pl.when(head % steps != 0)
        def _():
            dkv[:, :HEAD_SIZE] += d_key
            dkv[:, HEAD_SIZE:] += d_value

        @pl.when(head % steps == steps - 1)
        def _():
            dkv_ref[...] = dkv[...].astype(bf16)

    fixed = lambda shape: pl.BlockSpec(shape, lambda h: (0, 0))
    by_head = pl.BlockSpec((rows, together * HEAD_SIZE), lambda h: (0, h))
    by_group = pl.BlockSpec((keys, 2 * HEAD_SIZE), lambda h: (0, h // steps))
    return pl.pallas_call(
        kernel,
        grid=(heads // together,),
        in_specs=[
            by_head,
            by_group,
            by_head,
            fixed((rows, HEAD_SIZE)),
            fixed((rows, HEAD_SIZE)),
            fixed((1, rows)),
            fixed((1, rows)),
            fixed((keys, 1)),
            fixed((keys, 1)),
        ],
        out_specs=[by_head, by_group],
        out_shape=[
            jax.ShapeDtypeStruct((rows, width), bf16),
            jax.ShapeDtypeStruct(kv_all.shape, bf16),
        ],
        scratch_shapes=[pltpu.VMEM((keys, rows), f32), pltpu.VMEM((keys, 2 * HEAD_SIZE), f32)],
        compiler_params=kernel_params(),
        cost_estimate=pl.CostEstimate(
            flops=20 * rows * keys * width,
            bytes_accessed=8 * rows * width,
            transcendentals=rows * keys * heads,
        ),
    )(
        query,
        kv_all,
        d_mixed,
        *tables,
        query_marks[0][None, :],
        query_marks[1][None, :],
        key_marks[0][:, None],
        key_marks[1][:, None],
    )


gelu_scale = (2.0 / math.pi) ** 0.5
gelu_cube = 0.044715


def weight_block(weight, layer):
    return pl.BlockSpec((None, None) + weight.shape[2:], lambda t: (layer, 0, 0, 0))


def expert_forward(layer, part, arrived, router, chosen, own, weights, into=None):
    rows, width = arrived.shape
    hidden = weights[0].shape[3]
    tile = rows // 4
    kept = () if into is None else tuple(into)

    def kernel(
        x_ref, router_ref, chosen_ref, own_ref, wg_ref, wu_ref, wd_ref, *others
    ):
        out_ref, pre_ref, up_ref, gated_ref, gate_ref = others[len(kept) :]
        x = x_ref[...]
        logits = mm_nt(x, router_ref[...])
        among = chosen_ref[...] > 0.5
        weight = jnp.exp(
            jnp.where(among, logits, masked_score)
            - jnp.max(jnp.where(among, logits, masked_score), axis=1, keepdims=True)
        )
        weight = jnp.where(among, weight, 0.0)
        total = jnp.sum(weight, axis=1, keepdims=True)
        gate = jnp.sum(weight * own_ref[...], axis=1, keepdims=True)
        gate = gate / jnp.where(total > 0.0, total, 1.0)
        gate_ref[...] = gate
        for at in range(0, hidden, 256):
            part = slice(at, at + 256)
            gate_pre = mm(x, wg_ref[:, part])
            up_pre = mm(x, wu_ref[:, part])
            turn = jnp.tanh(gelu_scale * gate_pre * (1.0 + gelu_cube * gate_pre * gate_pre))
            active = 0.5 * gate_pre * (1.0 + turn) * up_pre
            gated_ref[:, part] = (gate * active).astype(bf16)
            pre_ref[:, part] = gate_pre.astype(bf16)
            up_ref[:, part] = up_pre.astype(bf16)
        out_ref[...] = mm(gated_ref[...], wd_ref[...]).astype(bf16)

    by_row = lambda columns: pl.BlockSpec((tile, columns), lambda t: (2 * part + t, 0))
    fixed = lambda x: pl.BlockSpec(x.shape, lambda t: (0, 0))
    produced, *results = pl.pallas_call(
        kernel,
        grid=(2,),
        in_specs=[by_row(width), fixed(router), by_row(chosen.shape[1]), fixed(own)]
        + [weight_block(w, layer) for w in weights]
        + [pl.BlockSpec(memory_space=pl.ANY)] * len(kept),
        out_specs=[pl.BlockSpec((tile, width), lambda t: (t, 0))]
        + [by_row(hidden), by_row(hidden), by_row(hidden), by_row(1)],
        out_shape=[
            jax.ShapeDtypeStruct((rows // 2, width), bf16),
            jax.ShapeDtypeStruct((rows, hidden), bf16),
            jax.ShapeDtypeStruct((rows, hidden), bf16),
            jax.ShapeDtypeStruct((rows, hidden), bf16),
            jax.ShapeDtypeStruct((rows, 1), f32),
        ],
        input_output_aliases={7 + k: 1 + k for k in range(len(kept))},
        compiler_params=kernel_params(),
        cost_estimate=pl.CostEstimate(
            flops=3 * rows * width * hidden,
            bytes_accessed=2 * rows * width + 6 * rows * hidden + 6 * width * hidden,
            transcendentals=rows * hidden // 2,
        ),
    )(arrived, router, chosen, own, *weights, *kept)
    return produced, results


def expert_backward(layer, part, d_arrived, gate_pre, up_pre, gate, marks, weights, into=None):
    rows, width = d_arrived.shape
    hidden = weights[0].shape[3]
    tile = rows // 4
    kept = () if into is None else (into,)

    def kernel(
        d_ref, pre_ref, up_ref, gate_ref, marks_ref, wg_ref, wu_ref, wd_ref, *others
    ):
        rows_ref, both_ref = others[len(kept) :]
        d_rows, gate = d_ref[...], gate_ref[...]
        d_gate_sum = jnp.zeros((tile, 1), f32)
        for at in range(0, hidden, 256):
            part = slice(at, at + 256)
            du = mm_nt(d_rows, wd_ref[part, :])
            v, up_value = pre_ref[:, part].astype(f32), up_ref[:, part].astype(f32)
            square = v * v
            turn = jnp.tanh(gelu_scale * v * (1.0 + gelu_cube * square))
            half = 0.5 * (1.0 + turn)
            unit = v * half
            slope = half + 0.5 * v * (1.0 - turn * turn) * (
                gelu_scale * (1.0 + 3.0 * gelu_cube * square)
            )
            d_gate_sum += jnp.sum(du * unit * up_value, axis=1, keepdims=True)
            d_active = (gate * du).astype(bf16).astype(f32)
            both_ref[:, part] = (d_active * slope * up_value).astype(bf16)
            both_ref[:, hidden + at : hidden + at + 256] = (d_active * unit).astype(bf16)
        coarse = d_gate_sum.astype(bf16).astype(f32)
        beside = coarse * marks_ref[0:1, :] + (d_gate_sum - coarse) * marks_ref[1:2, :]
        rows_ref[:, width:] = beside.astype(bf16)
        d_pre = mm_nt(both_ref[:, :hidden], wg_ref[...]) + mm_nt(both_ref[:, hidden:], wu_ref[...])
        rows_ref[:, :width] = d_pre.astype(bf16)

    by_row = lambda columns: pl.BlockSpec((tile, columns), lambda t: (2 * part + t, 0))
    return pl.pallas_call(
        kernel,
        grid=(2,),
        in_specs=[by_row(width), by_row(hidden), by_row(hidden), by_row(1)]
        + [pl.BlockSpec(marks.shape, lambda t: (0, 0))]
        + [weight_block(w, layer) for w in weights]
        + [pl.BlockSpec(memory_space=pl.ANY)] * len(kept),
        out_specs=[
            pl.BlockSpec((tile, width + marks.shape[1]), lambda t: (t, 0)),
            by_row(2 * hidden),
        ],
        out_shape=[
            jax.ShapeDtypeStruct((rows // 2, width + marks.shape[1]), bf16),
            jax.ShapeDtypeStruct((rows, 2 * hidden), bf16),
        ],
        input_output_aliases={8 + k: 1 + k for k in range(len(kept))},
        compiler_params=kernel_params(),
        cost_estimate=pl.CostEstimate(
            flops=3 * rows * width * hidden,
            bytes_accessed=2 * rows * width + 6 * rows * hidden + 6 * width * hidden,
            transcendentals=rows * hidden // 2,
        ),
    )(d_arrived, gate_pre, up_pre, gate, marks, *weights, *kept)


def documents(lengths_row, position):
    doc_ends = jnp.cumsum(lengths_row)
    doc_starts = doc_ends - lengths_row
    document_index = jnp.sum((position[:, None] >= doc_ends[None, :]).astype(jnp.int32), axis=1)
    doc_first = jnp.max(
        jnp.where(doc_starts[None, :] <= position[:, None], doc_starts[None, :], 0), axis=1
    )
    return (document_index, position - doc_first)


def slot_table(routes, order_row, experts, capacity):
    token_rows, top_count = routes.shape
    pair_count = token_rows * top_count
    pairs = jnp.arange(pair_count, dtype=jnp.int32)
    named = (order_row[:, None] == pairs[None, :]).astype(bf16)
    of_pair = (
        routes.reshape(pair_count)[:, None] == jnp.arange(experts, dtype=jnp.int32)[None, :]
    ).astype(bf16)
    ranked = mm(named, of_pair)
    earlier = (pairs[None, :] < pairs[:, None]).astype(bf16)
    before = mm(earlier, ranked.astype(bf16))
    code = jnp.where(before < capacity, before + 1.0, -1.0) * ranked
    back = mm_tn(code.astype(bf16), named)
    return jnp.sum(back.reshape(experts, token_rows, top_count), axis=2)


def chosen_softmax(logits, chosen):
    top = jnp.max(jnp.where(chosen, logits, masked_score), axis=-1, keepdims=True)
    weight = jnp.where(chosen, jnp.exp(jnp.where(chosen, logits - top, 0.0)), 0.0)
    total = jnp.sum(weight, axis=-1, keepdims=True)
    return weight / jnp.where(total > 0.0, total, 1.0)


class Lines:
    def __init__(self):
        self.experts = lax.axis_size("expert")
        self.count = self.experts // 2
        self.index = lax.axis_index("expert")
        self.line = self.index // 2
        self.side = self.index % 2

    def source(self, slot):
        count, line = self.count, self.line
        low = jnp.where(line + slot < count, line + slot, count - 1 - slot)
        mirror = count - 1 - line
        high = count - 1 - jnp.where(mirror + slot < count, mirror + slot, count - 1 - slot)
        return jnp.where(line < count // 2, low, high)

    def swap(self, values):
        return lax.ppermute(values, "expert", [(i, i ^ 1) for i in range(self.experts)])

    def even(self, values):
        return lax.ppermute(values, "expert", [(i, i ^ 2) for i in range(self.experts)])

    def odd(self, values):
        count, shards = self.count, lax.axis_size("shard")
        pairs = []
        for i in range(count):
            end = i in (0, count - 1)
            other = i if end else i + 1 if i % 2 else i - 1
            for k in range(2):
                for j in range(shards):
                    to = (2 * other + k) * shards + (j ^ 1 if end else j)
                    pairs.append(((2 * i + k) * shards + j, to))
        return lax.ppermute(values, ("expert", "shard"), pairs)

    def choose(self, table):
        value, seen = None, {}
        for line, array in table.items():
            seen.setdefault(id(array), (array, []))[1].append(line)
        for array, lines in seen.values():
            if value is None:
                value = array
            else:
                here = jnp.any(self.line == jnp.array(lines))
                value = jnp.where(here, array, value)
        return value

    def step_gather(self, held):
        last = len(held) == self.count - 1
        even, odd = held[-1]
        return held + [(self.even(odd), None if last else self.odd(even))]

    def slot(self, held, slot):
        count = self.count
        table = {}
        for line in range(count):
            near = line if line < count // 2 else count - 1 - line
            toward = near + slot < count
            distance = slot if toward else near + slot + 1 - count
            above = toward == (line < count // 2)
            table[line] = held[distance][0 if above == (line % 2 == 0) else 1]
        return self.choose(table)

    def pick(self, blocks, distance, even):
        count, half = self.count, self.count // 2
        table = {}
        for line in range(count):
            up = even == (line % 2 == 0)
            if not 0 <= (line + distance if up else line - distance) < count:
                continue
            if up:
                slot = distance if line < half else line + distance
            else:
                slot = distance if line >= half else count - 1 - line + distance
            table[line] = blocks[slot]
        return self.choose(table) if table else None

    def step_reduce(self, step, blocks, arrived):
        distance = self.count - 1 - step
        even, odd = self.pick(blocks, distance, True), self.pick(blocks, distance, False)
        if arrived is not None:
            from_even, from_odd = self.inward(arrived)
            even = even + from_odd
            odd = odd + from_even
        sent = None if odd is None else self.odd(odd.astype(bf16))
        return self.even(even.astype(bf16)), sent

    def inward(self, arrived):
        even, odd = arrived
        if odd is None:
            return even.astype(f32), 0.0
        end = (self.line == 0) | (self.line == self.count - 1)
        return even.astype(f32), jnp.where(end, 0.0, odd.astype(f32))

    def turn(self, values, steps):
        pairs = [
            (2 * i + k, 2 * ((i + steps) % self.count) + k)
            for i in range(self.count)
            for k in range(2)
        ]
        return lax.ppermute(values, "expert", pairs)


def core_swap(values):
    return lax.ppermute(values, "shard", [(i, i ^ 1) for i in range(lax.axis_size("shard"))])


def row_swap(values):
    return lax.ppermute(values, "shard", [(i, i ^ 2) for i in range(lax.axis_size("shard"))])


def column_units(lines):
    mine = lax.axis_index("shard")
    units = []
    for mask in (0, 1, 2, 3):
        first = lines.side if mask >= 2 else 0
        units += [(mine ^ mask) * 2 + first, (mine ^ mask) * 2 + 1 - first]
    return units


def column_parts(values, units):
    width = values.shape[1] // 8
    rows = values.shape[0]
    parts = [
        lax.dynamic_slice(values, (0, units[at] * width), (rows, 2 * width)) for at in (0, 2)
    ]
    return parts + [
        lax.dynamic_slice(values, (0, units[at] * width), (rows, width)) for at in range(4, 8)
    ]


def ordered_small(blocks):
    mine = lax.axis_index("shard")
    shape = blocks[0].shape
    whole = jnp.zeros(shape[:-1] + (4 * shape[-1],), blocks[0].dtype)
    for mask, block in blocks.items():
        at = (0,) * (len(shape) - 1) + ((mine ^ mask) * shape[-1],)
        whole = lax.dynamic_update_slice(whole, block, at)
    return whole


def split_columns(values):
    mine = lax.axis_index("shard")
    width = values.shape[1] // 4
    return [
        lax.dynamic_slice(values, (0, (mine ^ mask) * width), (values.shape[0], width))
        for mask in range(4)
    ]


def shard_rows_of(values):
    return jnp.concatenate([values, row_swap(values)], axis=0)


def shard_rows_all(pair):
    return jnp.concatenate([pair, core_swap(pair)], axis=0)


def exchange_blocks(blocks):
    pairs = lambda mask: [(i, i ^ mask) for i in range(lax.axis_size("shard"))]
    return [blocks[0]] + [lax.ppermute(blocks[r], "shard", pairs(r)) for r in (2, 1, 3)]


def own_columns(values):
    return jnp.concatenate(exchange_blocks(split_columns(values)), axis=0)


class ShardSummed:
    def __init__(self, columns, right):
        self.columns, self.right = columns, right
        self.width = columns[0].shape[1]
        self.moving = ()

    @property
    def value(self):
        return self.moving, self.columns, self.right

    @value.setter
    def value(self, value):
        self.moving, self.columns, self.right = value

    def product(self, k):
        return mm_tn(self.columns[k], self.right)

    def core(self):
        sent = [self.product(k).astype(bf16) for k in (3, 1)]
        self.moving = core_swap(jnp.concatenate(sent, axis=0))

    def row(self):
        self.came = self.moving
        across = self.product(2) + self.came[: self.width].astype(f32)
        self.moving = row_swap(across.astype(bf16))

    def keep(self):
        self.kept = self.product(0) + self.came[self.width :].astype(f32)

    def total(self):
        return self.kept + self.moving.astype(f32)


class Summed:
    def __init__(self, lines, part):
        self.lines = lines
        self.part = part
        self.value = ()

    def side(self):
        part = self.part
        half = part.shape[0] // 2
        lines = self.lines
        given = lax.dynamic_slice(part, ((1 - lines.side) * half, 0), (half, part.shape[1]))
        self.kept = lax.dynamic_slice(part, (lines.side * half, 0), (half, part.shape[1]))
        self.value = lines.swap(given.astype(bf16))

    def place(self, steps):
        return (self.lines.line + steps) % self.lines.count

    def scatter(self):
        lines = self.lines
        part = (self.kept + self.value.astype(f32)).reshape(lines.count, -1, self.kept.shape[1])
        low = part.astype(bf16)
        take = lambda steps, x: lax.dynamic_index_in_dim(x, self.place(steps), 0, keepdims=False)
        self.kept = take(0, part)
        self.value = tuple(
            lines.turn(take(steps, low), steps) for steps in range(1, lines.count)
        )

    def spread(self):
        own = self.kept
        for came in self.value:
            own = own + came.astype(f32)
        self.kept = own.astype(bf16)
        self.value = tuple(
            self.lines.turn(self.kept, -steps) for steps in range(1, self.lines.count)
        )

    def assembled(self):
        blocks = jnp.zeros((self.lines.count,) + self.kept.shape, bf16)
        for steps, block in enumerate((self.kept,) + self.value):
            blocks = lax.dynamic_update_slice(blocks, block[None], (self.place(steps), 0, 0))
        return blocks.reshape(-1, self.kept.shape[1])


def merged(sums):
    one = Summed(sums[0].lines, None)
    one.kept = jnp.concatenate([s.kept for s in sums], axis=1)
    one.value = jnp.concatenate([s.value for s in sums], axis=1)
    return one


class Joined:
    def __init__(self, lines, kept):
        self.lines, self.kept = lines, kept
        self.value = lines.swap(kept)

    def whole(self, take):
        low = self.lines.side == 0
        kept, value = take(self.kept), take(self.value)
        pair = (jnp.where(low, kept, value), jnp.where(low, value, kept))
        return jnp.concatenate(pair, axis=0).astype(f32)

    def put(self, whole, layer, take=lambda x: x):
        half = self.kept.shape[0]
        for rows, side in ((self.kept, self.lines.side), (self.value, 1 - self.lines.side)):
            block = take(rows).astype(f32)[None]
            whole = lax.dynamic_update_slice(whole, block, (layer, side * half, 0))
        return whole


class Sent:
    def __init__(self, routing, values):
        self.routing = routing
        self.held = [(values, values)]
        rows = 2 * routing.lines.count * routing.capacity
        self.buffer = jnp.zeros((rows, values.shape[1]), values.dtype)
        self.fars, self.ready = {}, {}

    @property
    def value(self):
        return self.held[-1], self.buffer, self.fars, self.ready

    @value.setter
    def value(self, value):
        self.held[-1], self.buffer, self.fars, self.ready = value

    def step(self):
        self.held = self.routing.lines.step_gather(self.held)

    def put(self, rows, block):
        at = block * self.routing.capacity
        self.buffer = lax.dynamic_update_slice(self.buffer, rows, (at, 0))

    def prepare(self, j):
        block = self.routing.lines.slot(self.held, j)
        self.ready[j] = mm(self.routing.mate_hot[j], block).astype(bf16)

    def send(self, j):
        if j not in self.ready:
            self.prepare(j)
        self.fars[j] = self.routing.lines.swap(self.ready.pop(j))

    def place(self, j):
        block = self.routing.lines.slot(self.held, j)
        self.put(mm(self.routing.own_hot[j], block).astype(bf16), j)

    def take(self, j):
        self.put(self.fars.pop(j), self.routing.lines.count + j)

    def round(self, j):
        if j < self.routing.lines.count - 1:
            self.step()
        self.send(j)
        if j > 0:
            self.take(j - 1)
        self.place(j)

    def total(self):
        for j in list(self.fars):
            self.take(j)
        return self.buffer


class Returned:
    def __init__(self, routing, far):
        self.routing = routing
        count = routing.lines.count
        self.blocks = [None] * count + self.cut(far)
        self.parts = [None] * count
        self.steps = 0
        self.came, self.arrived = {}, None

    @property
    def value(self):
        return self.came, self.arrived, self.blocks

    @value.setter
    def value(self, value):
        self.came, self.arrived, self.blocks = value

    def cut(self, rows):
        capacity = self.routing.capacity
        return [rows[at : at + capacity] for at in range(0, rows.shape[0], capacity)]

    def near(self, rows):
        self.blocks = self.cut(rows) + self.blocks[self.routing.lines.count :]

    def swap(self, j):
        lines = self.routing.lines
        self.came[j] = lines.swap(self.blocks[lines.count + j])

    def spread(self, j):
        own, far = self.routing.own_hot[j], self.routing.mate_hot[j]
        self.parts[j] = mm_tn(own, self.blocks[j]) + mm_tn(far, self.came.pop(j))

    def step(self):
        lines = self.routing.lines
        self.spread(lines.count - 1 - self.steps)
        self.arrived = lines.step_reduce(self.steps, self.parts, self.arrived)
        self.steps += 1

    def advance(self, stage):
        self.step()
        self.swap(self.routing.lines.count - 1 - stage)

    def total(self):
        self.spread(0)
        from_even, from_odd = self.routing.lines.inward(self.arrived)
        return self.parts[0] + from_even + from_odd


def settle(moving, *values):
    arrived, values = sync([m.value for m in moving], values)
    for m, value in zip(moving, arrived, strict=True):
        m.value = value
    return values


class Routing:
    pass


def per_device(
    tokens,
    lengths,
    routes,
    slot_order,
    cotangent,
    q_weight,
    key_matrix,
    value_matrix,
    out_weight,
    router_weight,
    attn_gain,
    ffn_gain,
    gate_weight,
    up_weight,
    down_weight,
):
    lines = Lines()
    layer_count = q_weight.shape[0]
    shard_count = lax.axis_size("shard")
    mine = lax.axis_index("shard")
    token_rows, model_width = tokens.shape
    pair_count = token_rows * routes.shape[1]
    experts = router_weight.shape[2]
    assert shard_count == 4 and experts == lines.experts and gate_weight.shape[1] == 1
    hidden_units = gate_weight.shape[3]
    capacity = (pair_count * 5 + 4 * experts - 1) // (4 * experts)
    assert capacity < 256
    sequence_length = token_rows * shard_count
    kv_width = KEY_VALUE_HEADS * HEAD_SIZE

    own_rows = jnp.arange(token_rows, dtype=jnp.int32)
    position = mine * token_rows + own_rows
    key_position = jnp.concatenate([(mine ^ mask) * token_rows + own_rows for mask in (0, 2, 1, 3)])
    query_doc, query_position = documents(lengths[0], position)
    key_doc = documents(lengths[0], key_position)[0]
    tables = rotary_tables(query_position)
    query_marks, key_marks = (query_doc, position), (key_doc, key_position)

    def paired(i):
        parts = []
        for at in range(0, kv_width, HEAD_SIZE):
            parts += [key_matrix[i, :, at : at + HEAD_SIZE], value_matrix[i, :, at : at + HEAD_SIZE]]
        return jnp.concatenate(parts, axis=1)

    small = jnp.concatenate(
        [router_weight.transpose(0, 2, 1), attn_gain[:, None, :], ffn_gain[:, None, :]], axis=1
    )
    routing = Routing()
    routing.lines, routing.capacity = lines, capacity
    late = Sent(routing, cotangent)
    units = column_units(lines)

    def side_half(shards, layer):
        half = shards.shape[1] // 2
        return lax.dynamic_slice(
            shards, (layer, lines.side * half, 0), (1, half, shards.shape[2])
        )[0]

    kv_first = paired(0)
    small_across, small_beside = row_swap(small), core_swap(small)
    kv_across, kv_beside = row_swap(side_half(kv_first[None], 0)), core_swap(kv_first)
    query_half = side_half(q_weight, 0)
    small_across, small_beside, kv_across, kv_beside, query_half, q_gated = sync(
        small_across, small_beside, kv_across, kv_beside, query_half, q_weight
    )
    slot_code = jnp.arange(1, capacity + 1, dtype=jnp.int32).astype(f32)[:, None]
    query_rows = tuple(mark[:, None] for mark in query_marks)
    key_rows = tuple(mark[None, :] for mark in key_marks)

    query_across = row_swap(query_half)
    query_own = q_gated[0]
    query_beside = core_swap(query_own)
    kv_crossed = lines.swap(kv_across)
    kv_across_beside = core_swap(kv_across)
    late.step()
    own_table = slot_table(routes, slot_order[0], experts, capacity)
    small_diagonal = core_swap(small_across)
    small = ordered_small({0: small, 1: small_beside, 2: small_across, 3: small_diagonal})
    routers = [small[i, :experts] for i in range(layer_count)]
    attn_gains = [small[i, experts].astype(f32)[None, :] for i in range(layer_count)]
    ffn_gains = [small[i, experts + 1].astype(f32)[None, :] for i in range(layer_count)]
    stream = tokens.astype(f32)
    normed, attn_inverse = norm_forward(stream, attn_gains[0])
    hidden = normed.astype(bf16)
    matched = column_parts(hidden, units)
    query_across, query_beside, kv_crossed, kv_across_beside, matched, own_table, later = settle(
        [late], query_across, query_beside, kv_crossed, kv_across_beside, matched, own_table,
        (out_weight, key_matrix, value_matrix),
    )
    every = lambda part: lax.all_gather(part, "shard", axis=0, tiled=True)
    gathered = [(None, None, every(later[0][0]))]
    tables, query_rows, key_rows, slot_code = sync(tables, query_rows, key_rows, slot_code)

    query_crossed = lines.swap(query_across)
    query_across_beside = core_swap(query_across)
    kv_pieces = [kv_first, kv_beside, kv_across, kv_crossed, kv_across_beside]
    kv_pieces.append(core_swap(kv_crossed))
    first_pair = shard_rows_of(project(matched, kv_pieces, tables))
    held_tables = [(own_table, own_table)]
    for _ in range(lines.count - 1):
        held_tables = lines.step_gather(held_tables)
    query_crossed, query_across_beside, first_pair, q_gated, later = settle(
        [late], query_crossed, query_across_beside, first_pair, q_gated, later
    )
    near_tables = jnp.stack([lines.slot(held_tables, j) for j in range(lines.count)], axis=0)
    query_pieces = [query_own, query_beside, query_across, query_crossed, query_across_beside]
    query_pieces.append(core_swap(query_crossed))

    def prepare_routing(near_tables, own_table):
        far_tables = lines.swap(near_tables)

        def hot_rows(codes, expert):
            code = lax.dynamic_index_in_dim(codes, expert, 1, keepdims=True)
            return (code == slot_code).astype(bf16)

        routing.own_hot = hot_rows(near_tables, lines.index)
        routing.mate_hot = hot_rows(near_tables, lines.index ^ 1)
        all_hot = jnp.concatenate([routing.own_hot, hot_rows(far_tables, lines.index)], axis=0)
        all_tables = jnp.concatenate([near_tables, far_tables], axis=0)
        row_chosen = jnp.einsum(
            "sct,set->sce", all_hot, (all_tables != 0.0).astype(bf16), preferred_element_type=f32
        ).reshape(2 * lines.count * capacity, experts)
        return own_table.T != 0.0, row_chosen

    own_expert = (jnp.arange(experts) == lines.index).astype(f32)[None, :]
    assert experts <= 64
    gate_marks = jnp.arange(128)[None, :] == lines.index + 64 * jnp.arange(2)[:, None]
    gate_marks = gate_marks.astype(f32)

    weights = (gate_weight, up_weight, down_weight)

    def small_sum(part):
        own = sum(exchange_blocks(split_columns(part)))
        return jnp.pad(own, ((0, -own.shape[0] % 128), (0, 0))).T

    last = layer_count - 1
    stored = []
    for i in range(layer_count):
        w_query, w_kv, w_out = gathered[i]
        if i == 0:
            late.step()
            kv_pair = first_pair
            q_pre = project(matched, query_pieces)
        else:
            if i == last:
                late.send(2)
            normed, attn_inverse = norm_forward(stream, attn_gains[i])
            hidden = normed.astype(bf16)
            kv_own = project([hidden], [w_kv], tables)
            kv_crossed = row_swap(kv_own)
            q_pre = mm(hidden, w_query)
            kv_own, kv_crossed, q_pre = settle([late], kv_own, kv_crossed, q_pre)
            kv_pair = jnp.concatenate([kv_own, kv_crossed], axis=0)
            if i == last:
                late.send(3)
                for k in range(4, lines.count):
                    late.step()
                    late.send(k)
        kv_all = shard_rows_all(kv_pair)
        query, mixed = attend(q_pre, kv_all, tables, query_rows, key_rows)
        stream_mid = stream + mm(mixed, w_out)
        normed_ffn, ffn_inverse = norm_forward(stream_mid, ffn_gains[i])
        routed = normed_ffn.astype(bf16)
        if i == last:
            (routed, gathered[0]) = settle([late], routed, gathered[0])
        else:
            routed, near_tables = settle([late], routed, near_tables)
            chosen_here, row_chosen = prepare_routing(near_tables, own_table)
        if i == 0:

            def paired_of(k):
                parts = []
                for at in range(0, kv_width, HEAD_SIZE):
                    parts += [later[m][k, :, at : at + HEAD_SIZE] for m in (1, 2)]
                return jnp.concatenate(parts, axis=1)
        gates = chosen_softmax(mm_nt(routed, routers[i]), chosen_here)
        sent = Sent(routing, routed)
        for j in range(lines.count):
            sent.round(j)
            if i == 0 and j < 2:
                late.prepare(j)
            if i == last:
                late.place(j)
                late.take(j)
            hidden, mixed, q_gated, later = settle([sent, late], hidden, mixed, q_gated, later)
            if i == 0 and j == 0:
                for k in range(1, layer_count):
                    gathered.append((every(q_gated[k]), every(paired_of(k)), every(later[0][k])))
                gathered[0] = (every(q_gated[0]), every(paired_of(0)), w_out)
        columns = [own_columns(hidden), own_columns(mixed)]
        arrived = sent.total()
        if i == 0:
            (arrived,) = settle([late], arrived)
        shared = (arrived, routers[i], row_chosen, own_expert, weights)
        produced, kept = expert_forward(i, 1, *shared)
        if i == 0:
            late.step()
            late.send(0)
        produced, kept = sync(produced, kept)
        back = Returned(routing, produced)
        back.swap(lines.count - 1)
        produced, kept = expert_forward(i, 0, *shared, into=kept)
        if i == 0:
            late.send(1)
        produced, kept = settle([late, back], produced, kept)
        back.near(produced)
        stored.append(
            dict(
                stream=stream,
                attn_inverse=attn_inverse,
                hidden_columns=columns[0],
                query=query,
                kv_all=kv_all,
                mixed_columns=columns[1],
                stream_mid=stream_mid,
                ffn_inverse=ffn_inverse,
                routed=routed,
                gates=gates,
                arrived=arrived,
                kept=kept,
            )
        )
        if i < last:
            for j in range(1, lines.count):
                back.advance(j)
                if i == last - 1 and j in (1, 2):
                    late.prepare(j + 1)
                if j == 1:
                    stored[i]["arrived_parts"] = split_columns(arrived)
                if j == 2:
                    stored[i]["gated_parts"] = split_columns(kept[2])
                parts = [stored[i].get(n, ()) for n in ("arrived_parts", "gated_parts")]
                parts = settle([back, late], parts)[0]
                stored[i].update(zip(("arrived_parts", "gated_parts"), parts))
            stream = stream_mid + back.total()

    own_width = model_width // shard_count
    results = dict(
        query=jnp.full((layer_count, own_width, model_width), 0.0, f32),
        out=jnp.full((layer_count, own_width, model_width), 1.0, f32),
        key=jnp.full((layer_count, own_width, kv_width), 0.0, f32),
        value=jnp.full((layer_count, own_width, kv_width), 1.0, f32),
        gate=jnp.full((layer_count, own_width, hidden_units), 0.0, f32),
        up=jnp.full((layer_count, own_width, hidden_units), 1.0, f32),
        down=jnp.full((layer_count, hidden_units // shard_count, model_width), 0.0, f32),
    )

    small_results = [None] * layer_count

    def put_experts(layer, both, down):
        for name, block in (
            ("gate", both[:, :hidden_units]),
            ("up", both[:, hidden_units:]),
            ("down", down),
        ):
            results[name] = lax.dynamic_update_slice(
                results[name], block.astype(f32)[None], (layer, 0, 0)
            )

    def put_kv(layer, joined, take):
        heads = lambda first: lambda x: jnp.concatenate(
            [take(x)[:, at : at + HEAD_SIZE] for at in range(first, 2 * kv_width, 2 * HEAD_SIZE)],
            axis=1,
        )
        results["key"] = joined.put(results["key"], layer, heads(0))
        results["value"] = joined.put(results["value"], layer, heads(HEAD_SIZE))
        rest = lambda x: take(x)[:, 2 * kv_width :]
        small_results[layer] = joined.whole(rest)

    output_back = back
    top = lines.count - 1
    d_arrived = late.total()
    upstream = cotangent.astype(f32)
    for i in reversed(range(layer_count)):
        w_query, w_kv, w_out = gathered[i]
        saved = stored[i]
        if i < last:
            sent = Sent(routing, upstream.astype(bf16))
            columns = stored[i + 1]["hidden_columns"]
            out_above, d_query, d_kv_low, small_grad = waiting
            small_part = small_grad
            for j in range(lines.count):
                sent.round(j)
                moving = []
                if j == 0:
                    d_kv_low = shard_rows_of(d_kv_low)
                if j == 1:
                    d_query = shard_rows_all(d_query)
                    d_kv_low = shard_rows_all(d_kv_low)
                    small_part = small_sum(small_grad)
                if j == 2:
                    query_above = Summed(lines, mm_tn(columns, d_query))
                    query_above.side()
                if j == 3:
                    kv_above = mm_tn(columns, d_kv_low)
                    kv_above = Summed(lines, jnp.concatenate([kv_above, small_part], axis=1))
                    kv_above.side()
                    moving = [query_above, kv_above]
                d_query, d_kv_low, small_part = settle(
                    [sent] + moving, d_query, d_kv_low, small_part
                )
                if j == 1:
                    results, d_query = sync(results, d_query)
                if j == 2:
                    names = ("hidden_columns", "mixed_columns")
                    first = [stored[0][name] for name in names]
                    first, d_query = sync(first, d_query)
                    stored[0].update(zip(names, first))
                if j == lines.count - 1:
                    d_query, both_grad, down_grad = sync(d_query, both_grad, down_grad)
            put_experts(last, both_grad, down_grad)
            d_arrived = sent.total()
            above = merged([out_above, kv_above, query_above])
            above.scatter()
        gate_pre, up_pre, gated, own_gate = saved["kept"]
        shared = (d_arrived, gate_pre, up_pre, own_gate, gate_marks, weights)
        if i == last:
            output_back.step()
        d_rows, d_both = expert_backward(i, 1, *shared)
        d_rows, d_both = sync(d_rows, d_both)
        back = Returned(routing, d_rows)
        back.swap(top)
        d_rows, d_both = expert_backward(i, 0, *shared, into=d_both)
        moving = [back, output_back if i == last else above]
        d_rows, d_both = settle(moving, d_rows, d_both)
        back.near(d_rows)
        if i == last:
            both = ShardSummed(split_columns(saved["arrived"]), d_both)
            down = ShardSummed(split_columns(gated), d_arrived)
        else:
            both = ShardSummed(saved["arrived_parts"], d_both)
            down = ShardSummed(saved["gated_parts"], d_arrived)
        for j in range(1, lines.count):
            back.advance(j)
            moving = [back, both, down]
            if j == 1:
                both.core()
            if j == 2:
                both.row()
                down.core()
                if i == last:
                    for k in reversed(range(2, top)):
                        output_back.swap(k)
                    moving.append(output_back)
            if j == 3:
                both.keep()
                down.row()
                moving = [back, both] + ([output_back] if i == last else [])
            settle(moving)
        down.keep()
        returned = back.total()
        d_gates = returned[:, model_width : model_width + experts]
        d_gates = d_gates + returned[:, model_width + 64 : model_width + 64 + experts]
        gates = saved["gates"]
        d_logits = gates * (d_gates - jnp.sum(gates * d_gates, axis=1, keepdims=True))
        d_logits = d_logits.astype(bf16)
        router_grad = mm_tn(d_logits, saved["routed"])
        d_routed = returned[:, :model_width] + mm(d_logits, routers[i])
        d_stream, ffn_gain_grad = norm_backward(
            saved["stream_mid"], saved["ffn_inverse"], ffn_gains[i], d_routed
        )
        upstream = upstream + d_stream
        d_branch = upstream.astype(bf16)
        d_mixed = mm_nt(d_branch, w_out).astype(bf16)
        if i == last:
            while output_back.steps < top - 1:
                output_back.step()
            output_back.swap(1)
            output_back.swap(0)
            moving = [output_back]
        else:
            above.spread()
            moving = []
        d_branch_crossed = row_swap(d_branch)
        d_query, d_kv = attend_back(
            saved["query"], saved["kv_all"], d_mixed, tables, query_marks, key_marks
        )
        d_query, d_kv, d_branch_crossed = settle(
            moving + [down], d_query, d_kv, d_branch_crossed
        )
        d_branch_pair = jnp.concatenate([d_branch, d_branch_crossed], axis=0)
        both_grad, down_grad = both.total(), down.total()
        pair_rows = 2 * token_rows
        d_kv_pair = d_kv[:pair_rows].astype(f32) + core_swap(d_kv[pair_rows:]).astype(f32)
        d_branch_all = shard_rows_all(d_branch_pair)
        d_kv_pair, d_branch_all, d_query = sync(d_kv_pair, d_branch_all, d_query)
        d_kv_crossed = row_swap(d_kv_pair[token_rows:].astype(bf16))
        d_hidden = mm_nt(d_query, w_query)
        out_part = mm_tn(saved["mixed_columns"], d_branch_all)
        d_kv_crossed, d_query, d_hidden, out_part = sync(
            d_kv_crossed, d_query, d_hidden, out_part
        )
        out_sum = Summed(lines, out_part)
        out_sum.side()
        moving = [out_sum]
        if i == last:
            output_back.step()
            moving.append(output_back)
        else:
            moving.append(above)
        d_query_pair = shard_rows_of(d_query)
        d_kv_low = turn_kv_back(d_kv_pair[:token_rows], d_kv_crossed, tables)
        d_hidden = d_hidden + mm_nt(d_kv_low, w_kv)
        d_stream, attn_gain_grad = norm_backward(
            saved["stream"], saved["attn_inverse"], attn_gains[i], d_hidden
        )
        upstream = upstream + d_stream
        small_grad = jnp.concatenate(
            [router_grad, attn_gain_grad[None, :], ffn_gain_grad[None, :]], axis=0
        )
        upstream, d_kv_low, small_grad = settle(moving, upstream, d_kv_low, small_grad)
        if i == last:
            output = (saved["stream_mid"] + output_back.total()).astype(bf16)
            out_above = out_sum
            waiting = (out_above, d_query_pair, d_kv_low, small_grad)

    hidden_columns = stored[0]["hidden_columns"]
    out_sum.scatter()
    d_kv_crossed = row_swap(d_kv_low)
    small_part = small_sum(small_grad)
    q_sum = Summed(lines, mm_tn(hidden_columns, shard_rows_all(d_query_pair)))
    q_sum.side()
    d_kv_crossed, small_part = settle([q_sum, out_sum], d_kv_crossed, small_part)
    d_kv_pair = jnp.concatenate([d_kv_low, d_kv_crossed], axis=0)
    q_sum.scatter()
    kv_part = mm_tn(hidden_columns, shard_rows_all(d_kv_pair))
    kv_sum = Summed(lines, jnp.concatenate([kv_part, small_part], axis=1))
    kv_sum.side()
    half_result = above.assembled()
    split = half_result.shape[1] - model_width
    above_first = Joined(lines, half_result[:, :split])
    out_sum.spread()
    above_second_rows = half_result[:, split:]
    (above_second_rows,) = settle([q_sum, kv_sum, out_sum], above_second_rows)
    q_sum.spread()
    kv_sum.scatter()
    out_join = Joined(lines, out_sum.assembled())
    above_second = Joined(lines, above_second_rows)
    put_experts(0, both_grad, down_grad)
    (results,) = settle([q_sum, kv_sum, out_join, above_first], results)
    q_join = Joined(lines, q_sum.assembled())
    kv_sum.spread()
    results["out"] = above_first.put(results["out"], last, lambda x: x[:, :model_width])
    put_kv(last, above_first, lambda x: x[:, model_width:])
    results["out"] = out_join.put(results["out"], 0)
    (results,) = settle([q_join, kv_sum, above_second], results)
    kv_join = Joined(lines, kv_sum.assembled())
    results["query"] = above_second.put(results["query"], last)
    results["query"] = q_join.put(results["query"], 0)
    put_kv(0, kv_join, lambda x: x)
    small_result = jnp.stack(small_results, axis=0)
    return (
        output,
        upstream.astype(bf16),
        results["query"],
        results["key"],
        results["value"],
        results["out"],
        small_result[:, :, :experts],
        small_result[:, :, experts],
        small_result[:, :, experts + 1],
        results["gate"][:, None],
        results["up"][:, None],
        results["down"][:, None],
    )


def solution(mesh):
    tokens_spec = P(("expert", "shard"), None)
    shard_spec = P(None, "shard", None)
    expert_spec = P(None, "expert", None, None)
    expert_grad_spec = P(None, "expert", "shard", None)
    return jax.shard_map(
        per_device,
        mesh=mesh,
        in_specs=(
            tokens_spec,
            P("expert", None),
            tokens_spec,
            tokens_spec,
            tokens_spec,
            shard_spec,
            shard_spec,
            shard_spec,
            shard_spec,
            shard_spec,
            P(None, "shard"),
            P(None, "shard"),
            expert_spec,
            expert_spec,
            expert_spec,
        ),
        out_specs=(
            tokens_spec,
            tokens_spec,
            shard_spec,
            shard_spec,
            shard_spec,
            shard_spec,
            shard_spec,
            P(None, "shard"),
            P(None, "shard"),
            expert_grad_spec,
            expert_grad_spec,
            expert_grad_spec,
        ),
        check_vma=False,
    )
```

```python
import math

import jax
import jax.numpy as jnp
from jax import lax
from jax.experimental import pallas as pl
from jax.experimental.pallas import tpu as pltpu
from jax.sharding import PartitionSpec as P

QUERY_HEADS = 12
KEY_VALUE_HEADS = 2
HEAD_SIZE = 128

norm_eps = 1e-06
rope_base = 10000.0
masked_score = -1e30

bf16 = jnp.bfloat16
f32 = jnp.float32


def mm(left, right):
    return jnp.dot(left, right, preferred_element_type=f32)


def mm_tn(left, right):
    return lax.dot_general(left, right, (((0,), (0,)), ((), ())), preferred_element_type=f32)


def mm_nt(left, right):
    return lax.dot_general(left, right, (((1,), (1,)), ((), ())), preferred_element_type=f32)


def norm_forward(values, gain):
    inverse = lax.rsqrt(jnp.mean(values * values, axis=-1, keepdims=True) + norm_eps)
    return values * inverse * gain, inverse


def norm_backward(values, inverse, gain, grad):
    scaled = grad * gain
    mean_part = jnp.mean(values * scaled, axis=-1, keepdims=True)
    d_values = inverse * scaled - values * (inverse * inverse * inverse * mean_part)
    d_gain = jnp.sum(grad * values * inverse, axis=0)
    return d_values, d_gain


def sync(*values):
    return lax.optimization_barrier(values)


def rotary_tables(position):
    half_width = HEAD_SIZE // 2
    frequency = rope_base ** (-(jnp.arange(half_width).astype(f32) * 2.0 / HEAD_SIZE))
    angles = position.astype(f32)[:, None] * frequency[None, :]
    cosine, sine = jnp.cos(angles), jnp.sin(angles)
    return jnp.concatenate([cosine, cosine], axis=1), jnp.concatenate([-sine, sine], axis=1)


def turned(values, cosine, sine):
    return values * cosine + pltpu.roll(values, HEAD_SIZE // 2, 1) * sine


def kernel_params():
    return pltpu.CompilerParams(vmem_limit_bytes=40 * 1024 * 1024)


def project(parts, weights, tables=None):
    rows, width = parts[0].shape[0], weights[0].shape[1]
    tile = width if tables else width // 3
    count = len(parts)

    def kernel(*refs):
        out_ref = refs[-1]
        value = mm(refs[0][...], refs[count][...])
        for k in range(1, count):
            value = value + mm(refs[k][...], refs[count + k][...])
        if tables is None:
            out_ref[...] = value
            return
        for at in range(0, width, HEAD_SIZE):
            part = value[:, at : at + HEAD_SIZE]
            if at // HEAD_SIZE % 2 == 0:
                part = turned(part, refs[2 * count][...], refs[2 * count + 1][...])
            out_ref[:, at : at + HEAD_SIZE] = part.astype(bf16)

    fixed = lambda x: pl.BlockSpec(x.shape, lambda t: (0, 0))
    columns = lambda x: pl.BlockSpec((x.shape[0], tile), lambda t: (0, t))
    extra = list(tables) if tables else []
    return pl.pallas_call(
        kernel,
        grid=(width // tile,),
        in_specs=[fixed(x) for x in parts]
        + [columns(x) for x in weights]
        + [fixed(x) for x in extra],
        out_specs=pl.BlockSpec((rows, tile), lambda t: (0, t)),
        out_shape=jax.ShapeDtypeStruct((rows, width), bf16 if tables else f32),
        compiler_params=kernel_params(),
        cost_estimate=pl.CostEstimate(
            flops=2 * rows * width * sum(x.shape[0] for x in weights),
            bytes_accessed=2 * sum(x.size for x in parts + weights),
            transcendentals=0,
        ),
    )(*parts, *weights, *extra)


def turn_kv_back(first, second, tables):
    rows, width = first.shape

    def kernel(first_ref, second_ref, cos_ref, sin_ref, out_ref):
        for at in range(0, width, HEAD_SIZE):
            columns = slice(at, at + HEAD_SIZE)
            part = first_ref[:, columns].astype(f32) + second_ref[:, columns].astype(f32)
            if at // HEAD_SIZE % 2 == 0:
                part = turned(part, cos_ref[...], -sin_ref[...])
            out_ref[:, columns] = part.astype(bf16)

    return pl.pallas_call(
        kernel,
        out_shape=jax.ShapeDtypeStruct((rows, width), bf16),
        compiler_params=kernel_params(),
    )(first, second, *tables)


def attend(q_pre, kv_all, tables, query_marks, key_marks):
    rows, width = q_pre.shape
    keys = kv_all.shape[0]
    heads = width // HEAD_SIZE
    group = heads // KEY_VALUE_HEADS
    together = 3 if group % 3 == 0 else 1
    scale = HEAD_SIZE ** (-0.5)

    def kernel(
        q_ref, kv_ref, cos_ref, sin_ref, qd_ref, qp_ref, kd_ref, kp_ref, turned_ref, out_ref, bias
    ):
        @pl.when(pl.program_id(0) == 0)
        def _():
            seen = (qd_ref[...] == kd_ref[...]) & (kp_ref[...] <= qp_ref[...])
            bias[...] = jnp.where(seen, 0.0, masked_score)

        for at in range(0, together * HEAD_SIZE, HEAD_SIZE):
            head = slice(at, at + HEAD_SIZE)
            query = turned(q_ref[:, head], cos_ref[...], sin_ref[...]).astype(bf16)
            turned_ref[:, head] = query
            scores = mm_nt(query, kv_ref[:, :HEAD_SIZE]) * scale + bias[...]
            weight = jnp.exp(scores - jnp.max(scores, axis=1, keepdims=True))
            total = jnp.sum(weight, axis=1, keepdims=True)
            probs = (weight * (1.0 / total)).astype(bf16)
            out_ref[:, head] = mm(probs, kv_ref[:, HEAD_SIZE:]).astype(bf16)

    fixed = lambda shape: pl.BlockSpec(shape, lambda h: (0, 0))
    by_head = pl.BlockSpec((rows, together * HEAD_SIZE), lambda h: (0, h))
    return pl.pallas_call(
        kernel,
        grid=(heads // together,),
        in_specs=[
            by_head,
            pl.BlockSpec((keys, 2 * HEAD_SIZE), lambda h: (0, h * together // group)),
            fixed((rows, HEAD_SIZE)),
            fixed((rows, HEAD_SIZE)),
            fixed((rows, 1)),
            fixed((rows, 1)),
            fixed((1, keys)),
            fixed((1, keys)),
        ],
        out_specs=[by_head, by_head],
        out_shape=[jax.ShapeDtypeStruct((rows, width), bf16)] * 2,
        scratch_shapes=[pltpu.VMEM((rows, keys), f32)],
        compiler_params=kernel_params(),
        cost_estimate=pl.CostEstimate(
            flops=8 * rows * keys * width,
            bytes_accessed=8 * rows * width,
            transcendentals=rows * keys * heads,
        ),
    )(
        q_pre,
        kv_all,
        *tables,
        *query_marks,
        *key_marks,
    )


def attend_back(query, kv_all, d_mixed, tables, query_marks, key_marks):
    rows, width = query.shape
    keys = kv_all.shape[0]
    heads = width // HEAD_SIZE
    group = heads // KEY_VALUE_HEADS
    together = 3 if group % 3 == 0 else 1
    steps = group // together
    scale = HEAD_SIZE ** (-0.5)

    def kernel(
        q_ref, kv_ref, dm_ref, cos_ref, sin_ref, qd_ref, qp_ref, kd_ref, kp_ref, dq_ref, dkv_ref,
        bias, dkv,
    ):
        head = pl.program_id(0)

        @pl.when(head == 0)
        def _():
            seen = (qd_ref[...] == kd_ref[...]) & (kp_ref[...] <= qp_ref[...])
            bias[...] = jnp.where(seen, 0.0, masked_score)

        key, value = kv_ref[:, :HEAD_SIZE], kv_ref[:, HEAD_SIZE:]
        d_key = d_value = 0.0
        for at in range(0, together * HEAD_SIZE, HEAD_SIZE):
            own = slice(at, at + HEAD_SIZE)
            query, d_out = q_ref[:, own], dm_ref[:, own]
            scores = mm_nt(key, query) * scale + bias[...]
            weight = jnp.exp(scores - jnp.max(scores, axis=0, keepdims=True))
            probs = weight * (1.0 / jnp.sum(weight, axis=0, keepdims=True))
            d_probs = mm_nt(value, d_out)
            mean = jnp.sum(probs * d_probs, axis=0, keepdims=True)
            d_scores = (probs * (d_probs - mean)).astype(bf16)
            d_value = d_value + mm(probs.astype(bf16), d_out)
            d_key = d_key + mm(d_scores, query) * scale
            d_query = mm_tn(d_scores, key) * scale
            dq_ref[:, own] = turned(d_query, cos_ref[...], -sin_ref[...]).astype(bf16)

        @pl.when(head % steps == 0)
        def _():
            dkv[:, :HEAD_SIZE] = d_key
            dkv[:, HEAD_SIZE:] = d_value

        @pl.when(head % steps != 0)
        def _():
            dkv[:, :HEAD_SIZE] += d_key
            dkv[:, HEAD_SIZE:] += d_value

        @pl.when(head % steps == steps - 1)
        def _():
            dkv_ref[...] = dkv[...].astype(bf16)

    fixed = lambda shape: pl.BlockSpec(shape, lambda h: (0, 0))
    by_head = pl.BlockSpec((rows, together * HEAD_SIZE), lambda h: (0, h))
    by_group = pl.BlockSpec((keys, 2 * HEAD_SIZE), lambda h: (0, h // steps))
    return pl.pallas_call(
        kernel,
        grid=(heads // together,),
        in_specs=[
            by_head,
            by_group,
            by_head,
            fixed((rows, HEAD_SIZE)),
            fixed((rows, HEAD_SIZE)),
            fixed((1, rows)),
            fixed((1, rows)),
            fixed((keys, 1)),
            fixed((keys, 1)),
        ],
        out_specs=[by_head, by_group],
        out_shape=[
            jax.ShapeDtypeStruct((rows, width), bf16),
            jax.ShapeDtypeStruct(kv_all.shape, bf16),
        ],
        scratch_shapes=[pltpu.VMEM((keys, rows), f32), pltpu.VMEM((keys, 2 * HEAD_SIZE), f32)],
        compiler_params=kernel_params(),
        cost_estimate=pl.CostEstimate(
            flops=20 * rows * keys * width,
            bytes_accessed=8 * rows * width,
            transcendentals=rows * keys * heads,
        ),
    )(
        query,
        kv_all,
        d_mixed,
        *tables,
        query_marks[0][None, :],
        query_marks[1][None, :],
        key_marks[0][:, None],
        key_marks[1][:, None],
    )


gelu_scale = (2.0 / math.pi) ** 0.5
gelu_cube = 0.044715


def weight_block(weight, layer):
    return pl.BlockSpec((None, None) + weight.shape[2:], lambda t: (layer, 0, 0, 0))


def expert_forward(layer, part, arrived, router, chosen, own, weights, into=None):
    rows, width = arrived.shape
    hidden = weights[0].shape[3]
    tile = rows // 4
    kept = () if into is None else tuple(into)

    def kernel(
        x_ref, router_ref, chosen_ref, own_ref, wg_ref, wu_ref, wd_ref, *others
    ):
        out_ref, pre_ref, up_ref, gated_ref, gate_ref = others[len(kept) :]
        x = x_ref[...]
        logits = mm_nt(x, router_ref[...])
        among = chosen_ref[...] > 0.5
        weight = jnp.exp(
            jnp.where(among, logits, masked_score)
            - jnp.max(jnp.where(among, logits, masked_score), axis=1, keepdims=True)
        )
        weight = jnp.where(among, weight, 0.0)
        total = jnp.sum(weight, axis=1, keepdims=True)
        gate = jnp.sum(weight * own_ref[...], axis=1, keepdims=True)
        gate = gate / jnp.where(total > 0.0, total, 1.0)
        gate_ref[...] = gate
        for at in range(0, hidden, 256):
            part = slice(at, at + 256)
            gate_pre = mm(x, wg_ref[:, part])
            up_pre = mm(x, wu_ref[:, part])
            turn = jnp.tanh(gelu_scale * gate_pre * (1.0 + gelu_cube * gate_pre * gate_pre))
            active = 0.5 * gate_pre * (1.0 + turn) * up_pre
            gated_ref[:, part] = (gate * active).astype(bf16)
            pre_ref[:, part] = gate_pre.astype(bf16)
            up_ref[:, part] = up_pre.astype(bf16)
        out_ref[...] = mm(gated_ref[...], wd_ref[...]).astype(bf16)

    by_row = lambda columns: pl.BlockSpec((tile, columns), lambda t: (2 * part + t, 0))
    fixed = lambda x: pl.BlockSpec(x.shape, lambda t: (0, 0))
    produced, *results = pl.pallas_call(
        kernel,
        grid=(2,),
        in_specs=[by_row(width), fixed(router), by_row(chosen.shape[1]), fixed(own)]
        + [weight_block(w, layer) for w in weights]
        + [pl.BlockSpec(memory_space=pl.ANY)] * len(kept),
        out_specs=[pl.BlockSpec((tile, width), lambda t: (t, 0))]
        + [by_row(hidden), by_row(hidden), by_row(hidden), by_row(1)],
        out_shape=[
            jax.ShapeDtypeStruct((rows // 2, width), bf16),
            jax.ShapeDtypeStruct((rows, hidden), bf16),
            jax.ShapeDtypeStruct((rows, hidden), bf16),
            jax.ShapeDtypeStruct((rows, hidden), bf16),
            jax.ShapeDtypeStruct((rows, 1), f32),
        ],
        input_output_aliases={7 + k: 1 + k for k in range(len(kept))},
        compiler_params=kernel_params(),
        cost_estimate=pl.CostEstimate(
            flops=3 * rows * width * hidden,
            bytes_accessed=2 * rows * width + 6 * rows * hidden + 6 * width * hidden,
            transcendentals=rows * hidden // 2,
        ),
    )(arrived, router, chosen, own, *weights, *kept)
    return produced, results


def expert_backward(layer, part, d_arrived, gate_pre, up_pre, gate, marks, weights, into=None):
    rows, width = d_arrived.shape
    hidden = weights[0].shape[3]
    tile = rows // 4
    kept = () if into is None else (into,)

    def kernel(
        d_ref, pre_ref, up_ref, gate_ref, marks_ref, wg_ref, wu_ref, wd_ref, *others
    ):
        rows_ref, both_ref = others[len(kept) :]
        d_rows, gate = d_ref[...], gate_ref[...]
        d_gate_sum = jnp.zeros((tile, 1), f32)
        for at in range(0, hidden, 256):
            part = slice(at, at + 256)
            du = mm_nt(d_rows, wd_ref[part, :])
            v, up_value = pre_ref[:, part].astype(f32), up_ref[:, part].astype(f32)
            square = v * v
            turn = jnp.tanh(gelu_scale * v * (1.0 + gelu_cube * square))
            half = 0.5 * (1.0 + turn)
            unit = v * half
            slope = half + 0.5 * v * (1.0 - turn * turn) * (
                gelu_scale * (1.0 + 3.0 * gelu_cube * square)
            )
            d_gate_sum += jnp.sum(du * unit * up_value, axis=1, keepdims=True)
            d_active = (gate * du).astype(bf16).astype(f32)
            both_ref[:, part] = (d_active * slope * up_value).astype(bf16)
            both_ref[:, hidden + at : hidden + at + 256] = (d_active * unit).astype(bf16)
        coarse = d_gate_sum.astype(bf16).astype(f32)
        beside = coarse * marks_ref[0:1, :] + (d_gate_sum - coarse) * marks_ref[1:2, :]
        rows_ref[:, width:] = beside.astype(bf16)
        d_pre = mm_nt(both_ref[:, :hidden], wg_ref[...]) + mm_nt(both_ref[:, hidden:], wu_ref[...])
        rows_ref[:, :width] = d_pre.astype(bf16)

    by_row = lambda columns: pl.BlockSpec((tile, columns), lambda t: (2 * part + t, 0))
    return pl.pallas_call(
        kernel,
        grid=(2,),
        in_specs=[by_row(width), by_row(hidden), by_row(hidden), by_row(1)]
        + [pl.BlockSpec(marks.shape, lambda t: (0, 0))]
        + [weight_block(w, layer) for w in weights]
        + [pl.BlockSpec(memory_space=pl.ANY)] * len(kept),
        out_specs=[
            pl.BlockSpec((tile, width + marks.shape[1]), lambda t: (t, 0)),
            by_row(2 * hidden),
        ],
        out_shape=[
            jax.ShapeDtypeStruct((rows // 2, width + marks.shape[1]), bf16),
            jax.ShapeDtypeStruct((rows, 2 * hidden), bf16),
        ],
        input_output_aliases={8 + k: 1 + k for k in range(len(kept))},
        compiler_params=kernel_params(),
        cost_estimate=pl.CostEstimate(
            flops=3 * rows * width * hidden,
            bytes_accessed=2 * rows * width + 6 * rows * hidden + 6 * width * hidden,
            transcendentals=rows * hidden // 2,
        ),
    )(d_arrived, gate_pre, up_pre, gate, marks, *weights, *kept)


def documents(lengths_row, position):
    doc_ends = jnp.cumsum(lengths_row)
    doc_starts = doc_ends - lengths_row
    document_index = jnp.sum((position[:, None] >= doc_ends[None, :]).astype(jnp.int32), axis=1)
    doc_first = jnp.max(
        jnp.where(doc_starts[None, :] <= position[:, None], doc_starts[None, :], 0), axis=1
    )
    return (document_index, position - doc_first)


def slot_table(routes, order_row, experts, capacity):
    token_rows, top_count = routes.shape
    pair_count = token_rows * top_count
    pairs = jnp.arange(pair_count, dtype=jnp.int32)
    named = (order_row[:, None] == pairs[None, :]).astype(bf16)
    of_pair = (
        routes.reshape(pair_count)[:, None] == jnp.arange(experts, dtype=jnp.int32)[None, :]
    ).astype(bf16)
    ranked = mm(named, of_pair)
    earlier = (pairs[None, :] < pairs[:, None]).astype(bf16)
    before = mm(earlier, ranked.astype(bf16))
    code = jnp.where(before < capacity, before + 1.0, -1.0) * ranked
    back = mm_tn(code.astype(bf16), named)
    return jnp.sum(back.reshape(experts, token_rows, top_count), axis=2)


def chosen_softmax(logits, chosen):
    top = jnp.max(jnp.where(chosen, logits, masked_score), axis=-1, keepdims=True)
    weight = jnp.where(chosen, jnp.exp(jnp.where(chosen, logits - top, 0.0)), 0.0)
    total = jnp.sum(weight, axis=-1, keepdims=True)
    return weight / jnp.where(total > 0.0, total, 1.0)


class Lines:
    def __init__(self):
        self.experts = lax.axis_size("expert")
        self.count = self.experts // 2
        self.index = lax.axis_index("expert")
        self.line = self.index // 2
        self.side = self.index % 2

    def source(self, slot):
        count, line = self.count, self.line
        low = jnp.where(line + slot < count, line + slot, count - 1 - slot)
        mirror = count - 1 - line
        high = count - 1 - jnp.where(mirror + slot < count, mirror + slot, count - 1 - slot)
        return jnp.where(line < count // 2, low, high)

    def swap(self, values):
        return lax.ppermute(values, "expert", [(i, i ^ 1) for i in range(self.experts)])

    def even(self, values):
        return lax.ppermute(values, "expert", [(i, i ^ 2) for i in range(self.experts)])

    def odd(self, values):
        count, shards = self.count, lax.axis_size("shard")
        pairs = []
        for i in range(count):
            end = i in (0, count - 1)
            other = i if end else i + 1 if i % 2 else i - 1
            for k in range(2):
                for j in range(shards):
                    to = (2 * other + k) * shards + (j ^ 1 if end else j)
                    pairs.append(((2 * i + k) * shards + j, to))
        return lax.ppermute(values, ("expert", "shard"), pairs)

    def choose(self, table):
        value, seen = None, {}
        for line, array in table.items():
            seen.setdefault(id(array), (array, []))[1].append(line)
        for array, lines in seen.values():
            if value is None:
                value = array
            else:
                here = jnp.any(self.line == jnp.array(lines))
                value = jnp.where(here, array, value)
        return value

    def step_gather(self, held):
        last = len(held) == self.count - 1
        even, odd = held[-1]
        return held + [(self.even(odd), None if last else self.odd(even))]

    def slot(self, held, slot):
        count = self.count
        table = {}
        for line in range(count):
            near = line if line < count // 2 else count - 1 - line
            toward = near + slot < count
            distance = slot if toward else near + slot + 1 - count
            above = toward == (line < count // 2)
            table[line] = held[distance][0 if above == (line % 2 == 0) else 1]
        return self.choose(table)

    def pick(self, blocks, distance, even):
        count, half = self.count, self.count // 2
        table = {}
        for line in range(count):
            up = even == (line % 2 == 0)
            if not 0 <= (line + distance if up else line - distance) < count:
                continue
            if up:
                slot = distance if line < half else line + distance
            else:
                slot = distance if line >= half else count - 1 - line + distance
            table[line] = blocks[slot]
        return self.choose(table) if table else None

    def step_reduce(self, step, blocks, arrived):
        distance = self.count - 1 - step
        even, odd = self.pick(blocks, distance, True), self.pick(blocks, distance, False)
        if arrived is not None:
            from_even, from_odd = self.inward(arrived)
            even = even + from_odd
            odd = odd + from_even
        sent = None if odd is None else self.odd(odd.astype(bf16))
        return self.even(even.astype(bf16)), sent

    def inward(self, arrived):
        even, odd = arrived
        if odd is None:
            return even.astype(f32), 0.0
        end = (self.line == 0) | (self.line == self.count - 1)
        return even.astype(f32), jnp.where(end, 0.0, odd.astype(f32))

    def turn(self, values, steps):
        pairs = [
            (2 * i + k, 2 * ((i + steps) % self.count) + k)
            for i in range(self.count)
            for k in range(2)
        ]
        return lax.ppermute(values, "expert", pairs)


def core_swap(values):
    return lax.ppermute(values, "shard", [(i, i ^ 1) for i in range(lax.axis_size("shard"))])


def row_swap(values):
    return lax.ppermute(values, "shard", [(i, i ^ 2) for i in range(lax.axis_size("shard"))])


def column_units(lines):
    mine = lax.axis_index("shard")
    units = []
    for mask in (0, 1, 2, 3):
        first = lines.side if mask >= 2 else 0
        units += [(mine ^ mask) * 2 + first, (mine ^ mask) * 2 + 1 - first]
    return units


def column_parts(values, units):
    width = values.shape[1] // 8
    rows = values.shape[0]
    parts = [
        lax.dynamic_slice(values, (0, units[at] * width), (rows, 2 * width)) for at in (0, 2)
    ]
    return parts + [
        lax.dynamic_slice(values, (0, units[at] * width), (rows, width)) for at in range(4, 8)
    ]


def ordered_small(blocks):
    mine = lax.axis_index("shard")
    shape = blocks[0].shape
    whole = jnp.zeros(shape[:-1] + (4 * shape[-1],), blocks[0].dtype)
    for mask, block in blocks.items():
        at = (0,) * (len(shape) - 1) + ((mine ^ mask) * shape[-1],)
        whole = lax.dynamic_update_slice(whole, block, at)
    return whole


def split_columns(values):
    mine = lax.axis_index("shard")
    width = values.shape[1] // 4
    return [
        lax.dynamic_slice(values, (0, (mine ^ mask) * width), (values.shape[0], width))
        for mask in range(4)
    ]


def shard_rows_of(values):
    return jnp.concatenate([values, row_swap(values)], axis=0)


def shard_rows_all(pair):
    return jnp.concatenate([pair, core_swap(pair)], axis=0)


def exchange_blocks(blocks):
    pairs = lambda mask: [(i, i ^ mask) for i in range(lax.axis_size("shard"))]
    return [blocks[0]] + [lax.ppermute(blocks[r], "shard", pairs(r)) for r in (2, 1, 3)]


def own_columns(values):
    return jnp.concatenate(exchange_blocks(split_columns(values)), axis=0)


class ShardSummed:
    def __init__(self, columns, right):
        self.columns, self.right = columns, right
        self.width = columns[0].shape[1]
        self.moving = ()

    @property
    def value(self):
        return self.moving, self.columns, self.right

    @value.setter
    def value(self, value):
        self.moving, self.columns, self.right = value

    def product(self, k):
        return mm_tn(self.columns[k], self.right)

    def core(self):
        sent = [self.product(k).astype(bf16) for k in (3, 1)]
        self.moving = core_swap(jnp.concatenate(sent, axis=0))

    def row(self):
        self.came = self.moving
        across = self.product(2) + self.came[: self.width].astype(f32)
        self.moving = row_swap(across.astype(bf16))

    def keep(self):
        self.kept = self.product(0) + self.came[self.width :].astype(f32)

    def total(self):
        return self.kept + self.moving.astype(f32)


class Summed:
    def __init__(self, lines, part):
        self.lines = lines
        self.part = part
        self.value = ()

    def side(self):
        part = self.part
        half = part.shape[0] // 2
        lines = self.lines
        given = lax.dynamic_slice(part, ((1 - lines.side) * half, 0), (half, part.shape[1]))
        self.kept = lax.dynamic_slice(part, (lines.side * half, 0), (half, part.shape[1]))
        self.value = lines.swap(given.astype(bf16))

    def place(self, steps):
        return (self.lines.line + steps) % self.lines.count

    def scatter(self):
        lines = self.lines
        part = (self.kept + self.value.astype(f32)).reshape(lines.count, -1, self.kept.shape[1])
        low = part.astype(bf16)
        take = lambda steps, x: lax.dynamic_index_in_dim(x, self.place(steps), 0, keepdims=False)
        self.kept = take(0, part)
        self.value = tuple(
            lines.turn(take(steps, low), steps) for steps in range(1, lines.count)
        )

    def spread(self):
        own = self.kept
        for came in self.value:
            own = own + came.astype(f32)
        self.kept = own.astype(bf16)
        self.value = tuple(
            self.lines.turn(self.kept, -steps) for steps in range(1, self.lines.count)
        )

    def assembled(self):
        blocks = jnp.zeros((self.lines.count,) + self.kept.shape, bf16)
        for steps, block in enumerate((self.kept,) + self.value):
            blocks = lax.dynamic_update_slice(blocks, block[None], (self.place(steps), 0, 0))
        return blocks.reshape(-1, self.kept.shape[1])


def merged(sums):
    one = Summed(sums[0].lines, None)
    one.kept = jnp.concatenate([s.kept for s in sums], axis=1)
    one.value = jnp.concatenate([s.value for s in sums], axis=1)
    return one


class Joined:
    def __init__(self, lines, kept):
        self.lines, self.kept = lines, kept
        self.value = lines.swap(kept)

    def whole(self, take):
        low = self.lines.side == 0
        kept, value = take(self.kept), take(self.value)
        pair = (jnp.where(low, kept, value), jnp.where(low, value, kept))
        return jnp.concatenate(pair, axis=0).astype(f32)

    def put(self, whole, layer, take=lambda x: x):
        half = self.kept.shape[0]
        for rows, side in ((self.kept, self.lines.side), (self.value, 1 - self.lines.side)):
            block = take(rows).astype(f32)[None]
            whole = lax.dynamic_update_slice(whole, block, (layer, side * half, 0))
        return whole


class Sent:
    def __init__(self, routing, values):
        self.routing = routing
        self.held = [(values, values)]
        rows = 2 * routing.lines.count * routing.capacity
        self.buffer = jnp.zeros((rows, values.shape[1]), values.dtype)
        self.fars, self.ready = {}, {}

    @property
    def value(self):
        return self.held[-1], self.buffer, self.fars, self.ready

    @value.setter
    def value(self, value):
        self.held[-1], self.buffer, self.fars, self.ready = value

    def step(self):
        self.held = self.routing.lines.step_gather(self.held)

    def put(self, rows, block):
        at = block * self.routing.capacity
        self.buffer = lax.dynamic_update_slice(self.buffer, rows, (at, 0))

    def prepare(self, j):
        block = self.routing.lines.slot(self.held, j)
        self.ready[j] = mm(self.routing.mate_hot[j], block).astype(bf16)

    def send(self, j):
        if j not in self.ready:
            self.prepare(j)
        self.fars[j] = self.routing.lines.swap(self.ready.pop(j))

    def place(self, j):
        block = self.routing.lines.slot(self.held, j)
        self.put(mm(self.routing.own_hot[j], block).astype(bf16), j)

    def take(self, j):
        self.put(self.fars.pop(j), self.routing.lines.count + j)

    def round(self, j):
        if j < self.routing.lines.count - 1:
            self.step()
        self.send(j)
        if j > 0:
            self.take(j - 1)
        self.place(j)

    def total(self):
        for j in list(self.fars):
            self.take(j)
        return self.buffer


class Returned:
    def __init__(self, routing, far):
        self.routing = routing
        count = routing.lines.count
        self.blocks = [None] * count + self.cut(far)
        self.parts = [None] * count
        self.steps = 0
        self.came, self.arrived = {}, None

    @property
    def value(self):
        return self.came, self.arrived, self.blocks

    @value.setter
    def value(self, value):
        self.came, self.arrived, self.blocks = value

    def cut(self, rows):
        capacity = self.routing.capacity
        return [rows[at : at + capacity] for at in range(0, rows.shape[0], capacity)]

    def near(self, rows):
        self.blocks = self.cut(rows) + self.blocks[self.routing.lines.count :]

    def swap(self, j):
        lines = self.routing.lines
        self.came[j] = lines.swap(self.blocks[lines.count + j])

    def spread(self, j):
        own, far = self.routing.own_hot[j], self.routing.mate_hot[j]
        self.parts[j] = mm_tn(own, self.blocks[j]) + mm_tn(far, self.came.pop(j))

    def step(self):
        lines = self.routing.lines
        self.spread(lines.count - 1 - self.steps)
        self.arrived = lines.step_reduce(self.steps, self.parts, self.arrived)
        self.steps += 1

    def advance(self, stage):
        self.step()
        self.swap(self.routing.lines.count - 1 - stage)

    def total(self):
        self.spread(0)
        from_even, from_odd = self.routing.lines.inward(self.arrived)
        return self.parts[0] + from_even + from_odd


def settle(moving, *values):
    arrived, values = sync([m.value for m in moving], values)
    for m, value in zip(moving, arrived, strict=True):
        m.value = value
    return values


class Routing:
    pass


def per_device(
    tokens,
    lengths,
    routes,
    slot_order,
    cotangent,
    q_weight,
    key_matrix,
    value_matrix,
    out_weight,
    router_weight,
    attn_gain,
    ffn_gain,
    gate_weight,
    up_weight,
    down_weight,
):
    lines = Lines()
    layer_count = q_weight.shape[0]
    shard_count = lax.axis_size("shard")
    mine = lax.axis_index("shard")
    token_rows, model_width = tokens.shape
    pair_count = token_rows * routes.shape[1]
    experts = router_weight.shape[2]
    assert shard_count == 4 and experts == lines.experts and gate_weight.shape[1] == 1
    hidden_units = gate_weight.shape[3]
    capacity = (pair_count * 5 + 4 * experts - 1) // (4 * experts)
    assert capacity < 256
    sequence_length = token_rows * shard_count
    kv_width = KEY_VALUE_HEADS * HEAD_SIZE

    own_rows = jnp.arange(token_rows, dtype=jnp.int32)
    position = mine * token_rows + own_rows
    key_position = jnp.concatenate([(mine ^ mask) * token_rows + own_rows for mask in (0, 2, 1, 3)])
    query_doc, query_position = documents(lengths[0], position)
    key_doc = documents(lengths[0], key_position)[0]
    tables = rotary_tables(query_position)
    query_marks, key_marks = (query_doc, position), (key_doc, key_position)

    def paired(i):
        parts = []
        for at in range(0, kv_width, HEAD_SIZE):
            parts += [key_matrix[i, :, at : at + HEAD_SIZE], value_matrix[i, :, at : at + HEAD_SIZE]]
        return jnp.concatenate(parts, axis=1)

    small = jnp.concatenate(
        [router_weight.transpose(0, 2, 1), attn_gain[:, None, :], ffn_gain[:, None, :]], axis=1
    )
    routing = Routing()
    routing.lines, routing.capacity = lines, capacity
    late = Sent(routing, cotangent)
    units = column_units(lines)

    def side_half(shards, layer):
        half = shards.shape[1] // 2
        return lax.dynamic_slice(
            shards, (layer, lines.side * half, 0), (1, half, shards.shape[2])
        )[0]

    kv_first = paired(0)
    small_across, small_beside = row_swap(small), core_swap(small)
    kv_across, kv_beside = row_swap(side_half(kv_first[None], 0)), core_swap(kv_first)
    query_half = side_half(q_weight, 0)
    small_across, small_beside, kv_across, kv_beside, query_half, q_gated = sync(
        small_across, small_beside, kv_across, kv_beside, query_half, q_weight
    )
    slot_code = jnp.arange(1, capacity + 1, dtype=jnp.int32).astype(f32)[:, None]
    query_rows = tuple(mark[:, None] for mark in query_marks)
    key_rows = tuple(mark[None, :] for mark in key_marks)

    query_across = row_swap(query_half)
    query_own = q_gated[0]
    query_beside = core_swap(query_own)
    kv_crossed = lines.swap(kv_across)
    kv_across_beside = core_swap(kv_across)
    late.step()
    own_table = slot_table(routes, slot_order[0], experts, capacity)
    small_diagonal = core_swap(small_across)
    small = ordered_small({0: small, 1: small_beside, 2: small_across, 3: small_diagonal})
    routers = [small[i, :experts] for i in range(layer_count)]
    attn_gains = [small[i, experts].astype(f32)[None, :] for i in range(layer_count)]
    ffn_gains = [small[i, experts + 1].astype(f32)[None, :] for i in range(layer_count)]
    stream = tokens.astype(f32)
    normed, attn_inverse = norm_forward(stream, attn_gains[0])
    hidden = normed.astype(bf16)
    matched = column_parts(hidden, units)
    query_across, query_beside, kv_crossed, kv_across_beside, matched, own_table, later = settle(
        [late], query_across, query_beside, kv_crossed, kv_across_beside, matched, own_table,
        (out_weight, key_matrix, value_matrix),
    )
    every = lambda part: lax.all_gather(part, "shard", axis=0, tiled=True)
    gathered = [(None, None, every(later[0][0]))]
    tables, query_rows, key_rows, slot_code = sync(tables, query_rows, key_rows, slot_code)

    query_crossed = lines.swap(query_across)
    query_across_beside = core_swap(query_across)
    kv_pieces = [kv_first, kv_beside, kv_across, kv_crossed, kv_across_beside]
    kv_pieces.append(core_swap(kv_crossed))
    first_own = project(matched, kv_pieces, tables)
    first_crossed = row_swap(first_own)
    held_tables = [(own_table, own_table)]
    for _ in range(lines.count - 1):
        held_tables = lines.step_gather(held_tables)
    query_crossed, query_across_beside, first_own, first_crossed, q_gated, later = settle(
        [late], query_crossed, query_across_beside, first_own, first_crossed, q_gated, later
    )
    first_pair = jnp.concatenate([first_own, first_crossed], axis=0)
    near_tables = jnp.stack([lines.slot(held_tables, j) for j in range(lines.count)], axis=0)
    query_pieces = [query_own, query_beside, query_across, query_crossed, query_across_beside]
    query_pieces.append(core_swap(query_crossed))

    def prepare_routing(near_tables, own_table):
        far_tables = lines.swap(near_tables)

        def hot_rows(codes, expert):
            code = lax.dynamic_index_in_dim(codes, expert, 1, keepdims=True)
            return (code == slot_code).astype(bf16)

        routing.own_hot = hot_rows(near_tables, lines.index)
        routing.mate_hot = hot_rows(near_tables, lines.index ^ 1)
        all_hot = jnp.concatenate([routing.own_hot, hot_rows(far_tables, lines.index)], axis=0)
        all_tables = jnp.concatenate([near_tables, far_tables], axis=0)
        row_chosen = jnp.einsum(
            "sct,set->sce", all_hot, (all_tables != 0.0).astype(bf16), preferred_element_type=f32
        ).reshape(2 * lines.count * capacity, experts)
        return own_table.T != 0.0, row_chosen

    own_expert = (jnp.arange(experts) == lines.index).astype(f32)[None, :]
    assert experts <= 64
    gate_marks = jnp.arange(128)[None, :] == lines.index + 64 * jnp.arange(2)[:, None]
    gate_marks = gate_marks.astype(f32)

    weights = (gate_weight, up_weight, down_weight)

    def small_sum(part):
        own = sum(exchange_blocks(split_columns(part)))
        return jnp.pad(own, ((0, -own.shape[0] % 128), (0, 0))).T

    last = layer_count - 1
    stored = []
    for i in range(layer_count):
        w_query, w_kv, w_out = gathered[i]
        if i == 0:
            late.step()
            kv_pair = first_pair
            q_pre = project(matched, query_pieces)
        else:
            if i == last:
                late.send(2)
            normed, attn_inverse = norm_forward(stream, attn_gains[i])
            hidden = normed.astype(bf16)
            kv_own = project([hidden], [w_kv], tables)
            kv_crossed = row_swap(kv_own)
            q_pre = mm(hidden, w_query)
            kv_own, kv_crossed, q_pre = settle([late], kv_own, kv_crossed, q_pre)
            kv_pair = jnp.concatenate([kv_own, kv_crossed], axis=0)
            if i == last:
                late.send(3)
                for k in range(4, lines.count):
                    late.step()
                    late.send(k)
        kv_all = shard_rows_all(kv_pair)
        query, mixed = attend(q_pre, kv_all, tables, query_rows, key_rows)
        stream_mid = stream + mm(mixed, w_out)
        normed_ffn, ffn_inverse = norm_forward(stream_mid, ffn_gains[i])
        routed = normed_ffn.astype(bf16)
        if i == last:
            (routed, gathered[0]) = settle([late], routed, gathered[0])
        else:
            routed, near_tables = settle([late], routed, near_tables)
            chosen_here, row_chosen = prepare_routing(near_tables, own_table)
        if i == 0:

            def paired_of(k):
                parts = []
                for at in range(0, kv_width, HEAD_SIZE):
                    parts += [later[m][k, :, at : at + HEAD_SIZE] for m in (1, 2)]
                return jnp.concatenate(parts, axis=1)
        gates = chosen_softmax(mm_nt(routed, routers[i]), chosen_here)
        sent = Sent(routing, routed)
        for j in range(lines.count):
            sent.round(j)
            if i == 0 and j < 2:
                late.prepare(j)
            if i == last:
                late.place(j)
                late.take(j)
            hidden, mixed, q_gated, later = settle([sent, late], hidden, mixed, q_gated, later)
            if i == 0 and j == 0:
                for k in range(1, layer_count):
                    gathered.append((every(q_gated[k]), every(paired_of(k)), every(later[0][k])))
                gathered[0] = (every(q_gated[0]), every(paired_of(0)), w_out)
        columns = [own_columns(hidden), own_columns(mixed)]
        arrived = sent.total()
        if i == 0:
            (arrived,) = settle([late], arrived)
        shared = (arrived, routers[i], row_chosen, own_expert, weights)
        produced, kept = expert_forward(i, 1, *shared)
        if i == 0:
            late.step()
            late.send(0)
        produced, kept = sync(produced, kept)
        back = Returned(routing, produced)
        back.swap(lines.count - 1)
        produced, kept = expert_forward(i, 0, *shared, into=kept)
        if i == 0:
            late.send(1)
        produced, kept = settle([late, back], produced, kept)
        back.near(produced)
        stored.append(
            dict(
                stream=stream,
                attn_inverse=attn_inverse,
                hidden_columns=columns[0],
                query=query,
                kv_all=kv_all,
                mixed_columns=columns[1],
                stream_mid=stream_mid,
                ffn_inverse=ffn_inverse,
                routed=routed,
                gates=gates,
                arrived=arrived,
                kept=kept,
            )
        )
        if i < last:
            for j in range(1, lines.count):
                back.advance(j)
                if i == last - 1 and j in (1, 2):
                    late.prepare(j + 1)
                if j == 1:
                    stored[i]["arrived_parts"] = split_columns(arrived)
                if j == 2:
                    stored[i]["gated_parts"] = split_columns(kept[2])
                parts = [stored[i].get(n, ()) for n in ("arrived_parts", "gated_parts")]
                parts = settle([back, late], parts)[0]
                stored[i].update(zip(("arrived_parts", "gated_parts"), parts))
            stream = stream_mid + back.total()

    own_width = model_width // shard_count
    results = dict(
        query=jnp.full((layer_count, own_width, model_width), 0.0, f32),
        out=jnp.full((layer_count, own_width, model_width), 1.0, f32),
        key=jnp.full((layer_count, own_width, kv_width), 0.0, f32),
        value=jnp.full((layer_count, own_width, kv_width), 1.0, f32),
        gate=jnp.full((layer_count, own_width, hidden_units), 0.0, f32),
        up=jnp.full((layer_count, own_width, hidden_units), 1.0, f32),
        down=jnp.full((layer_count, hidden_units // shard_count, model_width), 0.0, f32),
    )

    small_results = [None] * layer_count

    def put_experts(layer, both, down):
        for name, block in (
            ("gate", both[:, :hidden_units]),
            ("up", both[:, hidden_units:]),
            ("down", down),
        ):
            results[name] = lax.dynamic_update_slice(
                results[name], block.astype(f32)[None], (layer, 0, 0)
            )

    def put_kv(layer, joined, take):
        heads = lambda first: lambda x: jnp.concatenate(
            [take(x)[:, at : at + HEAD_SIZE] for at in range(first, 2 * kv_width, 2 * HEAD_SIZE)],
            axis=1,
        )
        results["key"] = joined.put(results["key"], layer, heads(0))
        results["value"] = joined.put(results["value"], layer, heads(HEAD_SIZE))
        rest = lambda x: take(x)[:, 2 * kv_width :]
        small_results[layer] = joined.whole(rest)

    output_back = back
    top = lines.count - 1
    d_arrived = late.total()
    upstream = cotangent.astype(f32)
    for i in reversed(range(layer_count)):
        w_query, w_kv, w_out = gathered[i]
        saved = stored[i]
        if i < last:
            sent = Sent(routing, upstream.astype(bf16))
            columns = stored[i + 1]["hidden_columns"]
            out_above, d_query, d_kv_low, small_grad = waiting
            small_part = small_grad
            for j in range(lines.count):
                sent.round(j)
                moving = []
                if j == 0:
                    d_kv_low = shard_rows_of(d_kv_low)
                if j == 1:
                    d_query = shard_rows_all(d_query)
                    d_kv_low = shard_rows_all(d_kv_low)
                    small_part = small_sum(small_grad)
                if j == 2:
                    query_above = Summed(lines, mm_tn(columns, d_query))
                    query_above.side()
                if j == 3:
                    kv_above = mm_tn(columns, d_kv_low)
                    kv_above = Summed(lines, jnp.concatenate([kv_above, small_part], axis=1))
                    kv_above.side()
                    moving = [query_above, kv_above]
                d_query, d_kv_low, small_part = settle(
                    [sent] + moving, d_query, d_kv_low, small_part
                )
                if j == 1:
                    results, d_query = sync(results, d_query)
                if j == 2:
                    names = ("hidden_columns", "mixed_columns")
                    first = [stored[0][name] for name in names]
                    first, d_query = sync(first, d_query)
                    stored[0].update(zip(names, first))
                if j == lines.count - 1:
                    d_query, both_grad, down_grad = sync(d_query, both_grad, down_grad)
            put_experts(last, both_grad, down_grad)
            d_arrived = sent.total()
            above = merged([out_above, kv_above, query_above])
            above.scatter()
        gate_pre, up_pre, gated, own_gate = saved["kept"]
        shared = (d_arrived, gate_pre, up_pre, own_gate, gate_marks, weights)
        if i == last:
            output_back.step()
        d_rows, d_both = expert_backward(i, 1, *shared)
        d_rows, d_both = sync(d_rows, d_both)
        back = Returned(routing, d_rows)
        back.swap(top)
        d_rows, d_both = expert_backward(i, 0, *shared, into=d_both)
        moving = [back, output_back if i == last else above]
        d_rows, d_both = settle(moving, d_rows, d_both)
        back.near(d_rows)
        if i == last:
            both = ShardSummed(split_columns(saved["arrived"]), d_both)
            down = ShardSummed(split_columns(gated), d_arrived)
        else:
            both = ShardSummed(saved["arrived_parts"], d_both)
            down = ShardSummed(saved["gated_parts"], d_arrived)
        for j in range(1, lines.count):
            back.advance(j)
            moving = [back, both, down]
            if j == 1:
                both.core()
            if j == 2:
                both.row()
                down.core()
                if i == last:
                    for k in reversed(range(2, top)):
                        output_back.swap(k)
                    moving.append(output_back)
            if j == 3:
                both.keep()
                down.row()
                moving = [back, both] + ([output_back] if i == last else [])
            settle(moving)
        down.keep()
        returned = back.total()
        d_gates = returned[:, model_width : model_width + experts]
        d_gates = d_gates + returned[:, model_width + 64 : model_width + 64 + experts]
        gates = saved["gates"]
        d_logits = gates * (d_gates - jnp.sum(gates * d_gates, axis=1, keepdims=True))
        d_logits = d_logits.astype(bf16)
        router_grad = mm_tn(d_logits, saved["routed"])
        d_routed = returned[:, :model_width] + mm(d_logits, routers[i])
        d_stream, ffn_gain_grad = norm_backward(
            saved["stream_mid"], saved["ffn_inverse"], ffn_gains[i], d_routed
        )
        upstream = upstream + d_stream
        d_branch = upstream.astype(bf16)
        d_mixed = mm_nt(d_branch, w_out).astype(bf16)
        if i == last:
            while output_back.steps < top - 1:
                output_back.step()
            output_back.swap(1)
            output_back.swap(0)
            moving = [output_back]
        else:
            above.spread()
            moving = []
        d_branch_crossed = row_swap(d_branch)
        d_query, d_kv = attend_back(
            saved["query"], saved["kv_all"], d_mixed, tables, query_marks, key_marks
        )
        d_query, d_kv, d_branch_crossed = settle(
            moving + [down], d_query, d_kv, d_branch_crossed
        )
        d_branch_pair = jnp.concatenate([d_branch, d_branch_crossed], axis=0)
        both_grad, down_grad = both.total(), down.total()
        pair_rows = 2 * token_rows
        d_kv_pair = d_kv[:pair_rows].astype(f32) + core_swap(d_kv[pair_rows:]).astype(f32)
        d_branch_all = shard_rows_all(d_branch_pair)
        d_kv_pair, d_branch_all, d_query = sync(d_kv_pair, d_branch_all, d_query)
        d_kv_crossed = row_swap(d_kv_pair[token_rows:].astype(bf16))
        d_hidden = mm_nt(d_query, w_query)
        out_part = mm_tn(saved["mixed_columns"], d_branch_all)
        d_kv_crossed, d_query, d_hidden, out_part = sync(
            d_kv_crossed, d_query, d_hidden, out_part
        )
        out_sum = Summed(lines, out_part)
        out_sum.side()
        moving = [out_sum]
        if i == last:
            output_back.step()
            moving.append(output_back)
        else:
            moving.append(above)
        d_query_pair = shard_rows_of(d_query)
        d_kv_low = turn_kv_back(d_kv_pair[:token_rows], d_kv_crossed, tables)
        d_hidden = d_hidden + mm_nt(d_kv_low, w_kv)
        d_stream, attn_gain_grad = norm_backward(
            saved["stream"], saved["attn_inverse"], attn_gains[i], d_hidden
        )
        upstream = upstream + d_stream
        small_grad = jnp.concatenate(
            [router_grad, attn_gain_grad[None, :], ffn_gain_grad[None, :]], axis=0
        )
        upstream, d_kv_low, small_grad = settle(moving, upstream, d_kv_low, small_grad)
        if i == last:
            output = (saved["stream_mid"] + output_back.total()).astype(bf16)
            out_above = out_sum
            waiting = (out_above, d_query_pair, d_kv_low, small_grad)

    hidden_columns = stored[0]["hidden_columns"]
    out_sum.scatter()
    d_kv_crossed = row_swap(d_kv_low)
    small_part = small_sum(small_grad)
    q_sum = Summed(lines, mm_tn(hidden_columns, shard_rows_all(d_query_pair)))
    q_sum.side()
    d_kv_crossed, small_part = settle([q_sum, out_sum], d_kv_crossed, small_part)
    d_kv_pair = jnp.concatenate([d_kv_low, d_kv_crossed], axis=0)
    q_sum.scatter()
    kv_part = mm_tn(hidden_columns, shard_rows_all(d_kv_pair))
    kv_sum = Summed(lines, jnp.concatenate([kv_part, small_part], axis=1))
    kv_sum.side()
    half_result = above.assembled()
    split = half_result.shape[1] - model_width
    above_first = Joined(lines, half_result[:, :split])
    out_sum.spread()
    above_second_rows = half_result[:, split:]
    (above_second_rows,) = settle([q_sum, kv_sum, out_sum], above_second_rows)
    q_sum.spread()
    kv_sum.scatter()
    out_join = Joined(lines, out_sum.assembled())
    above_second = Joined(lines, above_second_rows)
    put_experts(0, both_grad, down_grad)
    (results,) = settle([q_sum, kv_sum, out_join, above_first], results)
    q_join = Joined(lines, q_sum.assembled())
    kv_sum.spread()
    results["out"] = above_first.put(results["out"], last, lambda x: x[:, :model_width])
    put_kv(last, above_first, lambda x: x[:, model_width:])
    results["out"] = out_join.put(results["out"], 0)
    (results,) = settle([q_join, kv_sum, above_second], results)
    kv_join = Joined(lines, kv_sum.assembled())
    results["query"] = above_second.put(results["query"], last)
    results["query"] = q_join.put(results["query"], 0)
    put_kv(0, kv_join, lambda x: x)
    small_result = jnp.stack(small_results, axis=0)
    return (
        output,
        upstream.astype(bf16),
        results["query"],
        results["key"],
        results["value"],
        results["out"],
        small_result[:, :, :experts],
        small_result[:, :, experts],
        small_result[:, :, experts + 1],
        results["gate"][:, None],
        results["up"][:, None],
        results["down"][:, None],
    )


def solution(mesh):
    tokens_spec = P(("expert", "shard"), None)
    shard_spec = P(None, "shard", None)
    expert_spec = P(None, "expert", None, None)
    expert_grad_spec = P(None, "expert", "shard", None)
    return jax.shard_map(
        per_device,
        mesh=mesh,
        in_specs=(
            tokens_spec,
            P("expert", None),
            tokens_spec,
            tokens_spec,
            tokens_spec,
            shard_spec,
            shard_spec,
            shard_spec,
            shard_spec,
            shard_spec,
            P(None, "shard"),
            P(None, "shard"),
            expert_spec,
            expert_spec,
            expert_spec,
        ),
        out_specs=(
            tokens_spec,
            tokens_spec,
            shard_spec,
            shard_spec,
            shard_spec,
            shard_spec,
            shard_spec,
            P(None, "shard"),
            P(None, "shard"),
            expert_grad_spec,
            expert_grad_spec,
            expert_grad_spec,
        ),
        check_vma=False,
    )
```
